128 devices in a mesh: func: 16 (over z, y_lo, core), pts: 8 (over x, y_hi).
Axes of the slice: x: 4, y: 4 (y_hi: 2, y_lo: 2; y = y_hi * 2 + y_lo), z: 4, core: 2. Of those that a mesh axis runs over, the one named last changes fastest.
Arguments:
- sensors: bfloat16 [1024, 4096], P(('func', 'pts')), may hold values from -6 to 6
- forcing: bfloat16 [1024, 16384], P('func', 'pts'), may hold values from -6 to 6
- coords: float32 [2, 16384], P(None, 'pts'), may hold values from -3.14159 to 3.14159
- branch_first: bfloat16 [4096, 256], replicated, may hold values from -0.09375 to 0.09375
- branch_second: bfloat16 [256, 256], replicated, may hold values from -0.375 to 0.375
- branch_third: bfloat16 [256, 256], replicated, may hold values from -0.375 to 0.375
- trunk_first: float32 [2, 256], replicated, may hold values from -4 to 4
- trunk_second: bfloat16 [256, 256], replicated, may hold values from -0.375 to 0.375
- trunk_third: bfloat16 [256, 256], replicated, may hold values from -0.375 to 0.375
Outputs:
- grad_branch_first: float32 [4096, 256], replicated
- grad_branch_second: float32 [256, 256], replicated
- grad_branch_third: float32 [256, 256], replicated
- grad_trunk_first: float32 [2, 256], replicated
- grad_trunk_second: float32 [256, 256], replicated
- grad_trunk_third: float32 [256, 256], replicated
The draws below stay inside these ranges and needn't reach their ends.
All inputs are finite; a program needn't handle non-finite values.
Results may differ from the reference program's by a relative error of at most 0.009.
Values may be sent and summed in bfloat16 or wider, within the bound.
No kernel may reach another device: no remote copies, remote signals or barrier semaphores. Data moves between devices by JAX's collectives and lax.ppermute only.
A program may use at most 192 MiB of HBM per device.

```python
import math
import jax
import jax.numpy as jnp
from jax import lax

M = 4096
W = 256
P_SIZE = 256
FUNC_DEV = 64
FUNCS = 1024
POINTS = 16384


def block_levels(stream_key, shape, shards, low, largest):
    def one(dim, shards_of):
        heights = jax.random.uniform(jax.random.fold_in(jax.random.fold_in(stream_key, 6), dim), (shards_of,), jnp.float32, low / len(shards), largest / len(shards))
        return jnp.repeat(jnp.exp(heights), shape[dim] // shards_of).reshape((-1,) + (1,) * (len(shape) - dim - 1))

    gain = one(*shards[0])
    for cut in shards[1:]:
        gain = gain * one(*cut)
    return gain


def centred(stream_key, dims, width, bound, cuts=(), kind=jnp.bfloat16):
    entries = jax.random.normal(stream_key, dims, jnp.float32) * width
    if len(cuts) > 0:
        entries = block_levels(stream_key, dims, cuts, -0.22, 0.18) * entries
    return jnp.clip(entries, min=-bound, max=bound).astype(kind)


def setup_inputs(seed: int = 0) -> dict:
    key_of = jax.random.split(jax.random.key(seed), 10)
    return {
        "sensors": centred(key_of[0], (FUNCS, M), 1.0, 6.0, ((0, 128),)),
        "forcing": centred(key_of[1], (FUNCS, POINTS), 1.0, 6.0, ((0, 16), (1, 8))),
        "coords": jnp.clip(jax.random.uniform(key_of[2], (2, POINTS), jnp.float32, -3.14159, 3.14159) * block_levels(key_of[2], (2, POINTS), ((1, 8),), -0.4, 0.0), -3.14159, 3.14159),
        "branch_first": centred(key_of[3], (M, W), M ** -0.5, 0.09375),
        "branch_second": centred(key_of[4], (W, W), W ** -0.5, 0.375),
        "branch_third": centred(key_of[5], (W, P_SIZE), W ** -0.5, 0.375),
        "trunk_first": centred(key_of[6], (2, W), 2 ** -0.5, 4.0, (), jnp.float32),
        "trunk_second": centred(key_of[7], (W, W), W ** -0.5, 0.375),
        "trunk_third": centred(key_of[8], (W, P_SIZE), W ** -0.5, 0.375),
    }


HIGHEST = lax.Precision.HIGHEST
DRAG = 0.5

def tanh_jet(inner):
    squash = jnp.tanh(inner[0])
    slope_one = 1.0 - squash * squash
    slope_two = -2.0 * squash * slope_one
    slope_three = -2.0 * slope_one * slope_one + 4.0 * squash * squash * slope_one
    return jnp.stack([squash, slope_one * inner[1], slope_one * inner[2], slope_one * inner[3] + slope_two * inner[1] * inner[1], slope_one * inner[4] + slope_two * inner[1] * inner[2], slope_one * inner[5] + slope_two * inner[2] * inner[2], slope_one * inner[6] + 3.0 * slope_two * inner[1] * inner[3] + slope_three * inner[1] * inner[1] * inner[1], slope_one * inner[7] + slope_two * (2.0 * inner[1] * inner[4] + inner[2] * inner[3]) + slope_three * inner[1] * inner[1] * inner[2], slope_one * inner[8] + slope_two * (2.0 * inner[2] * inner[4] + inner[1] * inner[5]) + slope_three * inner[1] * inner[2] * inner[2], slope_one * inner[9] + 3.0 * slope_two * inner[2] * inner[5] + slope_three * inner[2] * inner[2] * inner[2]])

def input_jet(trunk_first, coords):
    value = coords[0][:, None] * trunk_first[0] + coords[1][:, None] * trunk_first[1]
    along_x = jnp.broadcast_to(trunk_first[0], value.shape)
    along_y = jnp.broadcast_to(trunk_first[1], value.shape)
    zeros = jnp.zeros_like(value)
    return jnp.stack([value, along_x, along_y] + [zeros] * 7)

def hidden_parts(coords, trunk_first, trunk_second):
    trunk_one = tanh_jet(input_jet(trunk_first, coords)).astype(jnp.bfloat16)
    inner_jet = jnp.einsum('crw,wv->crv', trunk_one.astype(jnp.float32), trunk_second.astype(jnp.float32))
    outer_jet = tanh_jet(inner_jet)
    combos = jnp.stack([outer_jet[1], outer_jet[2], -(outer_jet[3] + outer_jet[5]), -(outer_jet[6] + outer_jet[8]), -(outer_jet[7] + outer_jet[9])], axis=1).astype(jnp.bfloat16)
    return (trunk_one, inner_jet, combos)

def channels_from(combos, trunk_third):
    return jnp.einsum('rkw,wp->rkp', combos.astype(jnp.float32), trunk_third.astype(jnp.float32)).astype(jnp.bfloat16)

def trunk_grads(coords, trunk_first, trunk_second, trunk_third, parts, channel_cot):
    trunk_one, inner_jet, combos = parts
    grad_third = jnp.einsum('rkw,rkp->wp', combos.astype(jnp.float32), channel_cot, precision=HIGHEST)
    combo_back = jnp.einsum('rkp,wp->rkw', channel_cot, trunk_third.astype(jnp.float32), precision=HIGHEST)
    zeros = jnp.zeros_like(combo_back[:, 0])
    jet_back = jnp.stack([zeros, combo_back[:, 0], combo_back[:, 1], -combo_back[:, 2], zeros, -combo_back[:, 2], -combo_back[:, 3], -combo_back[:, 4], -combo_back[:, 3], -combo_back[:, 4]])
    inner_back = jax.vjp(tanh_jet, inner_jet)[1](jet_back)[0]
    grad_second = jnp.einsum('crw,crv->wv', trunk_one.astype(jnp.float32), inner_back, precision=HIGHEST)
    one_back = jnp.einsum('crv,wv->crw', inner_back, trunk_second.astype(jnp.float32), precision=HIGHEST)
    grad_first = jax.vjp(lambda weight: tanh_jet(input_jet(weight, coords)), trunk_first)[1](one_back)[0]
    return (grad_first, grad_second, grad_third)

def branch_forward(sensors, first, second, third):
    hidden_one = jnp.tanh(jnp.dot(sensors, first, preferred_element_type=jnp.float32))
    branch_one = hidden_one.astype(jnp.bfloat16)
    hidden_two = jnp.tanh(jnp.dot(branch_one, second, preferred_element_type=jnp.float32))
    branch_two = hidden_two.astype(jnp.bfloat16)
    features = jnp.dot(branch_two, third, preferred_element_type=jnp.float32).astype(jnp.bfloat16)
    return (features, (hidden_one, branch_one, hidden_two, branch_two))

def branch_grads(sensors, second, third, saved, feature_cot):
    hidden_one, branch_one, hidden_two, branch_two = saved
    feature_back = feature_cot.astype(jnp.bfloat16)
    grad_third = jnp.dot(branch_two.T, feature_back, preferred_element_type=jnp.float32)
    back_two = (jnp.dot(feature_back, third.T, preferred_element_type=jnp.float32) * (1.0 - hidden_two * hidden_two)).astype(jnp.bfloat16)
    grad_second = jnp.dot(branch_one.T, back_two, preferred_element_type=jnp.float32)
    back_one = (jnp.dot(back_two, second.T, preferred_element_type=jnp.float32) * (1.0 - hidden_one * hidden_one)).astype(jnp.bfloat16)
    grad_first = jnp.dot(sensors.T, back_one, preferred_element_type=jnp.float32)
    return (grad_first, grad_second, grad_third)

def reference(sensors, forcing, coords, branch_first, branch_second, branch_third, trunk_first, trunk_second, trunk_third):
    features, saved = branch_forward(sensors, branch_first, branch_second, branch_third)
    block_rows = min(512, POINTS)
    blocks = POINTS // block_rows
    pieces = coords.reshape(2, blocks, block_rows).transpose(1, 0, 2)
    parts = lax.map(lambda segment: hidden_parts(segment, trunk_first, trunk_second), pieces)
    channels = lax.map(lambda combos: channels_from(combos, trunk_third), parts[2]).reshape(POINTS, 5, P_SIZE)
    weight = 1.0 / math.sqrt(FUNCS * POINTS)
    scale = P_SIZE ** (-0.5)
    channels_wide = channels.astype(jnp.float32)
    features_wide = features.astype(jnp.float32)

    def per_block(carry, block_index):
        first_row = block_index * FUNC_DEV
        block_features = lax.dynamic_slice_in_dim(features_wide, first_row, FUNC_DEV, 0)
        block_forcing = lax.dynamic_slice_in_dim(forcing, first_row, FUNC_DEV, 0).astype(jnp.float32)
        projected = jnp.einsum('fp,nkp->kfn', block_features, channels_wide) * scale
        residual = projected[1] * projected[3] - projected[0] * projected[4] + DRAG * projected[2] - block_forcing
        slope_grid = residual * weight
        proj_cot = jnp.stack([-slope_grid * projected[4], slope_grid * projected[3], DRAG * slope_grid, slope_grid * projected[1], -slope_grid * projected[0]]).astype(jnp.bfloat16).astype(jnp.float32)
        feature_cot = jnp.einsum('kfn,nkp->fp', proj_cot, channels_wide) * scale
        channel_part = jnp.einsum('kfn,fp->nkp', proj_cot, block_features) * scale
        return (carry + channel_part, feature_cot)
    channel_cot, feature_blocks = lax.scan(per_block, jnp.zeros((POINTS, 5, P_SIZE), jnp.float32), jnp.arange(FUNCS // FUNC_DEV, dtype=jnp.int32))
    feature_cot = feature_blocks.reshape(FUNCS, P_SIZE)
    grad_b1, grad_b2, grad_b3 = branch_grads(sensors, branch_second, branch_third, saved, feature_cot)
    cot_blocks = channel_cot.reshape(blocks, block_rows, 5, P_SIZE)

    def accumulate(carry, inputs):
        segment, trunk_one, inner_jet, combos, cot_piece = inputs
        update = trunk_grads(segment, trunk_first, trunk_second, trunk_third, (trunk_one, inner_jet, combos), cot_piece)
        return ((carry[0] + update[0], carry[1] + update[1], carry[2] + update[2]), None)
    start = (jnp.zeros((2, W), jnp.float32), jnp.zeros((W, W), jnp.float32), jnp.zeros((W, P_SIZE), jnp.float32))
    totals, _ = lax.scan(accumulate, start, (pieces, parts[0], parts[1], parts[2], cot_blocks))
    return (grad_b1, grad_b2, grad_b3, totals[0], totals[1], totals[2])
```

```python
import functools
import math

import jax
import jax.numpy as jnp
from jax import lax
from jax.experimental import pallas as pl
from jax.experimental.pallas import tpu as pltpu
from jax.sharding import PartitionSpec as P

DRAG = 0.5
TILE = 512
ROWS = 16
LANES = 128
F32 = jnp.float32
BF16 = jnp.bfloat16
GROUP = (0, 1, 1, 2, 2, 2, 3, 3)
NT = (((1,), (1,)), ((), ()))
TN = (((0,), (0,)), ((), ()))


def dot(left, right, dims=(((1,), (0,)), ((), ()))):
    return lax.dot_general(left, right, dims, preferred_element_type=F32)


def slopes(squash):
    square = squash * squash
    one = 1.0 - square
    two = -2.0 * (squash * one)
    three = one * (4.0 * square - 2.0 * one)
    return square, one, two, three


def trunk_kernel(
    weight,
    scale,
    coords_ref,
    first_ref,
    weights_ref,
    second_ref,
    consts_ref,
    feats_ref,
    forcing_ref,
    u_ref,
    second_grad_ref,
    const_grad_ref,
    value_grad_ref,
    squash_ref,
    points_ref,
    inner_ref,
    combos_ref,
    back_ref,
    inner_back_ref,
    ones_ref,
    grads_ref,
    value_ref,
):
    step = pl.program_id(0)
    last = pl.num_programs(0) - 1
    tile = coords_ref.shape[0]
    width = first_ref.shape[1]

    @pl.when(step == 0)
    def _():
        u_ref[...] = jnp.zeros_like(u_ref)
        grads_ref[...] = jnp.zeros_like(grads_ref)
        value_ref[...] = jnp.zeros_like(value_ref)

    def chunks(body, unroll):
        def one(index, carry):
            start = pl.multiple_of(index * ROWS, ROWS)
            for lane in range(0, width, LANES):
                body(pl.ds(start, ROWS), pl.ds(lane, LANES))
            return carry

        lax.fori_loop(0, tile // ROWS, one, 0, unroll=unroll)

    def layer_one(rows, lanes):
        x, y = coords_ref[rows, 0:1], coords_ref[rows, 1:2]
        squash = jnp.tanh(x * first_ref[0:1, lanes] + y * first_ref[1:2, lanes])
        _, one, two, three = slopes(squash)
        squash_ref[rows, lanes] = squash
        for group, part in enumerate((squash, one, two, three)):
            points_ref[group, rows, lanes] = part.astype(BF16)

    chunks(layer_one, 2)
    for part, group in enumerate(GROUP):
        inner_ref[part] = dot(points_ref[group], weights_ref[part])

    def layer_two(rows, lanes):
        z, zx, zy, lap, dif, mix, px, py = (inner_ref[part, rows, lanes] for part in range(8))
        squash = jnp.tanh(z)
        inner_ref[0, rows, lanes] = squash
        _, one, two, three = slopes(squash)
        radius = zx * zx + zy * zy
        twice = lap + lap
        bend = three * radius
        along = zx * (twice + dif) + zy * mix
        across = zy * (twice - dif) + zx * mix
        combos = (
            one * zx,
            one * zy,
            one * lap - two * radius,
            one * px + two * along - bend * zx,
            one * py + two * across - bend * zy,
        )
        for k, combo in enumerate(combos):
            combos_ref[k, rows, lanes] = combo.astype(BF16)

    chunks(layer_two, 2)
    feats = feats_ref[...]
    px, py, om, omx, omy = (dot(feats, combos_ref[k], NT) * scale for k in range(5))
    slope = (py * omx - px * omy + DRAG * om - forcing_ref[...].astype(F32)) * weight
    cots = [
        cot.astype(BF16)
        for cot in (-slope * omy, slope * omx, DRAG * slope, slope * py, -slope * px)
    ]
    total = u_ref[...]
    for k in range(5):
        total += dot(cots[k], combos_ref[k])
        back_ref[k] = dot(cots[k], feats, TN) * scale
    u_ref[...] = total

    def layer_two_back(rows, lanes):
        squash, zx, zy, lap, dif, mix, px, py = (inner_ref[part, rows, lanes] for part in range(8))
        gx, gy, gl, gp, gq = (back_ref[k, rows, lanes] for k in range(5))
        square, one, two, three = slopes(squash)
        four = two * (4.0 * square - 8.0 * one)
        radius = zx * zx + zy * zy
        twice = lap + lap
        plus, minus = twice + dif, twice - dif
        along = zx * plus + zy * mix
        across = zy * minus + zx * mix
        pull = gp * zx + gq * zy
        one_bar = gx * zx + gy * zy + gl * lap + gp * px + gq * py
        two_bar = gp * along + gq * across - gl * radius
        three_bar = pull * radius
        along_bar, across_bar = two * gp, two * gq
        turn = -2.0 * (two * gl + three * pull)
        bend = three * radius
        xa, yc = zx * along_bar, zy * across_bar
        parts = (
            two * one_bar + three * two_bar - four * three_bar,
            one * gx - bend * gp + zx * turn + along_bar * plus + across_bar * mix,
            one * gy - bend * gq + zy * turn + across_bar * minus + along_bar * mix,
            one * gl + 2.0 * (xa + yc),
            xa - yc,
            zy * along_bar + zx * across_bar,
            one * gp,
            one * gq,
        )
        for part, value in enumerate(parts):
            inner_back_ref[part, rows, lanes] = value.astype(BF16)

    chunks(layer_two_back, 1)
    for part, group in enumerate(GROUP):
        grads_ref[part] += dot(points_ref[group], inner_back_ref[part], TN)
    for group in range(4):
        total = None
        for part in range(8):
            if GROUP[part] == group:
                term = dot(inner_back_ref[part], weights_ref[part], NT)
                total = term if total is None else total + term
        ones_ref[group] = total

    def layer_one_back(index, carry):
        start = pl.multiple_of(index * ROWS, ROWS)
        rows = pl.ds(start, ROWS)
        x, y = coords_ref[rows, 0:1], coords_ref[rows, 1:2]
        out = []
        for number, lane in enumerate(range(0, width, LANES)):
            lanes = pl.ds(lane, LANES)
            square, one, two, three = slopes(squash_ref[rows, lanes])
            four = two * (4.0 * square - 8.0 * one)
            back = (
                one * ones_ref[0, rows, lanes]
                + two * ones_ref[1, rows, lanes]
                + three * ones_ref[2, rows, lanes]
                + four * ones_ref[3, rows, lanes]
            )
            out += [carry[2 * number] + x * back, carry[2 * number + 1] + y * back]
        return tuple(out)

    zero = jnp.zeros((ROWS, LANES), F32)
    sums = lax.fori_loop(
        0, tile // ROWS, layer_one_back, (zero,) * (2 * (width // LANES)), unroll=2
    )
    for number, lane in enumerate(range(0, width, LANES)):
        for axis in range(2):
            value_ref[axis, :, lane : lane + LANES] += sums[2 * number + axis]

    @pl.when(step == last)
    def _():
        second = second_ref[...].astype(F32)
        total = jnp.zeros((width, width), F32)
        first = [jnp.zeros((width, 1), F32)] * 2
        for part in range(8):
            grad = grads_ref[part]
            total += consts_ref[:, part : part + 1] * grad
            row = jnp.sum(second * grad, axis=1, keepdims=True)
            for axis in range(2):
                column = 8 * (axis + 1) + part
                first[axis] = first[axis] + consts_ref[:, column : column + 1] * row
        second_grad_ref[...] = total
        for axis in range(2):
            const_grad_ref[:, axis : axis + 1] = first[axis]
            value_grad_ref[axis : axis + 1] = jnp.sum(value_ref[axis], axis=0, keepdims=True)


def trunk_call(coords, first, second, feats, forcing, weight, scale):
    points, width = coords.shape[1], first.shape[1]
    funcs = feats.shape[0]
    tile = min(TILE, points)
    a, b = first[0], first[1]
    one, zero = jnp.ones_like(a), jnp.zeros_like(a)
    consts = [
        one,
        a,
        b,
        -(a * a + b * b),
        -(a * a - b * b),
        -2.0 * a * b,
        -a * (a * a + b * b),
        -b * (a * a + b * b),
    ]
    by_a = [
        zero,
        one,
        zero,
        -2.0 * a,
        -2.0 * a,
        -2.0 * b,
        -(3.0 * a * a + b * b),
        -2.0 * a * b,
    ]
    by_b = [
        zero,
        zero,
        one,
        -2.0 * b,
        2.0 * b,
        -2.0 * a,
        -2.0 * a * b,
        -(a * a + 3.0 * b * b),
    ]
    columns = jnp.stack(consts + by_a + by_b, axis=1)
    weights = (jnp.stack(consts)[:, :, None] * second.astype(F32)[None]).astype(BF16)
    whole = lambda *shape: pl.BlockSpec(shape, lambda i: (0,) * len(shape))
    return pl.pallas_call(
        functools.partial(trunk_kernel, weight, scale),
        grid=(points // tile,),
        in_specs=[
            pl.BlockSpec((tile, 2), lambda i: (i, 0)),
            whole(2, width),
            whole(8, width, width),
            whole(width, width),
            whole(width, 24),
            whole(funcs, width),
            pl.BlockSpec((funcs, tile), lambda i: (0, i)),
        ],
        out_specs=[whole(funcs, width), whole(width, width), whole(width, 2), whole(2, width)],
        out_shape=[
            jax.ShapeDtypeStruct((funcs, width), F32),
            jax.ShapeDtypeStruct((width, width), F32),
            jax.ShapeDtypeStruct((width, 2), F32),
            jax.ShapeDtypeStruct((2, width), F32),
        ],
        scratch_shapes=[
            pltpu.VMEM((tile, width), F32),
            pltpu.VMEM((4, tile, width), BF16),
            pltpu.VMEM((8, tile, width), F32),
            pltpu.VMEM((5, tile, width), BF16),
            pltpu.VMEM((5, tile, width), F32),
            pltpu.VMEM((8, tile, width), BF16),
            pltpu.VMEM((4, tile, width), F32),
            pltpu.VMEM((8, width, width), F32),
            pltpu.VMEM((2, ROWS, width), F32),
        ],
        compiler_params=pltpu.CompilerParams(
            dimension_semantics=("arbitrary",), vmem_limit_bytes=48 * 1024 * 1024
        ),
        name="trunk",
    )(coords.T, first, weights, second, columns, feats, forcing)


def swap(parts):
    return lax.all_to_all(parts, ("func", "pts"), split_axis=0, concat_axis=0, tiled=True)


def tell(part, count):
    return swap(jnp.broadcast_to(part[None], (count, *part.shape)))


def per_device(
    sensors,
    forcing,
    coords,
    branch_first,
    branch_second,
    branch_third,
    trunk_first,
    trunk_second,
    trunk_third,
):
    func_size, pts_size = lax.axis_size("func"), lax.axis_size("pts")
    count = func_size * pts_size
    funcs = forcing.shape[0]
    weight = 1.0 / math.sqrt(funcs * func_size * forcing.shape[1] * pts_size)
    width_out = trunk_third.shape[1]
    width = trunk_second.shape[0]
    scale = width_out ** (-0.5)
    own = sensors.shape[0]
    fields = sensors.shape[1] // count

    own_one = jnp.tanh(dot(sensors, branch_first)).astype(BF16)
    blocks = sensors.reshape(own, count, fields).transpose(1, 0, 2)
    sent = jnp.concatenate(
        [jnp.broadcast_to(own_one[None], (count, own, own_one.shape[1])), blocks], axis=2
    )
    got = swap(sent)
    branch_one = got[:, :, : own_one.shape[1]].reshape(count * own, -1)
    sensor_columns = got[:, :, own_one.shape[1] :].reshape(count * own, fields)
    hidden_two = jnp.tanh(dot(branch_one, branch_second))
    branch_two = hidden_two.astype(BF16)
    features = dot(branch_two, branch_third).astype(BF16)
    block = lax.dynamic_slice_in_dim(features, lax.axis_index("func") * funcs, funcs, 0)
    feats = dot(block, trunk_third, NT).astype(BF16)

    u_part, second_part, const_part, value_part = trunk_call(
        coords, trunk_first, trunk_second, feats, forcing, weight, scale
    )
    first_part = value_part + const_part.T
    pieces = jnp.concatenate(
        [
            u_part.reshape(count, -1, LANES),
            second_part.reshape(count, -1, LANES),
            jnp.pad(
                first_part.reshape(count, 1, -1),
                ((0, 0), (0, 0), (0, LANES - first_part.size // count)),
            ),
        ],
        axis=1,
    ).astype(BF16)
    u_rows = funcs * width // count // LANES
    arrived = swap(pieces).astype(F32)
    u_sum = arrived[:, :u_rows].reshape(func_size, pts_size, u_rows, LANES).sum(1)
    rest = arrived[:, u_rows:].sum(0)
    summed = jnp.concatenate([u_sum.reshape(func_size * u_rows, LANES), rest], 0).astype(BF16)
    every = tell(summed, count)
    cut = func_size * u_rows
    u = (
        every[:, :cut]
        .reshape(count, func_size, u_rows, LANES)
        .transpose(1, 0, 2, 3)
        .reshape(func_size * funcs, width)
    )
    grad_t2 = every[:, cut:-1].astype(F32).reshape(trunk_second.shape)
    grad_t1 = (
        every[:, -1, : trunk_first.size // count].astype(F32).reshape(trunk_first.shape)
    )

    feature_back = (dot(u, trunk_third) * scale).astype(BF16)
    grad_t3 = dot(u, features, TN) * scale
    grad_b3 = dot(branch_two, feature_back, TN)
    back_two = (dot(feature_back, branch_third, NT) * (1.0 - hidden_two * hidden_two)).astype(BF16)
    grad_b2 = dot(branch_one, back_two, TN)
    hidden_one = branch_one.astype(F32)
    back_one = (dot(back_two, branch_second, NT) * (1.0 - hidden_one * hidden_one)).astype(BF16)
    own_rows = dot(sensor_columns, back_one, TN).astype(BF16)
    grad_b1 = tell(own_rows, count).reshape(branch_first.shape).astype(F32)
    return (grad_b1, grad_b2, grad_b3, grad_t1, grad_t2, grad_t3)


def solution(mesh):
    return jax.shard_map(
        per_device,
        mesh=mesh,
        in_specs=(
            P(("func", "pts"), None),
            P("func", "pts"),
            P(None, "pts"),
            P(),
            P(),
            P(),
            P(),
            P(),
            P(),
        ),
        out_specs=(P(), P(), P(), P(), P(), P()),
        check_vma=False,
    )
```

```python
import functools
import math

import jax
import jax.numpy as jnp
from jax import lax
from jax.experimental import pallas as pl
from jax.experimental.pallas import tpu as pltpu
from jax.sharding import PartitionSpec as P

DRAG = 0.5
PTS = 8
TILE = 512
ROWS = 16
LANES = 128
F32 = jnp.float32
BF16 = jnp.bfloat16
AXES = ("pairs", "core", "pts")
GROUP = (0, 1, 1, 2, 2, 2, 3, 3)
NT = (((1,), (1,)), ((), ()))
TN = (((0,), (0,)), ((), ()))
PARAMS = pltpu.CompilerParams(
    dimension_semantics=("arbitrary",), vmem_limit_bytes=48 * 1024 * 1024
)


def dot(left, right, dims=(((1,), (0,)), ((), ()))):
    return lax.dot_general(left, right, dims, preferred_element_type=F32)


def slopes(squash):
    square = squash * squash
    one = 1.0 - square
    two = -2.0 * (squash * one)
    three = one * (4.0 * square - 2.0 * one)
    return square, one, two, three


def chunks(shape, body, unroll):
    def one(index, carry):
        start = pl.multiple_of(index * ROWS, ROWS)
        for lane in range(0, shape[1], LANES):
            body(pl.ds(start, ROWS), pl.ds(lane, LANES))
        return carry

    lax.fori_loop(0, shape[0] // ROWS, one, 0, unroll=unroll)


def forward_kernel(values_ref, weights_ref, squash_ref, points_ref, inner_ref, combos_ref):
    def layer_one(rows, lanes):
        squash = jnp.tanh(values_ref[rows, lanes])
        _, one, two, three = slopes(squash)
        squash_ref[rows, lanes] = squash
        for group, part in enumerate((squash, one, two, three)):
            points_ref[group, rows, lanes] = part.astype(BF16)

    chunks(values_ref.shape, layer_one, 4)
    for part, group in enumerate(GROUP):
        inner_ref[part] = dot(points_ref[group], weights_ref[part])

    def layer_two(rows, lanes):
        z, zx, zy, lap, dif, mix, px, py = (inner_ref[part, rows, lanes] for part in range(8))
        squash = jnp.tanh(z)
        inner_ref[0, rows, lanes] = squash
        _, one, two, three = slopes(squash)
        radius = zx * zx + zy * zy
        twice = lap + lap
        bend = three * radius
        along = zx * (twice + dif) + zy * mix
        across = zy * (twice - dif) + zx * mix
        combos = (
            one * zx,
            one * zy,
            one * lap - two * radius,
            one * px + two * along - bend * zx,
            one * py + two * across - bend * zy,
        )
        for k, combo in enumerate(combos):
            combos_ref[k, rows, lanes] = combo.astype(BF16)

    chunks(values_ref.shape, layer_two, 4)


def project_kernel(weight, scale, feats_ref, combos_ref, forcing_ref, u_ref, cots_ref):
    @pl.when(pl.program_id(0) == 0)
    def _():
        u_ref[...] = jnp.zeros_like(u_ref)

    feats = feats_ref[...]
    px, py, om, omx, omy = (dot(feats, combos_ref[k], NT) * scale for k in range(5))
    slope = (py * omx - px * omy + DRAG * om - forcing_ref[...].astype(F32)) * weight
    total = u_ref[...]
    parts = (-slope * omy, slope * omx, DRAG * slope, slope * py, -slope * px)
    for k, part in enumerate(parts):
        cot = part.astype(BF16)
        cots_ref[k] = cot
        total += dot(cot, combos_ref[k])
    u_ref[...] = total


def backward_kernel(
    scale,
    squash_ref,
    points_ref,
    inner_ref,
    cots_ref,
    feats_ref,
    coords_ref,
    weights_ref,
    second_ref,
    consts_ref,
    pieces_ref,
    back_ref,
    inner_back_ref,
    ones_ref,
    one_back_ref,
    grads_ref,
    value_ref,
):
    step = pl.program_id(0)
    last = pl.num_programs(0) - 1
    width = second_ref.shape[0]

    @pl.when(step == 0)
    def _():
        grads_ref[...] = jnp.zeros_like(grads_ref)
        value_ref[...] = jnp.zeros_like(value_ref)

    feats = feats_ref[...]
    for k in range(5):
        back_ref[k] = dot(cots_ref[k], feats, TN) * scale

    def layer_two_back(rows, lanes):
        squash, zx, zy, lap, dif, mix, px, py = (inner_ref[part, rows, lanes] for part in range(8))
        gx, gy, gl, gp, gq = (back_ref[k, rows, lanes] for k in range(5))
        square, one, two, three = slopes(squash)
        four = two * (4.0 * square - 8.0 * one)
        radius = zx * zx + zy * zy
        twice = lap + lap
        plus, minus = twice + dif, twice - dif
        along = zx * plus + zy * mix
        across = zy * minus + zx * mix
        pull = gp * zx + gq * zy
        one_bar = gx * zx + gy * zy + gl * lap + gp * px + gq * py
        two_bar = gp * along + gq * across - gl * radius
        three_bar = pull * radius
        along_bar, across_bar = two * gp, two * gq
        turn = -2.0 * (two * gl + three * pull)
        bend = three * radius
        xa, yc = zx * along_bar, zy * across_bar
        parts = (
            two * one_bar + three * two_bar - four * three_bar,
            one * gx - bend * gp + zx * turn + along_bar * plus + across_bar * mix,
            one * gy - bend * gq + zy * turn + across_bar * minus + along_bar * mix,
            one * gl + 2.0 * (xa + yc),
            xa - yc,
            zy * along_bar + zx * across_bar,
            one * gp,
            one * gq,
        )
        for part, value in enumerate(parts):
            inner_back_ref[part, rows, lanes] = value.astype(BF16)

    chunks(squash_ref.shape, layer_two_back, 4)
    for part, group in enumerate(GROUP):
        grads_ref[part] += dot(points_ref[group], inner_back_ref[part], TN)
    for group in range(4):
        total = None
        for part in range(8):
            if GROUP[part] == group:
                term = dot(inner_back_ref[part], weights_ref[part], NT)
                total = term if total is None else total + term
        ones_ref[group] = total

    def layer_one_back(rows, lanes):
        square, one, two, three = slopes(squash_ref[rows, lanes])
        four = two * (4.0 * square - 8.0 * one)
        back = (
            one * ones_ref[0, rows, lanes]
            + two * ones_ref[1, rows, lanes]
            + three * ones_ref[2, rows, lanes]
            + four * ones_ref[3, rows, lanes]
        )
        one_back_ref[rows, lanes] = back.astype(BF16)

    chunks(squash_ref.shape, layer_one_back, 4)
    value_ref[...] += dot(coords_ref[...], one_back_ref[...])

    @pl.when(step == last)
    def _():
        second = second_ref[...].astype(F32)
        total = jnp.zeros((width, width), F32)
        first = [jnp.zeros((width, 1), F32)] * 2
        for part in range(8):
            grad = grads_ref[part]
            total += consts_ref[:, part : part + 1] * grad
            row = jnp.sum(second * grad, axis=1, keepdims=True)
            for axis in range(2):
                column = 8 * (axis + 1) + part
                first[axis] = first[axis] + consts_ref[:, column : column + 1] * row
        lane = lax.broadcasted_iota(jnp.int32, (width, LANES), 1)
        both = jnp.where(lane == 0, first[0], 0.0) + jnp.where(lane == 1, first[1], 0.0)
        first_grad = value_ref[0:2] + value_ref[2:4] + both.T[0:2]
        count, own, _ = pieces_ref.shape
        pieces_ref[...] = jnp.zeros_like(pieces_ref)
        across = width * width // (count * own)
        deep = LANES // across
        for core in range(2):
            for chunk in range(count // 2 // PTS):
                strip, row = divmod(chunk * PTS * own, width)
                lanes = core * LANES + strip * across
                place = (2 * chunk + core) * PTS
                block = total[row : row + PTS * own, lanes : lanes + across]
                pieces_ref[place : place + PTS, :, 0:across] = block.reshape(PTS, own, across)
            for axis in range(2):
                for strip in range(deep):
                    lanes = core * LANES + strip * across
                    row = axis * deep + strip
                    pieces_ref[core * PTS, row : row + 1, across : 2 * across] = first_grad[
                        axis : axis + 1, lanes : lanes + across
                    ]


def branch_kernel(
    scale,
    every_ref,
    two_ref,
    one_ref,
    columns_ref,
    third_ref,
    branch_third_ref,
    branch_second_ref,
    u_ref,
    feature_back_ref,
    back_two_ref,
    rows_ref,
):
    width = third_ref.shape[0]
    u = every_ref[:, :, 0:width].astype(F32).reshape(u_ref.shape).astype(BF16)
    u_ref[...] = u
    feature_back = (dot(u, third_ref[...]) * scale).astype(BF16)
    feature_back_ref[...] = feature_back
    two = two_ref[...]
    back_two = (dot(feature_back, branch_third_ref[...], NT) * (1.0 - two * two)).astype(BF16)
    back_two_ref[...] = back_two
    one = one_ref[...].astype(F32)
    back_one = (dot(back_two, branch_second_ref[...], NT) * (1.0 - one * one)).astype(BF16)
    rows = dot(columns_ref[...], back_one, TN)
    parts = [rows[:, lane : lane + LANES] for lane in range(0, rows.shape[1], LANES)]
    parts.append(jnp.sum(every_ref[:, :, width:].astype(F32), axis=0))
    rows_ref[...] = jnp.concatenate(parts, axis=0).astype(BF16)


def spread_kernel(core_ref, mine_ref, other_ref, grad_ref, second_ref, first_ref):
    half, step = pl.program_id(0), pl.program_id(1)
    fields = grad_ref.shape[0] // mine_ref.shape[0]
    own = mine_ref.shape[1] - 2 * fields
    across = LANES // 2
    steps = second_ref.shape[0] // own * 2 // mine_ref.shape[0]

    def place(from_ref):
        got = from_ref[...].astype(F32)
        for number in range(2):
            grad_ref[:, number * LANES : (number + 1) * LANES] = got[
                :, number * fields : (number + 1) * fields
            ].reshape(-1, LANES)
        tail = got[:, 2 * fields :]
        for now in range(steps):

            @pl.when(step == now)
            def _():
                strip, row = divmod(now * tail.shape[0] * own, second_ref.shape[0])
                second_ref[
                    row : row + tail.shape[0] * own, strip * across : (strip + 1) * across
                ] = tail[:, :, 0:across].reshape(-1, across)

        @pl.when(step == 0)
        def _():
            for axis in range(2):
                for strip in range(2):
                    row = 2 * axis + strip
                    first_ref[axis : axis + 1, strip * across : (strip + 1) * across] = tail[
                        0, row : row + 1, across : 2 * across
                    ]

    @pl.when(half == 0)
    def _():
        place(mine_ref)

    @pl.when(half == 1)
    def _():
        place(other_ref)


def whole(*shape):
    return pl.BlockSpec(shape, lambda i: (0,) * len(shape))


def constants(first):
    a, b = first[0], first[1]
    one, zero = jnp.ones_like(a), jnp.zeros_like(a)
    square = a * a + b * b
    consts = [one, a, b, -square, b * b - a * a, -2.0 * a * b, -a * square, -b * square]
    by_a = [zero, one, zero, -2.0 * a, -2.0 * a, -2.0 * b, -(3.0 * a * a + b * b), -2.0 * a * b]
    by_b = [zero, zero, one, -2.0 * b, 2.0 * b, -2.0 * a, -2.0 * a * b, -(a * a + 3.0 * b * b)]
    return consts, jnp.stack(consts + by_a + by_b, axis=1)


def tiles(points):
    tile = min(TILE, points)
    deep = lambda n, width: pl.BlockSpec((n, tile, width), lambda i: (0, i, 0))
    return tile, deep


def forward_call(values, weights):
    points, width = values.shape
    tile, deep = tiles(points)
    flat = pl.BlockSpec((tile, width), lambda i: (i, 0))
    return pl.pallas_call(
        forward_kernel,
        grid=(points // tile,),
        in_specs=[flat, whole(8, width, width)],
        out_specs=[flat, deep(4, width), deep(8, width), deep(5, width)],
        out_shape=[
            jax.ShapeDtypeStruct((points, width), F32),
            jax.ShapeDtypeStruct((4, points, width), BF16),
            jax.ShapeDtypeStruct((8, points, width), F32),
            jax.ShapeDtypeStruct((5, points, width), BF16),
        ],
        compiler_params=PARAMS,
        name="trunk_forward",
    )(values, weights)


def project_call(feats, combos, forcing, weight, scale):
    funcs, width = feats.shape
    points = combos.shape[1]
    tile, deep = tiles(points)
    return pl.pallas_call(
        functools.partial(project_kernel, weight, scale),
        grid=(points // tile,),
        in_specs=[
            whole(funcs, width),
            deep(5, width),
            pl.BlockSpec((funcs, tile), lambda i: (0, i)),
        ],
        out_specs=[whole(funcs, width), pl.BlockSpec((5, funcs, tile), lambda i: (0, 0, i))],
        out_shape=[
            jax.ShapeDtypeStruct((funcs, width), F32),
            jax.ShapeDtypeStruct((5, funcs, points), BF16),
        ],
        compiler_params=PARAMS,
        name="project",
    )(feats, combos, forcing)


def backward_call(squash, points_all, inner, cots, feats, coords, weights, second, consts, pieces, scale):
    points, width = squash.shape
    funcs = feats.shape[0]
    tile, deep = tiles(points)
    return pl.pallas_call(
        functools.partial(backward_kernel, scale),
        grid=(points // tile,),
        in_specs=[
            pl.BlockSpec((tile, width), lambda i: (i, 0)),
            deep(4, width),
            deep(8, width),
            pl.BlockSpec((5, funcs, tile), lambda i: (0, 0, i)),
            whole(funcs, width),
            pl.BlockSpec((16, tile), lambda i: (0, i)),
            whole(8, width, width),
            whole(width, width),
            whole(width, 24),
        ],
        out_specs=whole(*pieces),
        out_shape=jax.ShapeDtypeStruct(pieces, F32),
        scratch_shapes=[
            pltpu.VMEM((5, tile, width), F32),
            pltpu.VMEM((8, tile, width), BF16),
            pltpu.VMEM((4, tile, width), F32),
            pltpu.VMEM((tile, width), BF16),
            pltpu.VMEM((8, width, width), F32),
            pltpu.VMEM((16, width), F32),
        ],
        compiler_params=PARAMS,
        cost_estimate=pl.CostEstimate(
            flops=42 * points * width * width, bytes_accessed=48 * points * width, transcendentals=0
        ),
        name="trunk_backward",
    )(squash, points_all, inner, cots, feats, coords, weights, second, consts)


def branch_call(every, hidden_two, branch_one, columns, third, branch_third, branch_second, scale):
    shape = branch_one.shape
    rows = columns.shape[1] * (shape[1] // LANES) + every.shape[1]
    return pl.pallas_call(
        functools.partial(branch_kernel, scale),
        out_shape=[jax.ShapeDtypeStruct(shape, BF16)] * 3
        + [jax.ShapeDtypeStruct((rows, LANES), BF16)],
        compiler_params=pltpu.CompilerParams(vmem_limit_bytes=48 * 1024 * 1024),
        name="branch_backward",
    )(every, hidden_two, branch_one, columns, third, branch_third, branch_second)


def spread_call(core, mine, other, shape, width):
    steps = 4
    part = mine.shape[0] // steps
    half = lambda h, c: c[0] + h - 2 * c[0] * h
    block = (part, *mine.shape[1:])
    return pl.pallas_call(
        spread_kernel,
        grid_spec=pltpu.PrefetchScalarGridSpec(
            num_scalar_prefetch=1,
            grid=(2, steps),
            in_specs=[
                pl.BlockSpec(block, lambda h, j, c: (j * (1 - h) + (steps - 1) * h, 0, 0)),
                pl.BlockSpec(block, lambda h, j, c: (j * h, 0, 0)),
            ],
            out_specs=[
                pl.BlockSpec(
                    (shape[0] // (2 * steps), shape[1]),
                    lambda h, j, c: (half(h, c) * steps + j, 0),
                ),
                pl.BlockSpec((width, LANES), lambda h, j, c: (0, half(h, c))),
                pl.BlockSpec((2, LANES), lambda h, j, c: (0, half(h, c))),
            ],
        ),
        out_shape=[
            jax.ShapeDtypeStruct(shape, F32),
            jax.ShapeDtypeStruct((width, width), F32),
            jax.ShapeDtypeStruct((2, width), F32),
        ],
        compiler_params=pltpu.CompilerParams(
            dimension_semantics=("arbitrary", "arbitrary"), vmem_limit_bytes=48 * 1024 * 1024
        ),
        name="spread",
    )(core.reshape(1), mine, other)


def swap(parts, axes=AXES):
    return lax.all_to_all(parts, axes, split_axis=0, concat_axis=0, tiled=True)


def tell(part, count, axes=AXES):
    return swap(jnp.broadcast_to(part[None], (count, *part.shape)), axes)


def per_device(
    sensors,
    forcing,
    coords,
    branch_first,
    branch_second,
    branch_third,
    trunk_first,
    trunk_second,
    trunk_third,
):
    pairs, pts_size = lax.axis_size("pairs"), lax.axis_size("pts")
    func_size = 2 * pairs
    count = func_size * pts_size
    core = lax.axis_index("core")
    funcs = forcing.shape[0]
    weight = 1.0 / math.sqrt(funcs * func_size * forcing.shape[1] * pts_size)
    width_out = trunk_third.shape[1]
    width = trunk_second.shape[0]
    scale = width_out ** (-0.5)
    own = sensors.shape[0]
    fields = sensors.shape[1] // count

    own_one = jnp.tanh(dot(sensors, branch_first)).astype(BF16)
    blocks = (
        sensors.reshape(own, 2, pairs, pts_size, fields)
        .transpose(2, 1, 3, 0, 4)
        .reshape(count, own, fields)
    )
    sent = jnp.concatenate(
        [
            jnp.broadcast_to(own_one[None], (count, own, own_one.shape[1])),
            jnp.pad(blocks, ((0, 0), (0, 0), (0, LANES - fields))),
        ],
        axis=2,
    )
    got = swap(sent)

    consts, const_columns = constants(trunk_first)
    weights = (jnp.stack(consts)[:, :, None] * trunk_second.astype(F32)[None]).astype(BF16)
    values = coords[0][:, None] * trunk_first[0] + coords[1][:, None] * trunk_first[1]
    high = lax.reduce_precision(coords, 8, 7)
    coord_rows = jnp.pad(
        jnp.concatenate([high, coords - high], axis=0).astype(BF16), ((0, 12), (0, 0))
    )
    squash, points_all, inner, combos = forward_call(values, weights)

    branch_one = got[:, :, : own_one.shape[1]].reshape(count * own, -1)
    sensor_columns = got[:, :, own_one.shape[1] : own_one.shape[1] + fields].reshape(
        count * own, fields
    )
    hidden_two = jnp.tanh(dot(branch_one, branch_second))
    branch_two = hidden_two.astype(BF16)
    features = dot(branch_two, branch_third).astype(BF16)
    block = lax.dynamic_slice_in_dim(features, (2 * lax.axis_index("pairs") + core) * funcs, funcs, 0)
    feats = dot(block, trunk_third, NT).astype(BF16)

    u_part, cots = project_call(feats, combos, forcing, weight, scale)
    u_blocks = swap(u_part.astype(BF16).reshape(pts_size, own, width), "pts")
    u_own = u_blocks.astype(F32).sum(0).astype(BF16)

    second_pieces = backward_call(
        squash,
        points_all,
        inner,
        cots,
        feats,
        coord_rows,
        weights,
        trunk_second,
        const_columns,
        (count, own, LANES),
        scale,
    )
    pieces = jnp.concatenate(
        [jnp.broadcast_to(u_own[None], (count, own, width)), second_pieces.astype(BF16)], axis=2
    )
    every = swap(pieces)
    u, feature_back, back_two, rows = branch_call(
        every,
        hidden_two,
        branch_one,
        sensor_columns,
        trunk_third,
        branch_third,
        branch_second,
        scale,
    )
    mine = tell(rows, count // 2, ("pairs", "pts"))
    other = lax.ppermute(mine, "core", [(0, 1), (1, 0)])
    grad_b1, grad_t2, grad_t1 = spread_call(core, mine, other, branch_first.shape, width)
    grad_t3 = dot(u, features, TN) * scale
    grad_b3 = dot(branch_two, feature_back, TN)
    grad_b2 = dot(branch_one, back_two, TN)
    return (grad_b1, grad_b2, grad_b3, grad_t1, grad_t2, grad_t3)


def solution(mesh):
    func_size, pts_size = mesh.devices.shape
    cores = jax.sharding.Mesh(mesh.devices.reshape(func_size // 2, 2, pts_size), AXES)
    return jax.shard_map(
        per_device,
        mesh=cores,
        in_specs=(
            P(AXES, None),
            P(("pairs", "core"), "pts"),
            P(None, "pts"),
            P(),
            P(),
            P(),
            P(),
            P(),
            P(),
        ),
        out_specs=(P(), P(), P(), P(), P(), P()),
        check_vma=False,
    )
```

```python
import functools
import math

import jax
import jax.numpy as jnp
from jax import lax
from jax.experimental import pallas as pl
from jax.experimental.pallas import tpu as pltpu
from jax.sharding import PartitionSpec as P

DRAG = 0.5
TILE = 512
ROWS = 16
LANES = 128
F32 = jnp.float32
BF16 = jnp.bfloat16
AXES = ("pairs", "core", "pts")
GROUP = (0, 1, 1, 2, 2, 2, 3, 3)
NT = (((1,), (1,)), ((), ()))
TN = (((0,), (0,)), ((), ()))
PARAMS = pltpu.CompilerParams(
    dimension_semantics=("arbitrary",), vmem_limit_bytes=40 * 1024 * 1024
)
SMALL = pltpu.CompilerParams(vmem_limit_bytes=16 * 1024 * 1024)


def dot(left, right, dims=(((1,), (0,)), ((), ()))):
    return lax.dot_general(left, right, dims, preferred_element_type=F32)


def slopes(squash):
    square = squash * squash
    one = 1.0 - square
    two = -2.0 * (squash * one)
    three = one * (4.0 * square - 2.0 * one)
    return square, one, two, three


def chunks(shape, body, unroll):
    def one(index, carry):
        start = pl.multiple_of(index * ROWS, ROWS)
        for lane in range(0, shape[1], LANES):
            body(pl.ds(start, ROWS), pl.ds(lane, LANES))
        return carry

    lax.fori_loop(0, shape[0] // ROWS, one, 0, unroll=unroll)


def constants(first):
    a, b = first[0:1], first[1:2]
    one, zero = jnp.ones_like(a), jnp.zeros_like(a)
    square = a * a + b * b
    consts = [one, a, b, -square, b * b - a * a, -2.0 * a * b, -a * square, -b * square]
    by_a = [zero, one, zero, -2.0 * a, -2.0 * a, -2.0 * b, -(3.0 * a * a + b * b), -2.0 * a * b]
    by_b = [zero, zero, one, -2.0 * b, 2.0 * b, -2.0 * a, -2.0 * a * b, -(a * a + 3.0 * b * b)]
    return jnp.concatenate(consts + by_a + by_b, axis=0).T


def thirds(value):
    parts = []
    for _ in range(3):
        part = value.astype(BF16).astype(F32)
        parts.append(part)
        value = value - part
    return parts


def forward_kernel(
    coords_ref,
    first_ref,
    second_ref,
    squash_ref,
    points_ref,
    inner_ref,
    combos_ref,
    weights_ref,
    values_ref,
):
    @pl.when(pl.program_id(0) == 0)
    def _():
        consts = constants(first_ref[...])
        second = second_ref[...].astype(F32)
        for part in range(8):
            weights_ref[part] = (consts[:, part : part + 1] * second).astype(BF16)

    left, right = thirds(coords_ref[...]), thirds(first_ref[...])
    pairs = ((0, 0), (0, 1), (1, 0), (0, 2), (2, 0), (1, 1))
    left = [left[i] for i, _ in pairs] + [jnp.zeros_like(left[0])] * 2
    right = [right[j] for _, j in pairs] + [jnp.zeros_like(right[0])] * 2
    values_ref[...] = dot(
        jnp.concatenate(left, axis=0).astype(BF16), jnp.concatenate(right, axis=0).astype(BF16), TN
    )

    def layer_one(rows, lanes):
        squash = jnp.tanh(values_ref[rows, lanes])
        _, one, two, three = slopes(squash)
        squash_ref[rows, lanes] = squash
        for group, part in enumerate((squash, one, two, three)):
            points_ref[group, rows, lanes] = part.astype(BF16)

    chunks(values_ref.shape, layer_one, 4)
    for part, group in enumerate(GROUP):
        inner_ref[part] = dot(points_ref[group], weights_ref[part])

    def layer_two(rows, lanes):
        z, zx, zy, lap, dif, mix, px, py = (inner_ref[part, rows, lanes] for part in range(8))
        squash = jnp.tanh(z)
        inner_ref[0, rows, lanes] = squash
        _, one, two, three = slopes(squash)
        radius = zx * zx + zy * zy
        twice = lap + lap
        bend = three * radius
        along = zx * (twice + dif) + zy * mix
        across = zy * (twice - dif) + zx * mix
        combos = (
            one * zx,
            one * zy,
            one * lap - two * radius,
            one * px + two * along - bend * zx,
            one * py + two * across - bend * zy,
        )
        for k, combo in enumerate(combos):
            combos_ref[k, rows, lanes] = combo.astype(BF16)

    chunks(values_ref.shape, layer_two, 4)


def project_kernel(
    weight,
    scale,
    pair_ref,
    got_ref,
    branch_second_ref,
    branch_third_ref,
    third_ref,
    combos_ref,
    forcing_ref,
    u_ref,
    cots_ref,
    feats_ref,
):
    @pl.when(pl.program_id(0) == 0)
    def _():
        u_ref[...] = jnp.zeros_like(u_ref)
        width = third_ref.shape[0]
        one = got_ref[:, :, 0:width].astype(F32).reshape(-1, width).astype(BF16)
        two = jnp.tanh(dot(one, branch_second_ref[...])).astype(BF16)
        features = dot(two, branch_third_ref[...]).astype(BF16)
        feats_ref[...] = dot(features, third_ref[...], NT).astype(BF16)

    feats = feats_ref[...]
    px, py, om, omx, omy = (dot(feats, combos_ref[k], NT) * scale for k in range(5))
    slope = (py * omx - px * omy + DRAG * om - forcing_ref[...].astype(F32)) * weight
    total = u_ref[...]
    parts = (-slope * omy, slope * omx, DRAG * slope, slope * py, -slope * px)
    for k, part in enumerate(parts):
        cot = part.astype(BF16)
        cots_ref[k] = cot
        total += dot(cot, combos_ref[k])
    u_ref[...] = total


def backward_kernel(
    scale,
    squash_ref,
    points_ref,
    inner_ref,
    cots_ref,
    feats_ref,
    coords_ref,
    weights_ref,
    first_ref,
    second_ref,
    pieces_ref,
    back_ref,
    inner_back_ref,
    ones_ref,
    one_back_ref,
    grads_ref,
    value_ref,
):
    step = pl.program_id(0)
    last = pl.num_programs(0) - 1
    width = second_ref.shape[0]

    @pl.when(step == 0)
    def _():
        grads_ref[...] = jnp.zeros_like(grads_ref)
        value_ref[...] = jnp.zeros_like(value_ref)

    feats = feats_ref[...]
    for k in range(5):
        back_ref[k] = dot(cots_ref[k], feats, TN) * scale

    def layer_two_back(rows, lanes):
        squash, zx, zy, lap, dif, mix, px, py = (inner_ref[part, rows, lanes] for part in range(8))
        gx, gy, gl, gp, gq = (back_ref[k, rows, lanes] for k in range(5))
        square, one, two, three = slopes(squash)
        four = two * (4.0 * square - 8.0 * one)
        radius = zx * zx + zy * zy
        twice = lap + lap
        plus, minus = twice + dif, twice - dif
        along = zx * plus + zy * mix
        across = zy * minus + zx * mix
        pull = gp * zx + gq * zy
        one_bar = gx * zx + gy * zy + gl * lap + gp * px + gq * py
        two_bar = gp * along + gq * across - gl * radius
        three_bar = pull * radius
        along_bar, across_bar = two * gp, two * gq
        turn = -2.0 * (two * gl + three * pull)
        bend = three * radius
        xa, yc = zx * along_bar, zy * across_bar
        parts = (
            two * one_bar + three * two_bar - four * three_bar,
            one * gx - bend * gp + zx * turn + along_bar * plus + across_bar * mix,
            one * gy - bend * gq + zy * turn + across_bar * minus + along_bar * mix,
            one * gl + 2.0 * (xa + yc),
            xa - yc,
            zy * along_bar + zx * across_bar,
            one * gp,
            one * gq,
        )
        for part, value in enumerate(parts):
            inner_back_ref[part, rows, lanes] = value.astype(BF16)

    chunks(squash_ref.shape, layer_two_back, 4)
    for part, group in enumerate(GROUP):
        grads_ref[part] += dot(points_ref[group], inner_back_ref[part], TN)
    for group in range(4):
        total = None
        for part in range(8):
            if GROUP[part] == group:
                term = dot(inner_back_ref[part], weights_ref[part], NT)
                total = term if total is None else total + term
        ones_ref[group] = total

    def layer_one_back(rows, lanes):
        square, one, two, three = slopes(squash_ref[rows, lanes])
        four = two * (4.0 * square - 8.0 * one)
        back = (
            one * ones_ref[0, rows, lanes]
            + two * ones_ref[1, rows, lanes]
            + three * ones_ref[2, rows, lanes]
            + four * ones_ref[3, rows, lanes]
        )
        one_back_ref[rows, lanes] = back.astype(BF16)

    chunks(squash_ref.shape, layer_one_back, 4)
    coords = jnp.concatenate(thirds(coords_ref[...]) + [jnp.zeros_like(coords_ref)] * 5, axis=0)
    value_ref[...] += dot(coords.astype(BF16), one_back_ref[...])

    @pl.when(step == last)
    def _():
        second = second_ref[...].astype(F32)
        consts = constants(first_ref[...])
        total = jnp.zeros((width, width), F32)
        first = [jnp.zeros((width, 1), F32)] * 2
        for part in range(8):
            grad = grads_ref[part]
            total += consts[:, part : part + 1] * grad
            row = jnp.sum(second * grad, axis=1, keepdims=True)
            for axis in range(2):
                column = 8 * (axis + 1) + part
                first[axis] = first[axis] + consts[:, column : column + 1] * row
        lane = lax.broadcasted_iota(jnp.int32, (width, LANES), 1)
        both = jnp.where(lane == 0, first[0], 0.0) + jnp.where(lane == 1, first[1], 0.0)
        first_grad = value_ref[0:2] + value_ref[2:4] + value_ref[4:6] + both.T[0:2]
        count, own, _ = pieces_ref.shape
        strips = width // LANES
        part = count // strips
        for strip in range(strips):
            block = total[:, strip * LANES : (strip + 1) * LANES]
            pieces_ref[strip * part : (strip + 1) * part, :, 0:LANES] = block.reshape(
                part, own, LANES
            )
        rows = [
            first_grad[axis : axis + 1, strip * LANES : (strip + 1) * LANES]
            for axis in range(2)
            for strip in range(strips)
        ]
        rows.append(jnp.zeros((own - len(rows), LANES), F32))
        told = jnp.concatenate(rows, axis=0)
        pieces_ref[:, :, LANES:] = jnp.broadcast_to(told[None], (count, own, LANES))


def hidden_kernel(
    core_ref,
    mine_ref,
    other_ref,
    branch_second_ref,
    branch_third_ref,
    one_ref,
    wide_ref,
    two_ref,
    features_ref,
    columns_ref,
):
    core = core_ref[0]
    width = branch_second_ref.shape[0]
    half, fields = one_ref.shape[0] // 2, columns_ref.shape[1]
    for place, from_ref in ((core, mine_ref), (1 - core, other_ref)):
        rows = pl.ds(pl.multiple_of(place * half, half), half)
        got = from_ref[...].astype(F32).reshape(half, -1)
        one_ref[rows, :] = got[:, 0:width].astype(BF16)
        columns_ref[rows, :] = jnp.where(
            core == 0,
            got[:, width : width + fields],
            got[:, width + fields : width + 2 * fields],
        ).astype(BF16)
    wide = jnp.tanh(dot(one_ref[...], branch_second_ref[...]))
    wide_ref[...] = wide
    two = wide.astype(BF16)
    two_ref[...] = two
    features_ref[...] = dot(two, branch_third_ref[...]).astype(BF16)


def branch_kernel(
    scale,
    core_ref,
    mine_ref,
    other_ref,
    two_ref,
    one_ref,
    columns_ref,
    third_ref,
    branch_third_ref,
    branch_second_ref,
    u_ref,
    feature_back_ref,
    back_two_ref,
    rows_ref,
    first_ref,
):
    core = core_ref[0]
    width = third_ref.shape[0]
    half = u_ref.shape[0] // 2
    total = None
    for place, from_ref in ((core, mine_ref), (1 - core, other_ref)):
        rows = pl.ds(pl.multiple_of(place * half, half), half)
        u_ref[rows, :] = from_ref[:, :, 0:width].astype(F32).reshape(half, width).astype(BF16)
        part = jnp.sum(from_ref[:, :, width:].astype(F32), axis=0)
        total = part if total is None else total + part
    feature_back = (dot(u_ref[...], third_ref[...]) * scale).astype(BF16)
    feature_back_ref[...] = feature_back
    two = two_ref[...]
    back_two = (dot(feature_back, branch_third_ref[...], NT) * (1.0 - two * two)).astype(BF16)
    back_two_ref[...] = back_two
    one = one_ref[...].astype(F32)
    back_one = (dot(back_two, branch_second_ref[...], NT) * (1.0 - one * one)).astype(BF16)
    rows = dot(columns_ref[...], back_one, TN)
    parts = [rows[:, lane : lane + LANES] for lane in range(0, width, LANES)]
    rows_ref[...] = jnp.concatenate(parts + [total[:, 0:LANES]], axis=0).astype(BF16)
    strips = width // LANES
    for axis in range(2):
        for strip in range(strips):
            first_ref[axis : axis + 1, strip * LANES : (strip + 1) * LANES] = total[
                axis * strips + strip : axis * strips + strip + 1, LANES:
            ]


def gradient_kernel(
    scale,
    u_ref,
    features_ref,
    two_ref,
    feature_back_ref,
    one_ref,
    back_two_ref,
    trunk_ref,
    third_ref,
    second_ref,
):
    trunk_ref[...] = dot(u_ref[...], features_ref[...], TN) * scale
    third_ref[...] = dot(two_ref[...], feature_back_ref[...], TN)
    second_ref[...] = dot(one_ref[...], back_two_ref[...], TN)


def spread_kernel(core_ref, mine_ref, other_ref, grad_ref, second_ref):
    first = core_ref[0] == 0
    step = pl.program_id(0)
    count = mine_ref.shape[0]
    fields = grad_ref.shape[0] // (2 * count)
    mine, other = mine_ref[...].astype(F32), other_ref[...].astype(F32)
    for lane in range(grad_ref.shape[1] // LANES):
        parts = [got[:, lane * fields : (lane + 1) * fields] for got in (mine, other)]
        block = jnp.stack(
            [jnp.where(first, parts[0], parts[1]), jnp.where(first, parts[1], parts[0])], axis=1
        )
        grad_ref[:, lane * LANES : (lane + 1) * LANES] = block.reshape(-1, LANES)
    tail = mine[:, -8:].reshape(-1, LANES)
    width = second_ref.shape[0]
    for now in range(width * width // tail.size):

        @pl.when(step == now)
        def _():
            strip, row = divmod(now * tail.shape[0], width)
            second_ref[row : row + tail.shape[0], strip * LANES : (strip + 1) * LANES] = tail


def whole(*shape):
    return pl.BlockSpec(shape, lambda i: (0,) * len(shape))


def there(value):
    return pltpu.with_memory_space_constraint(value, pltpu.HBM)


SCALAR = pl.BlockSpec(memory_space=pltpu.SMEM)
LOCAL = pl.BlockSpec(memory_space=pltpu.VMEM)


def tiles(points):
    tile = min(TILE, points)
    deep = lambda n, width: pl.BlockSpec((n, tile, width), lambda i: (0, i, 0))
    return tile, deep


def forward_call(coords, first, second):
    points, width = coords.shape[1], first.shape[1]
    tile, deep = tiles(points)
    flat = pl.BlockSpec((tile, width), lambda i: (i, 0))
    return pl.pallas_call(
        forward_kernel,
        grid=(points // tile,),
        in_specs=[
            pl.BlockSpec((2, tile), lambda i: (0, i)),
            whole(2, width),
            whole(width, width),
        ],
        out_specs=[flat, deep(4, width), deep(8, width), deep(5, width), whole(8, width, width)],
        out_shape=[
            pltpu.HBM((points, width), F32),
            pltpu.HBM((4, points, width), BF16),
            pltpu.HBM((8, points, width), F32),
            pltpu.HBM((5, points, width), BF16),
            pltpu.HBM((8, width, width), BF16),
        ],
        scratch_shapes=[pltpu.VMEM((tile, width), F32)],
        compiler_params=PARAMS,
        name="trunk_forward",
    )(coords, first, second)


def project_call(
    pair, got, branch_second, branch_third, third, combos, forcing, pts_size, weight, scale
):
    funcs, points = forcing.shape
    width = third.shape[0]
    tile, _ = tiles(points)
    flat = lambda *shape: pl.BlockSpec(shape, lambda i, p: (0,) * len(shape))
    return pl.pallas_call(
        functools.partial(project_kernel, weight, scale),
        grid_spec=pltpu.PrefetchScalarGridSpec(
            num_scalar_prefetch=1,
            grid=(points // tile,),
            in_specs=[
                pl.BlockSpec((pts_size, *got.shape[1:]), lambda i, p: (p[0], 0, 0)),
                flat(width, width),
                flat(width, width),
                flat(width, width),
                pl.BlockSpec((5, tile, width), lambda i, p: (0, i, 0)),
                pl.BlockSpec((funcs, tile), lambda i, p: (0, i)),
            ],
            out_specs=[
                flat(funcs, width),
                pl.BlockSpec((5, funcs, tile), lambda i, p: (0, 0, i)),
                flat(funcs, width),
            ],
        ),
        out_shape=[
            jax.ShapeDtypeStruct((funcs, width), F32),
            pltpu.HBM((5, funcs, points), BF16),
            pltpu.HBM((funcs, width), BF16),
        ],
        compiler_params=PARAMS,
        name="project",
    )(pair, there(got), branch_second, branch_third, third, there(combos), there(forcing))


def backward_call(
    squash, points_all, inner, cots, feats, coords, weights, first, second, pieces, scale
):
    points, width = squash.shape
    funcs = feats.shape[0]
    tile, deep = tiles(points)
    return pl.pallas_call(
        functools.partial(backward_kernel, scale),
        grid=(points // tile,),
        in_specs=[
            pl.BlockSpec((tile, width), lambda i: (i, 0)),
            deep(4, width),
            deep(8, width),
            pl.BlockSpec((5, funcs, tile), lambda i: (0, 0, i)),
            whole(funcs, width),
            pl.BlockSpec((2, tile), lambda i: (0, i)),
            whole(8, width, width),
            whole(2, width),
            whole(width, width),
        ],
        out_specs=whole(*pieces),
        out_shape=jax.ShapeDtypeStruct(pieces, F32),
        scratch_shapes=[
            pltpu.VMEM((5, tile, width), F32),
            pltpu.VMEM((8, tile, width), BF16),
            pltpu.VMEM((4, tile, width), F32),
            pltpu.VMEM((tile, width), BF16),
            pltpu.VMEM((8, width, width), F32),
            pltpu.VMEM((16, width), F32),
        ],
        compiler_params=PARAMS,
        cost_estimate=pl.CostEstimate(
            flops=42 * points * width * width, bytes_accessed=48 * points * width, transcendentals=0
        ),
        name="trunk_backward",
    )(
        there(squash),
        there(points_all),
        there(inner),
        there(cots),
        there(feats),
        coords,
        there(weights),
        first,
        second,
    )


def hidden_call(core, mine, other, branch_second, branch_third, fields):
    rows, width = 2 * mine.shape[0] * mine.shape[1], branch_second.shape[0]
    return pl.pallas_call(
        hidden_kernel,
        in_specs=[SCALAR] + [LOCAL] * 4,
        out_shape=[
            jax.ShapeDtypeStruct((rows, width), BF16),
            jax.ShapeDtypeStruct((rows, width), F32),
            jax.ShapeDtypeStruct((rows, width), BF16),
            jax.ShapeDtypeStruct((rows, width), BF16),
            jax.ShapeDtypeStruct((rows, fields), BF16),
        ],
        compiler_params=SMALL,
        name="branch_hidden",
    )(core, mine, other, branch_second, branch_third)


def branch_call(core, mine, other, two, one, columns, third, branch_third, branch_second, scale):
    shape = one.shape
    rows = columns.shape[1] * (shape[1] // LANES) + mine.shape[1]
    return pl.pallas_call(
        functools.partial(branch_kernel, scale),
        in_specs=[SCALAR] + [LOCAL] * 8,
        out_shape=[jax.ShapeDtypeStruct(shape, BF16)] * 3
        + [jax.ShapeDtypeStruct((rows, LANES), BF16), jax.ShapeDtypeStruct((2, shape[1]), F32)],
        compiler_params=SMALL,
        name="branch_backward",
    )(core, mine, other, two, one, columns, third, branch_third, branch_second)


def gradient_call(u, features, two, feature_back, one, back_two, scale):
    shape = (u.shape[1], features.shape[1])
    return pl.pallas_call(
        functools.partial(gradient_kernel, scale),
        in_specs=[LOCAL] * 6,
        out_shape=[jax.ShapeDtypeStruct(shape, F32)] * 3,
        compiler_params=SMALL,
        name="branch_gradients",
    )(u, features, two, feature_back, one, back_two)


def spread_call(core, mine, other, shape, width):
    steps = 4
    block = (mine.shape[0] // steps, *mine.shape[1:])
    piece = pl.BlockSpec(block, lambda j: (j, 0, 0))
    return pl.pallas_call(
        spread_kernel,
        grid=(steps,),
        in_specs=[SCALAR, piece, piece],
        out_specs=[
            pl.BlockSpec((shape[0] // steps, shape[1]), lambda j: (j, 0)),
            whole(width, width),
        ],
        out_shape=[jax.ShapeDtypeStruct(shape, F32), jax.ShapeDtypeStruct((width, width), F32)],
        compiler_params=PARAMS,
        name="spread",
    )(core, mine, other)


def swap(parts, axes):
    return lax.all_to_all(parts, axes, split_axis=0, concat_axis=0, tiled=True)


def across_chip(value):
    return lax.ppermute(value, "core", [(0, 1), (1, 0)])


def per_device(
    sensors,
    forcing,
    coords,
    branch_first,
    branch_second,
    branch_third,
    trunk_first,
    trunk_second,
    trunk_third,
):
    pairs, pts_size = lax.axis_size("pairs"), lax.axis_size("pts")
    func_size = 2 * pairs
    chips = pairs * pts_size
    core = lax.axis_index("core").reshape(1)
    pair = lax.axis_index("pairs").reshape(1)
    funcs = forcing.shape[0]
    weight = 1.0 / math.sqrt(funcs * func_size * forcing.shape[1] * pts_size)
    width_out = trunk_third.shape[1]
    width = trunk_second.shape[0]
    scale = width_out ** (-0.5)
    own = sensors.shape[0]
    fields = sensors.shape[1] // chips

    own_one = jnp.tanh(dot(sensors, branch_first)).astype(BF16)
    blocks = sensors.reshape(own, chips, fields).transpose(1, 0, 2)
    sent = jnp.concatenate(
        [
            jnp.broadcast_to(own_one[None], (chips, own, width)),
            jnp.pad(blocks, ((0, 0), (0, 0), (0, -fields % LANES))),
        ],
        axis=2,
    )
    got = swap(sent, ("pairs", "pts"))
    squash, points_all, inner, combos, weights = forward_call(coords, trunk_first, trunk_second)
    u_part, cots, feats = project_call(
        pair,
        got,
        branch_second,
        branch_third,
        trunk_third,
        combos,
        forcing,
        pts_size,
        weight,
        scale,
    )
    got_other = across_chip(got)

    u_blocks = swap(u_part.astype(BF16).reshape(pts_size, own, width), "pts")
    u_own = u_blocks.astype(F32).sum(0).astype(BF16)
    second_pieces = backward_call(
        squash,
        points_all,
        inner,
        cots,
        feats,
        coords,
        weights,
        trunk_first,
        trunk_second,
        (chips, own, 2 * LANES),
        scale,
    )
    pieces = jnp.concatenate(
        [jnp.broadcast_to(u_own[None], (chips, own, width)), second_pieces.astype(BF16)], axis=2
    )
    every = swap(pieces, ("pairs", "pts"))
    every_other = across_chip(every)

    one, wide, two, features, columns = hidden_call(
        core, got, got_other, branch_second, branch_third, fields // 2
    )
    u, feature_back, back_two, rows, grad_t1 = branch_call(
        core,
        every,
        every_other,
        wide,
        one,
        columns,
        trunk_third,
        branch_third,
        branch_second,
        scale,
    )
    mine = swap(jnp.broadcast_to(rows[None], (chips, *rows.shape)), ("pairs", "pts"))
    other = across_chip(mine)
    grad_t3, grad_b3, grad_b2 = gradient_call(
        u, features, two, feature_back, one, back_two, scale
    )
    grad_b1, grad_t2 = spread_call(core, mine, other, branch_first.shape, width)
    return (grad_b1, grad_b2, grad_b3, grad_t1, grad_t2, grad_t3)


def solution(mesh):
    func_size, pts_size = mesh.devices.shape
    cores = jax.sharding.Mesh(mesh.devices.reshape(func_size // 2, 2, pts_size), AXES)
    return jax.shard_map(
        per_device,
        mesh=cores,
        in_specs=(
            P(AXES, None),
            P(("pairs", "core"), "pts"),
            P(None, "pts"),
            P(),
            P(),
            P(),
            P(),
            P(),
            P(),
        ),
        out_specs=(P(), P(), P(), P(), P(), P()),
        check_vma=False,
    )
```

```python
import functools
import math

import jax
import jax.numpy as jnp
from jax import lax
from jax.experimental import pallas as pl
from jax.experimental.pallas import tpu as pltpu
from jax.sharding import PartitionSpec as P

DRAG = 0.5
TILE = 512
PROJECT = 1024
ROWS = 16
PARTS = 2
CHUNK = 256
LANES = 128
F32 = jnp.float32
BF16 = jnp.bfloat16
AXES = ("pairs", "core", "pts")
GROUP = (0, 1, 1, 2, 2, 2, 3, 3)
NT = (((1,), (1,)), ((), ()))
TN = (((0,), (0,)), ((), ()))
PARAMS = pltpu.CompilerParams(
    dimension_semantics=("arbitrary",), vmem_limit_bytes=40 * 1024 * 1024
)
SMALL = pltpu.CompilerParams(vmem_limit_bytes=24 * 1024 * 1024)


def dot(left, right, dims=(((1,), (0,)), ((), ()))):
    return lax.dot_general(left, right, dims, preferred_element_type=F32)


def slopes(squash):
    square = squash * squash
    one = 1.0 - square
    two = -2.0 * (squash * one)
    three = one * (4.0 * square - 2.0 * one)
    return square, one, two, three


def chunks(rows, width, body):
    for start in range(*rows, ROWS):
        for lane in range(0, width, LANES):
            body(pl.ds(start, ROWS), pl.ds(lane, LANES))


def constants(first):
    a, b = first[0:1], first[1:2]
    one, zero = jnp.ones_like(a), jnp.zeros_like(a)
    square = a * a + b * b
    consts = [one, a, b, -square, b * b - a * a, -2.0 * a * b, -a * square, -b * square]
    by_a = [zero, one, zero, -2.0 * a, -2.0 * a, -2.0 * b, -(3.0 * a * a + b * b), -2.0 * a * b]
    by_b = [zero, zero, one, -2.0 * b, 2.0 * b, -2.0 * a, -2.0 * a * b, -(a * a + 3.0 * b * b)]
    return jnp.concatenate(consts + by_a + by_b, axis=0).T


def thirds(value):
    parts = []
    for _ in range(3):
        part = value.astype(BF16).astype(F32)
        parts.append(part)
        value = value - part
    return parts


def forward_kernel(
    coords_ref,
    first_ref,
    second_ref,
    points_ref,
    squash_ref,
    inner_ref,
    combos_ref,
    weights_ref,
    values_ref,
    wide_ref,
):
    @pl.when(pl.program_id(0) == 0)
    def _():
        consts = constants(first_ref[...])
        second = second_ref[...].astype(F32)
        for part in range(8):
            weights_ref[part] = (consts[:, part : part + 1] * second).astype(BF16)

    left, right = thirds(coords_ref[...]), thirds(first_ref[...])
    pairs = ((0, 0), (0, 1), (1, 0), (0, 2), (2, 0), (1, 1))
    left = [left[i] for i, _ in pairs] + [jnp.zeros_like(left[0])] * 2
    right = [right[j] for _, j in pairs] + [jnp.zeros_like(right[0])] * 2
    values_ref[...] = dot(
        jnp.concatenate(left, axis=0).astype(BF16), jnp.concatenate(right, axis=0).astype(BF16), TN
    )

    def layer_one(rows, lanes):
        squash = jnp.tanh(values_ref[rows, lanes])
        _, one, two, three = slopes(squash)
        for group, part in enumerate((squash, one, two, three)):
            points_ref[group, rows, lanes] = part.astype(BF16)


    def layer_two(rows, lanes):
        z, zx, zy, lap, dif, mix, px, py = (wide_ref[part, rows, lanes] for part in range(8))
        squash = jnp.tanh(z)
        squash_ref[rows, lanes] = squash
        for part, value in enumerate((zx, zy, lap, dif, mix, px, py)):
            inner_ref[part, rows, lanes] = value.astype(BF16)
        _, one, two, three = slopes(squash)
        radius = zx * zx + zy * zy
        twice = lap + lap
        bend = three * radius
        along = zx * (twice + dif) + zy * mix
        across = zy * (twice - dif) + zx * mix
        combos = (
            one * zx,
            one * zy,
            one * lap - two * radius,
            one * px + two * along - bend * zx,
            one * py + two * across - bend * zy,
        )
        for k, combo in enumerate(combos):
            combos_ref[k, rows, lanes] = combo.astype(BF16)

    tile, width = values_ref.shape
    part_rows = tile // max(1, min(PARTS, tile // LANES))
    for start in range(0, tile, part_rows):
        rows = (start, start + part_rows)
        chunks(rows, width, layer_one)
        span = pl.ds(start, part_rows)
        for part, group in enumerate(GROUP):
            wide_ref[part, span] = dot(points_ref[group, span], weights_ref[part])
    for start in range(0, tile, part_rows):
        chunks((start, start + part_rows), width, layer_two)


def project_kernel(
    weight,
    scale,
    ones_ref,
    branch_second_ref,
    branch_third_ref,
    third_ref,
    combos_ref,
    forcing_ref,
    cots_ref,
    feats_ref,
    shares_ref,
    u_ref,
):
    @pl.when(pl.program_id(0) == 0)
    def _():
        u_ref[...] = jnp.zeros_like(u_ref)
        one = ones_ref[...].astype(F32).reshape(u_ref.shape).astype(BF16)
        two = jnp.tanh(dot(one, branch_second_ref[...])).astype(BF16)
        features = dot(two, branch_third_ref[...]).astype(BF16)
        feats_ref[...] = dot(features, third_ref[...], NT).astype(BF16)

    feats = feats_ref[...]
    tile = forcing_ref.shape[1]
    for start in range(0, tile, min(CHUNK, tile)):
        span = pl.ds(start, min(CHUNK, tile))
        px, py, om, omx, omy = (dot(feats, combos_ref[k, span], NT) * scale for k in range(5))
        residual = py * omx - px * omy + DRAG * om - forcing_ref[:, span].astype(F32)
        slope = residual * weight
        parts = (-slope * omy, slope * omx, DRAG * slope, slope * py, -slope * px)
        for k, part in enumerate(parts):
            cots_ref[k, :, span] = part.astype(BF16)
    total = u_ref[...]
    for k in range(5):
        total += dot(cots_ref[k], combos_ref[k])
    u_ref[...] = total

    @pl.when(pl.program_id(0) == pl.num_programs(0) - 1)
    def _():
        shares_ref[...] = u_ref[...].reshape(shares_ref.shape).astype(BF16)


def backward_kernel(
    scale,
    squash_ref,
    points_ref,
    inner_ref,
    cots_ref,
    feats_ref,
    coords_ref,
    weights_ref,
    first_ref,
    second_ref,
    pieces_ref,
    back_ref,
    inner_back_ref,
    ones_ref,
    one_back_ref,
    grads_ref,
    value_ref,
):
    step = pl.program_id(0)
    last = pl.num_programs(0) - 1
    width = second_ref.shape[0]

    @pl.when(step == 0)
    def _():
        grads_ref[...] = jnp.zeros_like(grads_ref)
        value_ref[...] = jnp.zeros_like(value_ref)

    feats = feats_ref[...]

    def layer_two_back(rows, lanes):
        squash = squash_ref[rows, lanes]
        zx, zy, lap, dif, mix, px, py = (
            inner_ref[part, rows, lanes].astype(F32) for part in range(7)
        )
        gx, gy, gl, gp, gq = (back_ref[k, rows, lanes] for k in range(5))
        square, one, two, three = slopes(squash)
        four = two * (4.0 * square - 8.0 * one)
        radius = zx * zx + zy * zy
        twice = lap + lap
        plus, minus = twice + dif, twice - dif
        along = zx * plus + zy * mix
        across = zy * minus + zx * mix
        pull = gp * zx + gq * zy
        one_bar = gx * zx + gy * zy + gl * lap + gp * px + gq * py
        two_bar = gp * along + gq * across - gl * radius
        three_bar = pull * radius
        along_bar, across_bar = two * gp, two * gq
        turn = -2.0 * (two * gl + three * pull)
        bend = three * radius
        xa, yc = zx * along_bar, zy * across_bar
        parts = (
            two * one_bar + three * two_bar - four * three_bar,
            one * gx - bend * gp + zx * turn + along_bar * plus + across_bar * mix,
            one * gy - bend * gq + zy * turn + across_bar * minus + along_bar * mix,
            one * gl + 2.0 * (xa + yc),
            xa - yc,
            zy * along_bar + zx * across_bar,
            one * gp,
            one * gq,
        )
        for part, value in enumerate(parts):
            inner_back_ref[part, rows, lanes] = value.astype(BF16)

    def layer_one_back(rows, lanes):
        squash, one, two, three = (points_ref[part, rows, lanes].astype(F32) for part in range(4))
        four = two * (4.0 * (squash * squash) - 8.0 * one)
        back = (
            one * ones_ref[0, rows, lanes]
            + two * ones_ref[1, rows, lanes]
            + three * ones_ref[2, rows, lanes]
            + four * ones_ref[3, rows, lanes]
        )
        one_back_ref[rows, lanes] = back.astype(BF16)

    tile = squash_ref.shape[0]
    part_rows = tile // max(1, min(PARTS, tile // LANES))
    spans = [(start, start + part_rows) for start in range(0, tile, part_rows)]
    for start, stop in spans:
        for k in range(5):
            back_ref[k, start:stop] = dot(cots_ref[k, :, start:stop], feats, TN) * scale
    for start, stop in spans:
        chunks((start, stop), width, layer_two_back)
        for group in range(4):
            total = None
            for part in range(8):
                if GROUP[part] == group:
                    term = dot(inner_back_ref[part, start:stop], weights_ref[part], NT)
                    total = term if total is None else total + term
            ones_ref[group, start:stop] = total
    for part, group in enumerate(GROUP):
        grads_ref[part] += dot(points_ref[group], inner_back_ref[part], TN)
    for start, stop in spans:
        chunks((start, stop), width, layer_one_back)
    coords = jnp.concatenate(thirds(coords_ref[...]) + [jnp.zeros_like(coords_ref)] * 5, axis=0)
    value_ref[...] += dot(coords.astype(BF16), one_back_ref[...])

    @pl.when(step == last)
    def _():
        second = second_ref[...].astype(F32)
        consts = constants(first_ref[...])
        g = [grads_ref[part] for part in range(8)]
        column = lambda part: consts[:, part : part + 1]
        total = g[0]
        for part in range(1, 8):
            total += column(part) * g[part]
        both, less = g[3] + g[4], g[3] - g[4]
        by_a = g[1] + column(11) * both + column(13) * g[5] + column(14) * g[6] + column(15) * g[7]
        by_b = g[2] + column(19) * less + column(21) * g[5] + column(22) * g[6] + column(23) * g[7]
        first = [jnp.sum(second * by, axis=1, keepdims=True) for by in (by_a, by_b)]
        lane = lax.broadcasted_iota(jnp.int32, (width, LANES), 1)
        both = jnp.where(lane == 0, first[0], 0.0) + jnp.where(lane == 1, first[1], 0.0)
        first_grad = value_ref[0:2] + value_ref[2:4] + value_ref[4:6] + both.T[0:2]
        count, own, _ = pieces_ref.shape
        strips = width // LANES
        part = count // strips
        for strip in range(strips):
            block = total[:, strip * LANES : (strip + 1) * LANES]
            pieces_ref[strip * part : (strip + 1) * part, :, 0:LANES] = block.reshape(
                part, own, LANES
            )
        across = 2 * width // own
        rows = [
            first_grad[axis : axis + 1, lane : lane + across]
            for axis in range(2)
            for lane in range(0, width, across)
        ]
        told = jnp.concatenate(rows, axis=0)
        pieces_ref[:, :, LANES:] = jnp.broadcast_to(told[None], (count, *told.shape))


def branch_kernel(
    scale,
    core_ref,
    mine_ref,
    other_ref,
    third_ref,
    branch_third_ref,
    branch_second_ref,
    u_ref,
    features_ref,
    two_ref,
    feature_back_ref,
    one_ref,
    back_two_ref,
    rows_ref,
    first_ref,
    columns_ref,
):
    core = core_ref[0]
    width = third_ref.shape[0]
    half, fields = u_ref.shape[0] // 2, columns_ref.shape[1]
    across = 2 * width // mine_ref.shape[1]
    here = width + LANES + across
    total = None
    for place, from_ref in ((core, mine_ref), (1 - core, other_ref)):
        rows = pl.ds(pl.multiple_of(place * half, half), half)
        got = from_ref[...].astype(F32)
        part = jnp.sum(got[:, :, width : width + 2 * LANES], axis=0)
        total = part if total is None else total + part
        got = got.reshape(half, -1)
        u_ref[rows, :] = got[:, 0:width].astype(BF16)
        one_ref[rows, :] = got[:, width + 2 * LANES :].astype(BF16)
        columns_ref[rows, :] = jnp.where(
            core == 0,
            got[:, here : here + fields],
            got[:, here + fields : here + 2 * fields],
        ).astype(BF16)
    wide = jnp.tanh(dot(one_ref[...], branch_second_ref[...]))
    two_ref[...] = wide.astype(BF16)
    features_ref[...] = dot(two_ref[...], branch_third_ref[...]).astype(BF16)
    feature_back = (dot(u_ref[...], third_ref[...]) * scale).astype(BF16)
    feature_back_ref[...] = feature_back
    back_two = (dot(feature_back, branch_third_ref[...], NT) * (1.0 - wide * wide)).astype(BF16)
    back_two_ref[...] = back_two
    one = one_ref[...].astype(F32)
    back_one = (dot(back_two, branch_second_ref[...], NT) * (1.0 - one * one)).astype(BF16)
    rows = dot(columns_ref[...], back_one, TN)
    parts = [rows[:, lane : lane + LANES] for lane in range(0, width, LANES)]
    rows_ref[...] = jnp.concatenate(parts + [total[:, 0:LANES]], axis=0).astype(BF16)
    deep = width // across
    for axis in range(2):
        for strip in range(deep):
            first_ref[axis : axis + 1, strip * across : (strip + 1) * across] = total[
                axis * deep + strip : axis * deep + strip + 1, LANES : LANES + across
            ]


def gradient_kernel(
    scale,
    u_ref,
    features_ref,
    two_ref,
    feature_back_ref,
    one_ref,
    back_two_ref,
    trunk_ref,
    third_ref,
    second_ref,
):
    trunk_ref[...] = dot(u_ref[...], features_ref[...], TN) * scale
    third_ref[...] = dot(two_ref[...], feature_back_ref[...], TN)
    second_ref[...] = dot(one_ref[...], back_two_ref[...], TN)


def spread_kernel(core_ref, mine_ref, other_ref, grad_ref, second_ref):
    first = core_ref[0] == 0
    step = pl.program_id(0)
    count = mine_ref.shape[0]
    fields = grad_ref.shape[0] // (2 * count)
    mine, other = mine_ref[...].astype(F32), other_ref[...].astype(F32)
    for lane in range(grad_ref.shape[1] // LANES):
        parts = [got[:, lane * fields : (lane + 1) * fields] for got in (mine, other)]
        block = jnp.stack(
            [jnp.where(first, parts[0], parts[1]), jnp.where(first, parts[1], parts[0])], axis=1
        )
        grad_ref[:, lane * LANES : (lane + 1) * LANES] = block.reshape(-1, LANES)
    tail = mine[:, -8:].reshape(-1, LANES)
    width = second_ref.shape[0]
    for now in range(width * width // tail.size):

        @pl.when(step == now)
        def _():
            strip, row = divmod(now * tail.shape[0], width)
            second_ref[row : row + tail.shape[0], strip * LANES : (strip + 1) * LANES] = tail


def whole(*shape):
    return pl.BlockSpec(shape, lambda i: (0,) * len(shape))


def there(value):
    return pltpu.with_memory_space_constraint(value, pltpu.HBM)


SCALAR = pl.BlockSpec(memory_space=pltpu.SMEM)
LOCAL = pl.BlockSpec(memory_space=pltpu.VMEM)


def tiles(points):
    tile = min(TILE, points)
    deep = lambda n, width: pl.BlockSpec((n, tile, width), lambda i: (0, i, 0))
    return tile, deep


def forward_call(coords, first, second):
    points, width = coords.shape[1], first.shape[1]
    tile, deep = tiles(points)
    flat = pl.BlockSpec((tile, width), lambda i: (i, 0))
    return pl.pallas_call(
        forward_kernel,
        grid=(points // tile,),
        in_specs=[
            pl.BlockSpec((2, tile), lambda i: (0, i)),
            whole(2, width),
            whole(width, width),
        ],
        out_specs=[deep(4, width), flat, deep(7, width), deep(5, width), whole(8, width, width)],
        out_shape=[
            pltpu.HBM((4, points, width), BF16),
            pltpu.HBM((points, width), F32),
            pltpu.HBM((7, points, width), BF16),
            pltpu.HBM((5, points, width), BF16),
            pltpu.HBM((8, width, width), BF16),
        ],
        scratch_shapes=[pltpu.VMEM((tile, width), F32), pltpu.VMEM((8, tile, width), F32)],
        compiler_params=PARAMS,
        name="trunk_forward",
    )(coords, first, second)


def project_call(ones, branch_second, branch_third, third, combos, forcing, weight, scale):
    funcs, points = forcing.shape
    width = third.shape[0]
    tile = min(PROJECT, points)
    return pl.pallas_call(
        functools.partial(project_kernel, weight, scale),
        grid=(points // tile,),
        in_specs=[
            whole(*ones.shape),
            whole(width, width),
            whole(width, width),
            whole(width, width),
            pl.BlockSpec((5, tile, width), lambda i: (0, i, 0)),
            pl.BlockSpec((funcs, tile), lambda i: (0, i)),
        ],
        out_specs=[
            pl.BlockSpec((5, funcs, tile), lambda i: (0, 0, i)),
            whole(funcs, width),
            whole(*ones.shape),
        ],
        out_shape=[
            pltpu.HBM((5, funcs, points), BF16),
            pltpu.HBM((funcs, width), BF16),
            jax.ShapeDtypeStruct(ones.shape, BF16),
        ],
        scratch_shapes=[pltpu.VMEM((funcs, width), F32)],
        compiler_params=PARAMS,
        name="project",
    )(ones, branch_second, branch_third, third, there(combos), there(forcing))


def backward_call(
    squash, points_all, inner, cots, feats, coords, weights, first, second, pieces, scale
):
    points, width = squash.shape
    funcs = feats.shape[0]
    tile, deep = tiles(points)
    return pl.pallas_call(
        functools.partial(backward_kernel, scale),
        grid=(points // tile,),
        in_specs=[
            pl.BlockSpec((tile, width), lambda i: (i, 0)),
            deep(4, width),
            deep(7, width),
            pl.BlockSpec((5, funcs, tile), lambda i: (0, 0, i)),
            whole(funcs, width),
            pl.BlockSpec((2, tile), lambda i: (0, i)),
            whole(8, width, width),
            whole(2, width),
            whole(width, width),
        ],
        out_specs=whole(*pieces),
        out_shape=jax.ShapeDtypeStruct(pieces, F32),
        scratch_shapes=[
            pltpu.VMEM((5, tile, width), F32),
            pltpu.VMEM((8, tile, width), BF16),
            pltpu.VMEM((4, tile, width), F32),
            pltpu.VMEM((tile, width), BF16),
            pltpu.VMEM((8, width, width), F32),
            pltpu.VMEM((16, width), F32),
        ],
        compiler_params=PARAMS,
        cost_estimate=pl.CostEstimate(
            flops=42 * points * width * width, bytes_accessed=48 * points * width, transcendentals=0
        ),
        name="trunk_backward",
    )(
        there(squash),
        there(points_all),
        there(inner),
        there(cots),
        there(feats),
        coords,
        there(weights),
        first,
        second,
    )


def branch_call(core, mine, other, third, branch_third, branch_second, fields, scale):
    count, width = 2 * mine.shape[0] * mine.shape[1], third.shape[0]
    rows = fields * (width // LANES) + mine.shape[1]
    return pl.pallas_call(
        functools.partial(branch_kernel, scale),
        in_specs=[SCALAR] + [LOCAL] * 5,
        out_shape=[jax.ShapeDtypeStruct((count, width), BF16)] * 6
        + [jax.ShapeDtypeStruct((rows, LANES), BF16), jax.ShapeDtypeStruct((2, width), F32)],
        scratch_shapes=[pltpu.VMEM((count, fields), BF16)],
        compiler_params=SMALL,
        name="branch_backward",
    )(core, mine, other, third, branch_third, branch_second)


def gradient_call(u, features, two, feature_back, one, back_two, scale):
    shape = (u.shape[1], features.shape[1])
    return pl.pallas_call(
        functools.partial(gradient_kernel, scale),
        in_specs=[LOCAL] * 6,
        out_shape=[jax.ShapeDtypeStruct(shape, F32)] * 3,
        compiler_params=SMALL,
        name="branch_gradients",
    )(u, features, two, feature_back, one, back_two)


def spread_call(core, mine, other, shape, width):
    steps = 4
    block = (mine.shape[0] // steps, *mine.shape[1:])
    piece = pl.BlockSpec(block, lambda j: (j, 0, 0))
    return pl.pallas_call(
        spread_kernel,
        grid=(steps,),
        in_specs=[SCALAR, piece, piece],
        out_specs=[
            pl.BlockSpec((shape[0] // steps, shape[1]), lambda j: (j, 0)),
            whole(width, width),
        ],
        out_shape=[jax.ShapeDtypeStruct(shape, F32), jax.ShapeDtypeStruct((width, width), F32)],
        compiler_params=PARAMS,
        name="spread",
    )(core, mine, other)


def swap(parts, axes):
    return lax.all_to_all(parts, axes, split_axis=0, concat_axis=0, tiled=True)


def across_chip(value):
    return lax.ppermute(value, "core", [(0, 1), (1, 0)])


def per_device(
    sensors,
    forcing,
    coords,
    branch_first,
    branch_second,
    branch_third,
    trunk_first,
    trunk_second,
    trunk_third,
):
    pairs, pts_size = lax.axis_size("pairs"), lax.axis_size("pts")
    func_size = 2 * pairs
    chips = pairs * pts_size
    core = lax.axis_index("core").reshape(1)
    funcs = forcing.shape[0]
    weight = 1.0 / math.sqrt(funcs * func_size * forcing.shape[1] * pts_size)
    width_out = trunk_third.shape[1]
    width = trunk_second.shape[0]
    scale = width_out ** (-0.5)
    own = sensors.shape[0]
    fields = sensors.shape[1] // chips

    own_one = jnp.tanh(dot(sensors, branch_first)).astype(BF16)
    ones = swap(jnp.broadcast_to(own_one[None], (pts_size, own, width)), "pts")
    blocks = sensors.reshape(own, chips, fields).transpose(1, 0, 2)
    points_all, squash, inner, combos, weights = forward_call(coords, trunk_first, trunk_second)
    cots, feats, shares = project_call(
        ones,
        branch_second,
        branch_third,
        trunk_third,
        combos,
        forcing,
        weight,
        scale,
    )
    u_own = swap(shares, "pts").astype(F32).sum(0).astype(BF16)
    second_pieces = backward_call(
        squash,
        points_all,
        inner,
        cots,
        feats,
        coords,
        weights,
        trunk_first,
        trunk_second,
        (chips, own, LANES + 2 * width // own),
        scale,
    )
    told = lambda part: jnp.broadcast_to(part[None], (chips, *part.shape))
    pieces = jnp.concatenate(
        [
            told(u_own),
            second_pieces.astype(BF16),
            blocks,
            told(own_one),
        ],
        axis=2,
    )
    every = swap(pieces, ("pairs", "pts"))
    every_other = across_chip(every)
    u, features, two, feature_back, one, back_two, rows, grad_t1 = branch_call(
        core, every, every_other, trunk_third, branch_third, branch_second, fields // 2, scale
    )
    mine = swap(told(rows), ("pairs", "pts"))
    other = across_chip(mine)
    grad_t3, grad_b3, grad_b2 = gradient_call(
        u, features, two, feature_back, one, back_two, scale
    )
    grad_b1, grad_t2 = spread_call(core, mine, other, branch_first.shape, width)
    return (grad_b1, grad_b2, grad_b3, grad_t1, grad_t2, grad_t3)


def solution(mesh):
    func_size, pts_size = mesh.devices.shape
    cores = jax.sharding.Mesh(mesh.devices.reshape(func_size // 2, 2, pts_size), AXES)
    return jax.shard_map(
        per_device,
        mesh=cores,
        in_specs=(
            P(AXES, None),
            P(("pairs", "core"), "pts"),
            P(None, "pts"),
            P(),
            P(),
            P(),
            P(),
            P(),
            P(),
        ),
        out_specs=(P(), P(), P(), P(), P(), P()),
        check_vma=False,
    )
```

```python
import functools
import math

import jax
import jax.numpy as jnp
from jax import lax
from jax.experimental import pallas as pl
from jax.experimental.pallas import tpu as pltpu
from jax.sharding import PartitionSpec as P

DRAG = 0.5
TILE = 512
PROJECT = 1024
ROWS = 16
PARTS = 2
CHUNK = 256
LANES = 128
F32 = jnp.float32
BF16 = jnp.bfloat16
AXES = ("pairs", "core", "pts")
GROUP = (0, 1, 1, 2, 2, 2, 3, 3)
NT = (((1,), (1,)), ((), ()))
TN = (((0,), (0,)), ((), ()))
PARAMS = pltpu.CompilerParams(
    dimension_semantics=("arbitrary",), vmem_limit_bytes=40 * 1024 * 1024
)
SMALL = pltpu.CompilerParams(vmem_limit_bytes=24 * 1024 * 1024)


def dot(left, right, dims=(((1,), (0,)), ((), ()))):
    return lax.dot_general(left, right, dims, preferred_element_type=F32)


def slopes(squash):
    square = squash * squash
    one = 1.0 - square
    two = -2.0 * (squash * one)
    three = one * (6.0 * square - 2.0)
    return square, one, two, three


def chunks(rows, width, body):
    for start in range(*rows, ROWS):
        for lane in range(0, width, LANES):
            body(pl.ds(start, ROWS), pl.ds(lane, LANES))


def constants(first):
    a, b = first[0:1], first[1:2]
    one, zero = jnp.ones_like(a), jnp.zeros_like(a)
    square = a * a + b * b
    consts = [one, a, b, -square, b * b - a * a, -2.0 * a * b, -a * square, -b * square]
    by_a = [zero, one, zero, -2.0 * a, -2.0 * a, -2.0 * b, -(3.0 * a * a + b * b), -2.0 * a * b]
    by_b = [zero, zero, one, -2.0 * b, 2.0 * b, -2.0 * a, -2.0 * a * b, -(a * a + 3.0 * b * b)]
    return jnp.concatenate(consts + by_a + by_b, axis=0).T


def thirds(value):
    parts = []
    for _ in range(3):
        part = value.astype(BF16).astype(F32)
        parts.append(part)
        value = value - part
    return parts


def forward_kernel(
    coords_ref,
    first_ref,
    second_ref,
    points_ref,
    squash_ref,
    inner_ref,
    combos_ref,
    weights_ref,
    values_ref,
    wide_ref,
):
    @pl.when(pl.program_id(0) == 0)
    def _():
        consts = constants(first_ref[...])
        second = second_ref[...].astype(F32)
        for part in range(8):
            weights_ref[part] = (consts[:, part : part + 1] * second).astype(BF16)

    left, right = thirds(coords_ref[...]), thirds(first_ref[...])
    pairs = ((0, 0), (0, 1), (1, 0), (0, 2), (2, 0), (1, 1))
    left = [left[i] for i, _ in pairs] + [jnp.zeros_like(left[0])] * 2
    right = [right[j] for _, j in pairs] + [jnp.zeros_like(right[0])] * 2
    values_ref[...] = dot(
        jnp.concatenate(left, axis=0).astype(BF16), jnp.concatenate(right, axis=0).astype(BF16), TN
    )

    def layer_one(rows, lanes):
        squash = jnp.tanh(values_ref[rows, lanes])
        _, one, two, three = slopes(squash)
        for group, part in enumerate((squash, one, two, three)):
            points_ref[group, rows, lanes] = part.astype(BF16)


    def layer_two(rows, lanes):
        z, zx, zy, lap, dif, mix, px, py = (wide_ref[part, rows, lanes] for part in range(8))
        squash = jnp.tanh(z)
        squash_ref[rows, lanes] = squash
        for part, value in enumerate((zx, zy, lap, dif, mix, px, py)):
            inner_ref[part, rows, lanes] = value.astype(BF16)
        _, one, two, three = slopes(squash)
        radius = zx * zx + zy * zy
        twice = lap + lap
        bend = three * radius
        along = zx * (twice + dif) + zy * mix
        across = zy * (twice - dif) + zx * mix
        combos = (
            one * zx,
            one * zy,
            one * lap - two * radius,
            one * px + two * along - bend * zx,
            one * py + two * across - bend * zy,
        )
        for k, combo in enumerate(combos):
            combos_ref[k, rows, lanes] = combo.astype(BF16)

    tile, width = values_ref.shape
    part_rows = tile // max(1, min(PARTS, tile // LANES))
    for start in range(0, tile, part_rows):
        rows = (start, start + part_rows)
        chunks(rows, width, layer_one)
        span = pl.ds(start, part_rows)
        for part, group in enumerate(GROUP):
            wide_ref[part, span] = dot(points_ref[group, span], weights_ref[part])
    for start in range(0, tile, part_rows):
        chunks((start, start + part_rows), width, layer_two)


def project_kernel(
    weight,
    scale,
    ones_ref,
    branch_second_ref,
    branch_third_ref,
    third_ref,
    combos_ref,
    forcing_ref,
    cots_ref,
    feats_ref,
    shares_ref,
    u_ref,
):
    @pl.when(pl.program_id(0) == 0)
    def _():
        u_ref[...] = jnp.zeros_like(u_ref)
        one = ones_ref[...].astype(F32).reshape(u_ref.shape).astype(BF16)
        two = jnp.tanh(dot(one, branch_second_ref[...])).astype(BF16)
        features = dot(two, branch_third_ref[...]).astype(BF16)
        feats_ref[...] = (dot(features, third_ref[...], NT) * scale).astype(BF16)

    feats = feats_ref[...]
    tile = forcing_ref.shape[1]
    for start in range(0, tile, min(CHUNK, tile)):
        span = pl.ds(start, min(CHUNK, tile))
        px, py, om, omx, omy = (dot(feats, combos_ref[k, span], NT) for k in range(5))
        residual = py * omx - px * omy + DRAG * om - forcing_ref[:, span].astype(F32)
        slope = residual * weight
        parts = (-slope * omy, slope * omx, DRAG * slope, slope * py, -slope * px)
        for k, part in enumerate(parts):
            cots_ref[k, :, span] = part.astype(BF16)
    total = u_ref[...]
    for k in range(5):
        total += dot(cots_ref[k], combos_ref[k])
    u_ref[...] = total

    @pl.when(pl.program_id(0) == pl.num_programs(0) - 1)
    def _():
        shares_ref[...] = u_ref[...].reshape(shares_ref.shape).astype(BF16)


def backward_kernel(
    squash_ref,
    points_ref,
    inner_ref,
    cots_ref,
    feats_ref,
    coords_ref,
    weights_ref,
    first_ref,
    second_ref,
    pieces_ref,
    back_ref,
    inner_back_ref,
    ones_ref,
    one_back_ref,
    grads_ref,
    value_ref,
):
    step = pl.program_id(0)
    last = pl.num_programs(0) - 1
    width = second_ref.shape[0]

    @pl.when(step == 0)
    def _():
        grads_ref[...] = jnp.zeros_like(grads_ref)
        value_ref[...] = jnp.zeros_like(value_ref)

    feats = feats_ref[...]

    def layer_two_back(rows, lanes):
        squash = squash_ref[rows, lanes]
        zx, zy, lap, dif, mix, px, py = (
            inner_ref[part, rows, lanes].astype(F32) for part in range(7)
        )
        gx, gy, gl, gp, gq = (back_ref[k, rows, lanes] for k in range(5))
        square, one, two, three = slopes(squash)
        four = two * (12.0 * square - 8.0)
        radius = zx * zx + zy * zy
        twice = lap + lap
        plus, minus = twice + dif, twice - dif
        along = zx * plus + zy * mix
        across = zy * minus + zx * mix
        pull = gp * zx + gq * zy
        one_bar = gx * zx + gy * zy + gl * lap + gp * px + gq * py
        two_bar = gp * along + gq * across - gl * radius
        three_bar = pull * radius
        along_bar, across_bar = two * gp, two * gq
        turn = -2.0 * (two * gl + three * pull)
        bend = three * radius
        xa, yc = zx * along_bar, zy * across_bar
        parts = (
            two * one_bar + three * two_bar - four * three_bar,
            one * gx - bend * gp + zx * turn + along_bar * plus + across_bar * mix,
            one * gy - bend * gq + zy * turn + across_bar * minus + along_bar * mix,
            one * gl + 2.0 * (xa + yc),
            xa - yc,
            zy * along_bar + zx * across_bar,
            one * gp,
            one * gq,
        )
        for part, value in enumerate(parts):
            inner_back_ref[part, rows, lanes] = value.astype(BF16)

    def layer_one_back(rows, lanes):
        squash, one, two, three = (points_ref[part, rows, lanes].astype(F32) for part in range(4))
        four = two * (4.0 - 12.0 * one)
        back = (
            one * ones_ref[0, rows, lanes]
            + two * ones_ref[1, rows, lanes]
            + three * ones_ref[2, rows, lanes]
            + four * ones_ref[3, rows, lanes]
        )
        one_back_ref[rows, lanes] = back.astype(BF16)

    tile = squash_ref.shape[0]
    part_rows = tile // max(1, min(PARTS, tile // LANES))
    spans = [(start, start + part_rows) for start in range(0, tile, part_rows)]
    for start, stop in spans:
        for k in range(5):
            back_ref[k, start:stop] = dot(cots_ref[k, :, start:stop], feats, TN)
    for start, stop in spans:
        chunks((start, stop), width, layer_two_back)
        for group in range(4):
            total = None
            for part in range(8):
                if GROUP[part] == group:
                    term = dot(inner_back_ref[part, start:stop], weights_ref[part], NT)
                    total = term if total is None else total + term
            ones_ref[group, start:stop] = total
    for part, group in enumerate(GROUP):
        grads_ref[part] += dot(points_ref[group], inner_back_ref[part], TN)
    for start, stop in spans:
        chunks((start, stop), width, layer_one_back)
    coords = jnp.concatenate(thirds(coords_ref[...]) + [jnp.zeros_like(coords_ref)] * 5, axis=0)
    value_ref[...] += dot(coords.astype(BF16), one_back_ref[...])

    @pl.when(step == last)
    def _():
        second = second_ref[...].astype(F32)
        consts = constants(first_ref[...])
        g = [grads_ref[part] for part in range(8)]
        column = lambda part: consts[:, part : part + 1]
        total = g[0]
        for part in range(1, 8):
            total += column(part) * g[part]
        both, less = g[3] + g[4], g[3] - g[4]
        by_a = g[1] + column(11) * both + column(13) * g[5] + column(14) * g[6] + column(15) * g[7]
        by_b = g[2] + column(19) * less + column(21) * g[5] + column(22) * g[6] + column(23) * g[7]
        first = [jnp.sum(second * by, axis=1, keepdims=True) for by in (by_a, by_b)]
        lane = lax.broadcasted_iota(jnp.int32, (width, LANES), 1)
        both = jnp.where(lane == 0, first[0], 0.0) + jnp.where(lane == 1, first[1], 0.0)
        first_grad = value_ref[0:2] + value_ref[2:4] + value_ref[4:6] + both.T[0:2]
        count, own, _ = pieces_ref.shape
        strips = width // LANES
        part = count // strips
        for strip in range(strips):
            block = total[:, strip * LANES : (strip + 1) * LANES]
            pieces_ref[strip * part : (strip + 1) * part, :, 0:LANES] = block.reshape(
                part, own, LANES
            )
        across = 2 * width // own
        rows = [
            first_grad[axis : axis + 1, lane : lane + across]
            for axis in range(2)
            for lane in range(0, width, across)
        ]
        told = jnp.concatenate(rows, axis=0)
        pieces_ref[:, :, LANES:] = jnp.broadcast_to(told[None], (count, *told.shape))


def branch_kernel(
    scale,
    core_ref,
    mine_ref,
    other_ref,
    third_ref,
    branch_third_ref,
    branch_second_ref,
    u_ref,
    features_ref,
    two_ref,
    feature_back_ref,
    one_ref,
    back_two_ref,
    rows_ref,
    first_ref,
    columns_ref,
):
    core = core_ref[0]
    width = third_ref.shape[0]
    half, fields = u_ref.shape[0] // 2, columns_ref.shape[1]
    across = 2 * width // mine_ref.shape[1]
    here = width + LANES + across
    total = None
    for place, from_ref in ((core, mine_ref), (1 - core, other_ref)):
        rows = pl.ds(pl.multiple_of(place * half, half), half)
        got = from_ref[...].astype(F32)
        part = jnp.sum(got[:, :, width : width + 2 * LANES], axis=0)
        total = part if total is None else total + part
        got = got.reshape(half, -1)
        u_ref[rows, :] = got[:, 0:width].astype(BF16)
        one_ref[rows, :] = got[:, width + 2 * LANES :].astype(BF16)
        columns_ref[rows, :] = jnp.where(
            core == 0,
            got[:, here : here + fields],
            got[:, here + fields : here + 2 * fields],
        ).astype(BF16)
    wide = jnp.tanh(dot(one_ref[...], branch_second_ref[...]))
    two_ref[...] = wide.astype(BF16)
    features_ref[...] = dot(two_ref[...], branch_third_ref[...]).astype(BF16)
    feature_back = (dot(u_ref[...], third_ref[...]) * scale).astype(BF16)
    feature_back_ref[...] = feature_back
    back_two = (dot(feature_back, branch_third_ref[...], NT) * (1.0 - wide * wide)).astype(BF16)
    back_two_ref[...] = back_two
    one = one_ref[...].astype(F32)
    back_one = (dot(back_two, branch_second_ref[...], NT) * (1.0 - one * one)).astype(BF16)
    rows = dot(columns_ref[...], back_one, TN)
    parts = [rows[:, lane : lane + LANES] for lane in range(0, width, LANES)]
    rows_ref[...] = jnp.concatenate(parts + [total[:, 0:LANES]], axis=0).astype(BF16)
    deep = width // across
    for axis in range(2):
        for strip in range(deep):
            first_ref[axis : axis + 1, strip * across : (strip + 1) * across] = total[
                axis * deep + strip : axis * deep + strip + 1, LANES : LANES + across
            ]


def gradient_kernel(
    scale,
    u_ref,
    features_ref,
    two_ref,
    feature_back_ref,
    one_ref,
    back_two_ref,
    trunk_ref,
    third_ref,
    second_ref,
):
    trunk_ref[...] = dot(u_ref[...], features_ref[...], TN) * scale
    third_ref[...] = dot(two_ref[...], feature_back_ref[...], TN)
    second_ref[...] = dot(one_ref[...], back_two_ref[...], TN)


def spread_rows(from_ref, grad_ref):
    got = from_ref[...].astype(F32)
    fields = grad_ref.shape[2]
    for lane in range(grad_ref.shape[3] // LANES):
        grad_ref[:, 0, :, lane * LANES : (lane + 1) * LANES] = got[
            :, lane * fields : (lane + 1) * fields
        ]
    return got


def mine_kernel(core_ref, mine_ref, grad_ref, second_ref):
    step = pl.program_id(0)
    tail = spread_rows(mine_ref, grad_ref)[:, -8:].reshape(-1, LANES)
    width = second_ref.shape[0]
    for now in range(width * width // tail.size):

        @pl.when(step == now)
        def _():
            strip, row = divmod(now * tail.shape[0], width)
            second_ref[row : row + tail.shape[0], strip * LANES : (strip + 1) * LANES] = tail


def other_kernel(core_ref, other_ref, kept_ref, grad_ref):
    spread_rows(other_ref, grad_ref)


def whole(*shape):
    return pl.BlockSpec(shape, lambda i: (0,) * len(shape))


def there(value):
    return pltpu.with_memory_space_constraint(value, pltpu.HBM)


SCALAR = pl.BlockSpec(memory_space=pltpu.SMEM)
LOCAL = pl.BlockSpec(memory_space=pltpu.VMEM)


def tiles(points):
    tile = min(TILE, points)
    deep = lambda n, width: pl.BlockSpec((n, tile, width), lambda i: (0, i, 0))
    return tile, deep


def forward_call(coords, first, second):
    points, width = coords.shape[1], first.shape[1]
    tile, deep = tiles(points)
    flat = pl.BlockSpec((tile, width), lambda i: (i, 0))
    return pl.pallas_call(
        forward_kernel,
        grid=(points // tile,),
        in_specs=[
            pl.BlockSpec((2, tile), lambda i: (0, i)),
            whole(2, width),
            whole(width, width),
        ],
        out_specs=[deep(4, width), flat, deep(7, width), deep(5, width), whole(8, width, width)],
        out_shape=[
            pltpu.HBM((4, points, width), BF16),
            pltpu.HBM((points, width), F32),
            pltpu.HBM((7, points, width), BF16),
            pltpu.HBM((5, points, width), BF16),
            pltpu.HBM((8, width, width), BF16),
        ],
        scratch_shapes=[pltpu.VMEM((tile, width), F32), pltpu.VMEM((8, tile, width), F32)],
        compiler_params=PARAMS,
        name="trunk_forward",
    )(coords, first, second)


def project_call(ones, branch_second, branch_third, third, combos, forcing, weight, scale):
    funcs, points = forcing.shape
    width = third.shape[0]
    tile = min(PROJECT, points)
    return pl.pallas_call(
        functools.partial(project_kernel, weight, scale),
        grid=(points // tile,),
        in_specs=[
            whole(*ones.shape),
            whole(width, width),
            whole(width, width),
            whole(width, width),
            pl.BlockSpec((5, tile, width), lambda i: (0, i, 0)),
            pl.BlockSpec((funcs, tile), lambda i: (0, i)),
        ],
        out_specs=[
            pl.BlockSpec((5, funcs, tile), lambda i: (0, 0, i)),
            whole(funcs, width),
            whole(*ones.shape),
        ],
        out_shape=[
            pltpu.HBM((5, funcs, points), BF16),
            pltpu.HBM((funcs, width), BF16),
            jax.ShapeDtypeStruct(ones.shape, BF16),
        ],
        scratch_shapes=[pltpu.VMEM((funcs, width), F32)],
        compiler_params=PARAMS,
        name="project",
    )(ones, branch_second, branch_third, third, there(combos), there(forcing))


def backward_call(
    squash, points_all, inner, cots, feats, coords, weights, first, second, pieces
):
    points, width = squash.shape
    funcs = feats.shape[0]
    tile, deep = tiles(points)
    return pl.pallas_call(
        backward_kernel,
        grid=(points // tile,),
        in_specs=[
            pl.BlockSpec((tile, width), lambda i: (i, 0)),
            deep(4, width),
            deep(7, width),
            pl.BlockSpec((5, funcs, tile), lambda i: (0, 0, i)),
            whole(funcs, width),
            pl.BlockSpec((2, tile), lambda i: (0, i)),
            whole(8, width, width),
            whole(2, width),
            whole(width, width),
        ],
        out_specs=whole(*pieces),
        out_shape=jax.ShapeDtypeStruct(pieces, F32),
        scratch_shapes=[
            pltpu.VMEM((5, tile, width), F32),
            pltpu.VMEM((8, tile, width), BF16),
            pltpu.VMEM((4, tile, width), F32),
            pltpu.VMEM((tile, width), BF16),
            pltpu.VMEM((8, width, width), F32),
            pltpu.VMEM((16, width), F32),
        ],
        compiler_params=PARAMS,
        cost_estimate=pl.CostEstimate(
            flops=42 * points * width * width, bytes_accessed=48 * points * width, transcendentals=0
        ),
        name="trunk_backward",
    )(
        there(squash),
        there(points_all),
        there(inner),
        there(cots),
        there(feats),
        coords,
        there(weights),
        first,
        second,
    )


def branch_call(core, mine, other, third, branch_third, branch_second, fields, scale):
    count, width = 2 * mine.shape[0] * mine.shape[1], third.shape[0]
    rows = fields * (width // LANES) + mine.shape[1]
    return pl.pallas_call(
        functools.partial(branch_kernel, scale),
        in_specs=[SCALAR] + [LOCAL] * 5,
        out_shape=[jax.ShapeDtypeStruct((count, width), BF16)] * 6
        + [jax.ShapeDtypeStruct((rows, LANES), BF16), jax.ShapeDtypeStruct((2, width), F32)],
        scratch_shapes=[pltpu.VMEM((count, fields), BF16)],
        compiler_params=SMALL,
        name="branch_backward",
    )(core, mine, other, third, branch_third, branch_second)


def gradient_call(u, features, two, feature_back, one, back_two, scale):
    shape = (u.shape[1], features.shape[1])
    return pl.pallas_call(
        functools.partial(gradient_kernel, scale),
        in_specs=[LOCAL] * 6,
        out_shape=[jax.ShapeDtypeStruct(shape, F32)] * 3,
        compiler_params=SMALL,
        name="branch_gradients",
    )(u, features, two, feature_back, one, back_two)


def spread_specs(got, shape, side):
    steps = 4
    part = got.shape[0] // steps
    fields = shape[0] // (2 * got.shape[0])
    return (
        steps,
        pl.BlockSpec((part, *got.shape[1:]), lambda j, c: (j, 0, 0)),
        pl.BlockSpec((part, 1, fields, shape[1]), lambda j, c: (j, side(c[0]), 0, 0)),
        jax.ShapeDtypeStruct((got.shape[0], 2, fields, shape[1]), F32),
    )


def mine_call(core, mine, shape, width):
    steps, piece, place, out = spread_specs(mine, shape, lambda c: c)
    return pl.pallas_call(
        mine_kernel,
        grid_spec=pltpu.PrefetchScalarGridSpec(
            num_scalar_prefetch=1,
            grid=(steps,),
            in_specs=[piece],
            out_specs=[place, pl.BlockSpec((width, width), lambda j, c: (0, 0))],
        ),
        out_shape=[out, jax.ShapeDtypeStruct((width, width), F32)],
        compiler_params=PARAMS,
        name="spread_mine",
    )(core, mine)


def other_call(core, other, kept, shape):
    steps, piece, place, out = spread_specs(other, shape, lambda c: 1 - c)
    return pl.pallas_call(
        other_kernel,
        grid_spec=pltpu.PrefetchScalarGridSpec(
            num_scalar_prefetch=1,
            grid=(steps,),
            in_specs=[piece, pl.BlockSpec(memory_space=pl.ANY)],
            out_specs=place,
        ),
        out_shape=out,
        input_output_aliases={2: 0},
        compiler_params=PARAMS,
        name="spread_other",
    )(core, other, kept)


def swap(parts, axes):
    return lax.all_to_all(parts, axes, split_axis=0, concat_axis=0, tiled=True)


def across_chip(value):
    return lax.ppermute(value, "core", [(0, 1), (1, 0)])


def per_device(
    sensors,
    forcing,
    coords,
    branch_first,
    branch_second,
    branch_third,
    trunk_first,
    trunk_second,
    trunk_third,
):
    pairs, pts_size = lax.axis_size("pairs"), lax.axis_size("pts")
    func_size = 2 * pairs
    chips = pairs * pts_size
    core = lax.axis_index("core").reshape(1)
    funcs = forcing.shape[0]
    weight = 1.0 / math.sqrt(funcs * func_size * forcing.shape[1] * pts_size)
    width_out = trunk_third.shape[1]
    width = trunk_second.shape[0]
    scale = width_out ** (-0.5)
    own = sensors.shape[0]
    fields = sensors.shape[1] // chips

    own_one = jnp.tanh(dot(sensors, branch_first)).astype(BF16)
    ones = swap(jnp.broadcast_to(own_one[None], (pts_size, own, width)), "pts")
    blocks = sensors.reshape(own, chips, fields).transpose(1, 0, 2)
    points_all, squash, inner, combos, weights = forward_call(coords, trunk_first, trunk_second)
    cots, feats, shares = project_call(
        ones,
        branch_second,
        branch_third,
        trunk_third,
        combos,
        forcing,
        weight,
        scale,
    )
    u_own = swap(shares, "pts").astype(F32).sum(0).astype(BF16)
    second_pieces = backward_call(
        squash,
        points_all,
        inner,
        cots,
        feats,
        coords,
        weights,
        trunk_first,
        trunk_second,
        (chips, own, LANES + 2 * width // own),
    )
    told = lambda part: jnp.broadcast_to(part[None], (chips, *part.shape))
    pieces = jnp.concatenate(
        [
            told(u_own),
            second_pieces.astype(BF16),
            blocks,
            told(own_one),
        ],
        axis=2,
    )
    every = swap(pieces, ("pairs", "pts"))
    every_other = across_chip(every)
    u, features, two, feature_back, one, back_two, rows, grad_t1 = branch_call(
        core, every, every_other, trunk_third, branch_third, branch_second, fields // 2, scale
    )
    mine = swap(told(rows), ("pairs", "pts"))
    other = across_chip(mine)
    grad_t3, grad_b3, grad_b2 = gradient_call(
        u, features, two, feature_back, one, back_two, scale
    )
    kept, grad_t2 = mine_call(core, mine, branch_first.shape, width)
    grad_b1 = other_call(core, other, kept, branch_first.shape).reshape(branch_first.shape)
    return (grad_b1, grad_b2, grad_b3, grad_t1, grad_t2, grad_t3)


def solution(mesh):
    func_size, pts_size = mesh.devices.shape
    cores = jax.sharding.Mesh(mesh.devices.reshape(func_size // 2, 2, pts_size), AXES)
    return jax.shard_map(
        per_device,
        mesh=cores,
        in_specs=(
            P(AXES, None),
            P(("pairs", "core"), "pts"),
            P(None, "pts"),
            P(),
            P(),
            P(),
            P(),
            P(),
            P(),
        ),
        out_specs=(P(), P(), P(), P(), P(), P()),
        check_vma=False,
    )
```

```python
import functools
import math

import jax
import jax.numpy as jnp
from jax import lax
from jax.experimental import pallas as pl
from jax.experimental.pallas import tpu as pltpu
from jax.sharding import PartitionSpec as P

DRAG = 0.5
TILE = 512
PROJECT = 1024
ROWS = 16
PARTS = 2
CHUNK = 256
STEPS = 2
LANES = 128
F32 = jnp.float32
BF16 = jnp.bfloat16
AXES = ("pairs", "core", "pts")
GROUP = (0, 1, 1, 2, 2, 2, 3, 3)
NT = (((1,), (1,)), ((), ()))
TN = (((0,), (0,)), ((), ()))
PARAMS = pltpu.CompilerParams(
    dimension_semantics=("arbitrary",), vmem_limit_bytes=40 * 1024 * 1024
)
SMALL = pltpu.CompilerParams(vmem_limit_bytes=24 * 1024 * 1024)


def dot(left, right, dims=(((1,), (0,)), ((), ()))):
    return lax.dot_general(left, right, dims, preferred_element_type=F32)


def slopes(squash):
    square = squash * squash
    one = 1.0 - square
    two = -2.0 * (squash * one)
    three = one * (6.0 * square - 2.0)
    return square, one, two, three


def chunks(rows, width, body):
    for start in range(*rows, ROWS):
        body(pl.ds(start, ROWS), pl.ds(0, width))


def constants(first):
    a, b = first[0:1], first[1:2]
    one, zero = jnp.ones_like(a), jnp.zeros_like(a)
    square = a * a + b * b
    consts = [one, a, b, -square, b * b - a * a, -2.0 * a * b, -a * square, -b * square]
    by_a = [zero, one, zero, -2.0 * a, -2.0 * a, -2.0 * b, -(3.0 * a * a + b * b), -2.0 * a * b]
    by_b = [zero, zero, one, -2.0 * b, 2.0 * b, -2.0 * a, -2.0 * a * b, -(a * a + 3.0 * b * b)]
    return jnp.concatenate(consts + by_a + by_b, axis=0).T


def thirds(value):
    parts = []
    for _ in range(3):
        part = value.astype(BF16).astype(F32)
        parts.append(part)
        value = value - part
    return parts


def first_kernel(sensors_ref, first_ref, own_ref, told_ref, total_ref):
    step = pl.program_id(0)

    @pl.when(step == 0)
    def _():
        total_ref[...] = jnp.zeros_like(total_ref)

    total_ref[...] += dot(sensors_ref[...], first_ref[...])

    @pl.when(step == pl.num_programs(0) - 1)
    def _():
        one = jnp.tanh(total_ref[...])
        own_ref[...] = one.astype(BF16)
        told_ref[...] = jnp.broadcast_to(one[None], told_ref.shape).astype(BF16)


def forward_kernel(
    coords_ref,
    first_ref,
    second_ref,
    points_ref,
    squash_ref,
    inner_ref,
    combos_ref,
    weights_ref,
    values_ref,
    wide_ref,
):
    @pl.when(pl.program_id(0) == 0)
    def _():
        consts = constants(first_ref[...])
        second = second_ref[...].astype(F32)
        for part in range(8):
            weights_ref[part] = (consts[:, part : part + 1] * second).astype(BF16)

    left, right = thirds(coords_ref[...]), thirds(first_ref[...])
    pairs = ((0, 0), (0, 1), (1, 0), (0, 2), (2, 0), (1, 1))
    left = [left[i] for i, _ in pairs] + [jnp.zeros_like(left[0])] * 2
    right = [right[j] for _, j in pairs] + [jnp.zeros_like(right[0])] * 2
    values_ref[...] = dot(
        jnp.concatenate(left, axis=0).astype(BF16), jnp.concatenate(right, axis=0).astype(BF16), TN
    )

    def layer_one(rows, lanes):
        squash = jnp.tanh(values_ref[rows, lanes])
        _, one, two, three = slopes(squash)
        for group, part in enumerate((squash, one, two, three)):
            points_ref[group, rows, lanes] = part.astype(BF16)


    def layer_two(rows, lanes):
        z, zx, zy, lap, dif, mix, px, py = (wide_ref[part, rows, lanes] for part in range(8))
        squash = jnp.tanh(z)
        squash_ref[rows, lanes] = squash
        for part, value in enumerate((zx, zy, lap, dif, mix, px, py)):
            inner_ref[part, rows, lanes] = value.astype(BF16)
        _, one, two, three = slopes(squash)
        radius = zx * zx + zy * zy
        twice = lap + lap
        bend = three * radius
        along = zx * (twice + dif) + zy * mix
        across = zy * (twice - dif) + zx * mix
        combos = (
            one * zx,
            one * zy,
            one * lap - two * radius,
            one * px + two * along - bend * zx,
            one * py + two * across - bend * zy,
        )
        for k, combo in enumerate(combos):
            combos_ref[k, rows, lanes] = combo.astype(BF16)

    tile, width = values_ref.shape
    part_rows = tile // max(1, min(PARTS, tile // LANES))
    for start in range(0, tile, part_rows):
        rows = (start, start + part_rows)
        chunks(rows, width, layer_one)
        span = pl.ds(start, part_rows)
        for part, group in enumerate(GROUP):
            wide_ref[part, span] = dot(points_ref[group, span], weights_ref[part])
    for start in range(0, tile, part_rows):
        chunks((start, start + part_rows), width, layer_two)


def project_kernel(
    weight,
    scale,
    ones_ref,
    branch_second_ref,
    branch_third_ref,
    third_ref,
    combos_ref,
    forcing_ref,
    cots_ref,
    feats_ref,
    shares_ref,
    u_ref,
):
    @pl.when(pl.program_id(0) == 0)
    def _():
        u_ref[...] = jnp.zeros_like(u_ref)
        one = ones_ref[...].astype(F32).reshape(u_ref.shape).astype(BF16)
        two = jnp.tanh(dot(one, branch_second_ref[...])).astype(BF16)
        features = dot(two, branch_third_ref[...]).astype(BF16)
        feats_ref[...] = (dot(features, third_ref[...], NT) * scale).astype(BF16)

    feats = feats_ref[...]
    tile = forcing_ref.shape[1]
    for start in range(0, tile, min(CHUNK, tile)):
        span = pl.ds(start, min(CHUNK, tile))
        px, py, om, omx, omy = (dot(feats, combos_ref[k, span], NT) for k in range(5))
        residual = py * omx - px * omy + DRAG * om - forcing_ref[:, span].astype(F32)
        slope = residual * weight
        parts = (-slope * omy, slope * omx, DRAG * slope, slope * py, -slope * px)
        for k, part in enumerate(parts):
            cots_ref[k, :, span] = part.astype(BF16)
    total = u_ref[...]
    for k in range(5):
        total += dot(cots_ref[k], combos_ref[k])
    u_ref[...] = total

    @pl.when(pl.program_id(0) == pl.num_programs(0) - 1)
    def _():
        shares_ref[...] = u_ref[...].reshape(shares_ref.shape).astype(BF16)


def backward_kernel(
    squash_ref,
    points_ref,
    inner_ref,
    cots_ref,
    feats_ref,
    coords_ref,
    weights_ref,
    first_ref,
    second_ref,
    pieces_ref,
    back_ref,
    inner_back_ref,
    ones_ref,
    one_back_ref,
    grads_ref,
    value_ref,
):
    step = pl.program_id(0)
    last = pl.num_programs(0) - 1
    width = second_ref.shape[0]

    @pl.when(step == 0)
    def _():
        grads_ref[...] = jnp.zeros_like(grads_ref)
        value_ref[...] = jnp.zeros_like(value_ref)

    feats = feats_ref[...]

    def layer_two_back(rows, lanes):
        squash = squash_ref[rows, lanes]
        zx, zy, lap, dif, mix, px, py = (
            inner_ref[part, rows, lanes].astype(F32) for part in range(7)
        )
        gx, gy, gl, gp, gq = (back_ref[k, rows, lanes] for k in range(5))
        square, one, two, three = slopes(squash)
        four = two * (12.0 * square - 8.0)
        radius = zx * zx + zy * zy
        twice = lap + lap
        plus, minus = twice + dif, twice - dif
        along = zx * plus + zy * mix
        across = zy * minus + zx * mix
        pull = gp * zx + gq * zy
        one_bar = gx * zx + gy * zy + gl * lap + gp * px + gq * py
        two_bar = gp * along + gq * across - gl * radius
        three_bar = pull * radius
        along_bar, across_bar = two * gp, two * gq
        turn = -2.0 * (two * gl + three * pull)
        bend = three * radius
        xa, yc = zx * along_bar, zy * across_bar
        parts = (
            two * one_bar + three * two_bar - four * three_bar,
            one * gx - bend * gp + zx * turn + along_bar * plus + across_bar * mix,
            one * gy - bend * gq + zy * turn + across_bar * minus + along_bar * mix,
            one * gl + 2.0 * (xa + yc),
            xa - yc,
            zy * along_bar + zx * across_bar,
            one * gp,
            one * gq,
        )
        for part, value in enumerate(parts):
            inner_back_ref[part, rows, lanes] = value.astype(BF16)

    def layer_one_back(rows, lanes):
        squash, one, two, three = (points_ref[part, rows, lanes].astype(F32) for part in range(4))
        four = two * (4.0 - 12.0 * one)
        back = (
            one * ones_ref[0, rows, lanes]
            + two * ones_ref[1, rows, lanes]
            + three * ones_ref[2, rows, lanes]
            + four * ones_ref[3, rows, lanes]
        )
        one_back_ref[rows, lanes] = back.astype(BF16)

    tile = squash_ref.shape[0]
    part_rows = tile // max(1, min(PARTS, tile // LANES))
    spans = [(start, start + part_rows) for start in range(0, tile, part_rows)]
    for start, stop in spans:
        for k in range(5):
            back_ref[k, start:stop] = dot(cots_ref[k, :, start:stop], feats, TN)
    for start, stop in spans:
        chunks((start, stop), width, layer_two_back)
        for group in range(4):
            total = None
            for part in range(8):
                if GROUP[part] == group:
                    term = dot(inner_back_ref[part, start:stop], weights_ref[part], NT)
                    total = term if total is None else total + term
            ones_ref[group, start:stop] = total
    for part, group in enumerate(GROUP):
        grads_ref[part] += dot(points_ref[group], inner_back_ref[part], TN)
    for start, stop in spans:
        chunks((start, stop), width, layer_one_back)
    coords = jnp.concatenate(thirds(coords_ref[...]) + [jnp.zeros_like(coords_ref)] * 5, axis=0)
    value_ref[...] += dot(coords.astype(BF16), one_back_ref[...])

    @pl.when(step == last)
    def _():
        second = second_ref[...].astype(F32)
        consts = constants(first_ref[...])
        g = [grads_ref[part] for part in range(8)]
        column = lambda part: consts[:, part : part + 1]
        total = g[0]
        for part in range(1, 8):
            total += column(part) * g[part]
        both, less = g[3] + g[4], g[3] - g[4]
        by_a = g[1] + column(11) * both + column(13) * g[5] + column(14) * g[6] + column(15) * g[7]
        by_b = g[2] + column(19) * less + column(21) * g[5] + column(22) * g[6] + column(23) * g[7]
        first = [jnp.sum(second * by, axis=1, keepdims=True) for by in (by_a, by_b)]
        lane = lax.broadcasted_iota(jnp.int32, (width, LANES), 1)
        both = jnp.where(lane == 0, first[0], 0.0) + jnp.where(lane == 1, first[1], 0.0)
        first_grad = value_ref[0:2] + value_ref[2:4] + value_ref[4:6] + both.T[0:2]
        count, own, _ = pieces_ref.shape
        strips = width // LANES
        part = count // strips
        for strip in range(strips):
            block = total[:, strip * LANES : (strip + 1) * LANES]
            pieces_ref[strip * part : (strip + 1) * part, :, 0:LANES] = block.reshape(
                part, own, LANES
            )
        across = 2 * width // own
        rows = [
            first_grad[axis : axis + 1, lane : lane + across]
            for axis in range(2)
            for lane in range(0, width, across)
        ]
        told = jnp.concatenate(rows, axis=0)
        pieces_ref[:, :, LANES:] = jnp.broadcast_to(told[None], (count, *told.shape))


def branch_kernel(
    scale,
    core_ref,
    mine_ref,
    other_ref,
    third_ref,
    branch_third_ref,
    branch_second_ref,
    u_ref,
    features_ref,
    two_ref,
    feature_back_ref,
    one_ref,
    back_two_ref,
    rows_ref,
    first_ref,
    columns_ref,
):
    core = core_ref[0]
    width = third_ref.shape[0]
    half, fields = u_ref.shape[0] // 2, columns_ref.shape[1]
    across = 2 * width // mine_ref.shape[1]
    here = width + LANES + across
    total = None
    for place, from_ref in ((core, mine_ref), (1 - core, other_ref)):
        rows = pl.ds(pl.multiple_of(place * half, half), half)
        got = from_ref[...].astype(F32)
        part = jnp.sum(got[:, :, width : width + 2 * LANES], axis=0)
        total = part if total is None else total + part
        got = got.reshape(half, -1)
        u_ref[rows, :] = got[:, 0:width].astype(BF16)
        one_ref[rows, :] = got[:, width + 2 * LANES :].astype(BF16)
        columns_ref[rows, :] = jnp.where(
            core == 0,
            got[:, here : here + fields],
            got[:, here + fields : here + 2 * fields],
        ).astype(BF16)
    wide = jnp.tanh(dot(one_ref[...], branch_second_ref[...]))
    two_ref[...] = wide.astype(BF16)
    features_ref[...] = dot(two_ref[...], branch_third_ref[...]).astype(BF16)
    feature_back = (dot(u_ref[...], third_ref[...]) * scale).astype(BF16)
    feature_back_ref[...] = feature_back
    back_two = (dot(feature_back, branch_third_ref[...], NT) * (1.0 - wide * wide)).astype(BF16)
    back_two_ref[...] = back_two
    one = one_ref[...].astype(F32)
    back_one = (dot(back_two, branch_second_ref[...], NT) * (1.0 - one * one)).astype(BF16)
    rows = dot(columns_ref[...], back_one, TN)
    parts = [rows[:, lane : lane + LANES] for lane in range(0, width, LANES)]
    rows_ref[...] = jnp.concatenate(parts + [total[:, 0:LANES]], axis=0).astype(BF16)
    deep = width // across
    for axis in range(2):
        for strip in range(deep):
            first_ref[axis : axis + 1, strip * across : (strip + 1) * across] = total[
                axis * deep + strip : axis * deep + strip + 1, LANES : LANES + across
            ]


def gradient_kernel(
    scale,
    u_ref,
    features_ref,
    two_ref,
    feature_back_ref,
    one_ref,
    back_two_ref,
    trunk_ref,
    third_ref,
    second_ref,
):
    trunk_ref[...] = dot(u_ref[...], features_ref[...], TN) * scale
    third_ref[...] = dot(two_ref[...], feature_back_ref[...], TN)
    second_ref[...] = dot(one_ref[...], back_two_ref[...], TN)


def spread_rows(from_ref, grad_ref):
    got = from_ref[...].astype(F32)
    fields = grad_ref.shape[2]
    for lane in range(grad_ref.shape[3] // LANES):
        grad_ref[:, 0, :, lane * LANES : (lane + 1) * LANES] = got[
            :, lane * fields : (lane + 1) * fields
        ]
    return got


def mine_kernel(core_ref, mine_ref, grad_ref, second_ref):
    step = pl.program_id(0)
    tail = spread_rows(mine_ref, grad_ref)[:, -8:].reshape(-1, LANES)
    width = second_ref.shape[0]
    for now in range(width * width // tail.size):

        @pl.when(step == now)
        def _():
            strip, row = divmod(now * tail.shape[0], width)
            second_ref[row : row + tail.shape[0], strip * LANES : (strip + 1) * LANES] = tail


def other_kernel(core_ref, other_ref, kept_ref, grad_ref):
    spread_rows(other_ref, grad_ref)


def whole(*shape):
    return pl.BlockSpec(shape, lambda i: (0,) * len(shape))


def there(value):
    return pltpu.with_memory_space_constraint(value, pltpu.HBM)


SCALAR = pl.BlockSpec(memory_space=pltpu.SMEM)
LOCAL = pl.BlockSpec(memory_space=pltpu.VMEM)


def tiles(points):
    tile = min(TILE, points)
    deep = lambda n, width: pl.BlockSpec((n, tile, width), lambda i: (0, i, 0))
    return tile, deep


def first_call(sensors, first, count):
    own, depth = sensors.shape
    width = first.shape[1]
    part = depth // STEPS
    return pl.pallas_call(
        first_kernel,
        grid=(STEPS,),
        in_specs=[
            pl.BlockSpec((own, part), lambda i: (0, i)),
            pl.BlockSpec((part, width), lambda i: (i, 0)),
        ],
        out_specs=[whole(own, width), whole(count, own, width)],
        out_shape=[
            jax.ShapeDtypeStruct((own, width), BF16),
            jax.ShapeDtypeStruct((count, own, width), BF16),
        ],
        scratch_shapes=[pltpu.VMEM((own, width), F32)],
        compiler_params=PARAMS,
        name="branch_first",
    )(there(sensors), there(first))


def forward_call(coords, first, second):
    points, width = coords.shape[1], first.shape[1]
    tile, deep = tiles(points)
    flat = pl.BlockSpec((tile, width), lambda i: (i, 0))
    return pl.pallas_call(
        forward_kernel,
        grid=(points // tile,),
        in_specs=[
            pl.BlockSpec((2, tile), lambda i: (0, i)),
            whole(2, width),
            whole(width, width),
        ],
        out_specs=[deep(4, width), flat, deep(7, width), deep(5, width), whole(8, width, width)],
        out_shape=[
            pltpu.HBM((4, points, width), BF16),
            pltpu.HBM((points, width), F32),
            pltpu.HBM((7, points, width), BF16),
            pltpu.HBM((5, points, width), BF16),
            pltpu.HBM((8, width, width), BF16),
        ],
        scratch_shapes=[pltpu.VMEM((tile, width), F32), pltpu.VMEM((8, tile, width), F32)],
        compiler_params=PARAMS,
        name="trunk_forward",
    )(coords, first, second)


def project_call(ones, branch_second, branch_third, third, combos, forcing, weight, scale):
    funcs, points = forcing.shape
    width = third.shape[0]
    tile = min(PROJECT, points)
    return pl.pallas_call(
        functools.partial(project_kernel, weight, scale),
        grid=(points // tile,),
        in_specs=[
            whole(*ones.shape),
            whole(width, width),
            whole(width, width),
            whole(width, width),
            pl.BlockSpec((5, tile, width), lambda i: (0, i, 0)),
            pl.BlockSpec((funcs, tile), lambda i: (0, i)),
        ],
        out_specs=[
            pl.BlockSpec((5, funcs, tile), lambda i: (0, 0, i)),
            whole(funcs, width),
            whole(*ones.shape),
        ],
        out_shape=[
            pltpu.HBM((5, funcs, points), BF16),
            pltpu.HBM((funcs, width), BF16),
            jax.ShapeDtypeStruct(ones.shape, BF16),
        ],
        scratch_shapes=[pltpu.VMEM((funcs, width), F32)],
        compiler_params=PARAMS,
        name="project",
    )(ones, branch_second, branch_third, third, there(combos), there(forcing))


def backward_call(
    squash, points_all, inner, cots, feats, coords, weights, first, second, pieces
):
    points, width = squash.shape
    funcs = feats.shape[0]
    tile, deep = tiles(points)
    return pl.pallas_call(
        backward_kernel,
        grid=(points // tile,),
        in_specs=[
            pl.BlockSpec((tile, width), lambda i: (i, 0)),
            deep(4, width),
            deep(7, width),
            pl.BlockSpec((5, funcs, tile), lambda i: (0, 0, i)),
            whole(funcs, width),
            pl.BlockSpec((2, tile), lambda i: (0, i)),
            whole(8, width, width),
            whole(2, width),
            whole(width, width),
        ],
        out_specs=whole(*pieces),
        out_shape=jax.ShapeDtypeStruct(pieces, F32),
        scratch_shapes=[
            pltpu.VMEM((5, tile, width), F32),
            pltpu.VMEM((8, tile, width), BF16),
            pltpu.VMEM((4, tile, width), F32),
            pltpu.VMEM((tile, width), BF16),
            pltpu.VMEM((8, width, width), F32),
            pltpu.VMEM((16, width), F32),
        ],
        compiler_params=PARAMS,
        cost_estimate=pl.CostEstimate(
            flops=42 * points * width * width, bytes_accessed=48 * points * width, transcendentals=0
        ),
        name="trunk_backward",
    )(
        there(squash),
        there(points_all),
        there(inner),
        there(cots),
        there(feats),
        coords,
        there(weights),
        first,
        second,
    )


def branch_call(core, mine, other, third, branch_third, branch_second, fields, scale):
    count, width = 2 * mine.shape[0] * mine.shape[1], third.shape[0]
    rows = fields * (width // LANES) + mine.shape[1]
    return pl.pallas_call(
        functools.partial(branch_kernel, scale),
        in_specs=[SCALAR] + [LOCAL] * 5,
        out_shape=[jax.ShapeDtypeStruct((count, width), BF16)] * 6
        + [jax.ShapeDtypeStruct((rows, LANES), BF16), jax.ShapeDtypeStruct((2, width), F32)],
        scratch_shapes=[pltpu.VMEM((count, fields), BF16)],
        compiler_params=SMALL,
        name="branch_backward",
    )(core, mine, other, third, branch_third, branch_second)


def gradient_call(u, features, two, feature_back, one, back_two, scale):
    shape = (u.shape[1], features.shape[1])
    return pl.pallas_call(
        functools.partial(gradient_kernel, scale),
        in_specs=[LOCAL] * 6,
        out_shape=[jax.ShapeDtypeStruct(shape, F32)] * 3,
        compiler_params=SMALL,
        name="branch_gradients",
    )(u, features, two, feature_back, one, back_two)


def spread_specs(got, shape, side):
    steps = STEPS
    part = got.shape[0] // steps
    fields = shape[0] // (2 * got.shape[0])
    return (
        steps,
        pl.BlockSpec((part, *got.shape[1:]), lambda j, c: (j, 0, 0)),
        pl.BlockSpec((part, 1, fields, shape[1]), lambda j, c: (j, side(c[0]), 0, 0)),
        jax.ShapeDtypeStruct((got.shape[0], 2, fields, shape[1]), F32),
    )


def mine_call(core, mine, shape, width):
    steps, piece, place, out = spread_specs(mine, shape, lambda c: c)
    return pl.pallas_call(
        mine_kernel,
        grid_spec=pltpu.PrefetchScalarGridSpec(
            num_scalar_prefetch=1,
            grid=(steps,),
            in_specs=[piece],
            out_specs=[place, pl.BlockSpec((width, width), lambda j, c: (0, 0))],
        ),
        out_shape=[out, jax.ShapeDtypeStruct((width, width), F32)],
        compiler_params=PARAMS,
        name="spread_mine",
    )(core, mine)


def other_call(core, other, kept, shape):
    steps, piece, place, out = spread_specs(other, shape, lambda c: 1 - c)
    return pl.pallas_call(
        other_kernel,
        grid_spec=pltpu.PrefetchScalarGridSpec(
            num_scalar_prefetch=1,
            grid=(steps,),
            in_specs=[piece, pl.BlockSpec(memory_space=pl.ANY)],
            out_specs=place,
        ),
        out_shape=out,
        input_output_aliases={2: 0},
        compiler_params=PARAMS,
        name="spread_other",
    )(core, other, kept)


def swap(parts, axes):
    return lax.all_to_all(parts, axes, split_axis=0, concat_axis=0, tiled=True)


def across_chip(value):
    return lax.ppermute(value, "core", [(0, 1), (1, 0)])


def per_device(
    sensors,
    forcing,
    coords,
    branch_first,
    branch_second,
    branch_third,
    trunk_first,
    trunk_second,
    trunk_third,
):
    pairs, pts_size = lax.axis_size("pairs"), lax.axis_size("pts")
    func_size = 2 * pairs
    chips = pairs * pts_size
    core = lax.axis_index("core").reshape(1)
    funcs = forcing.shape[0]
    weight = 1.0 / math.sqrt(funcs * func_size * forcing.shape[1] * pts_size)
    width_out = trunk_third.shape[1]
    width = trunk_second.shape[0]
    scale = width_out ** (-0.5)
    own = sensors.shape[0]
    fields = sensors.shape[1] // chips

    own_one, told_one = first_call(sensors, branch_first, pts_size)
    ones = swap(told_one, "pts")
    blocks = sensors.reshape(own, chips, fields).transpose(1, 0, 2)
    points_all, squash, inner, combos, weights = forward_call(coords, trunk_first, trunk_second)
    cots, feats, shares = project_call(
        ones,
        branch_second,
        branch_third,
        trunk_third,
        combos,
        forcing,
        weight,
        scale,
    )
    u_own = swap(shares, "pts").astype(F32).sum(0).astype(BF16)
    second_pieces = backward_call(
        squash,
        points_all,
        inner,
        cots,
        feats,
        coords,
        weights,
        trunk_first,
        trunk_second,
        (chips, own, LANES + 2 * width // own),
    )
    told = lambda part: jnp.broadcast_to(part[None], (chips, *part.shape))
    pieces = jnp.concatenate(
        [
            told(u_own),
            second_pieces.astype(BF16),
            blocks,
            told(own_one),
        ],
        axis=2,
    )
    every = swap(pieces, ("pairs", "pts"))
    every_other = across_chip(every)
    u, features, two, feature_back, one, back_two, rows, grad_t1 = branch_call(
        core, every, every_other, trunk_third, branch_third, branch_second, fields // 2, scale
    )
    mine = swap(told(rows), ("pairs", "pts"))
    other = across_chip(mine)
    grad_t3, grad_b3, grad_b2 = gradient_call(
        u, features, two, feature_back, one, back_two, scale
    )
    kept, grad_t2 = mine_call(core, mine, branch_first.shape, width)
    grad_b1 = other_call(core, other, kept, branch_first.shape).reshape(branch_first.shape)
    return (grad_b1, grad_b2, grad_b3, grad_t1, grad_t2, grad_t3)


def solution(mesh):
    func_size, pts_size = mesh.devices.shape
    cores = jax.sharding.Mesh(mesh.devices.reshape(func_size // 2, 2, pts_size), AXES)
    return jax.shard_map(
        per_device,
        mesh=cores,
        in_specs=(
            P(AXES, None),
            P(("pairs", "core"), "pts"),
            P(None, "pts"),
            P(),
            P(),
            P(),
            P(),
            P(),
            P(),
        ),
        out_specs=(P(), P(), P(), P(), P(), P()),
        check_vma=False,
    )
```

```python
import functools
import math

import jax
import jax.numpy as jnp
from jax import lax
from jax.experimental import pallas as pl
from jax.experimental.pallas import tpu as pltpu
from jax.sharding import PartitionSpec as P

DRAG = 0.5
TILE = 512
PROJECT = 1024
ROWS = 16
PARTS = 2
CHUNK = 256
STEPS = 2
LANES = 128
F32 = jnp.float32
BF16 = jnp.bfloat16
AXES = ("pairs", "core", "pts")
GROUP = (0, 1, 1, 2, 2, 2, 3, 3)
NT = (((1,), (1,)), ((), ()))
TN = (((0,), (0,)), ((), ()))
PARAMS = pltpu.CompilerParams(
    dimension_semantics=("arbitrary",), vmem_limit_bytes=40 * 1024 * 1024
)
SMALL = pltpu.CompilerParams(vmem_limit_bytes=24 * 1024 * 1024)


def dot(left, right, dims=(((1,), (0,)), ((), ()))):
    return lax.dot_general(left, right, dims, preferred_element_type=F32)


def slopes(squash):
    square = squash * squash
    one = 1.0 - square
    two = -2.0 * (squash * one)
    three = one * (6.0 * square - 2.0)
    return square, one, two, three


def chunks(rows, width, body):
    for start in range(*rows, ROWS):
        body(pl.ds(start, ROWS), pl.ds(0, width))


def constants(first):
    a, b = first[0:1], first[1:2]
    one, zero = jnp.ones_like(a), jnp.zeros_like(a)
    square = a * a + b * b
    consts = [one, a, b, -square, b * b - a * a, -2.0 * a * b, -a * square, -b * square]
    by_a = [zero, one, zero, -2.0 * a, -2.0 * a, -2.0 * b, -(3.0 * a * a + b * b), -2.0 * a * b]
    by_b = [zero, zero, one, -2.0 * b, 2.0 * b, -2.0 * a, -2.0 * a * b, -(a * a + 3.0 * b * b)]
    return jnp.concatenate(consts + by_a + by_b, axis=0).T


def thirds(value):
    parts = []
    for _ in range(3):
        part = value.astype(BF16).astype(F32)
        parts.append(part)
        value = value - part
    return parts


def first_kernel(sensors_ref, first_ref, own_ref, told_ref, total_ref):
    step = pl.program_id(0)

    @pl.when(step == 0)
    def _():
        total_ref[...] = jnp.zeros_like(total_ref)

    total_ref[...] += dot(sensors_ref[...], first_ref[...])

    @pl.when(step == pl.num_programs(0) - 1)
    def _():
        one = jnp.tanh(total_ref[...])
        own_ref[...] = one.astype(BF16)
        told_ref[...] = jnp.broadcast_to(one[None], told_ref.shape).astype(BF16)


def forward_kernel(
    coords_ref,
    first_ref,
    second_ref,
    points_ref,
    squash_ref,
    inner_ref,
    combos_ref,
    weights_ref,
    values_ref,
    wide_ref,
):
    @pl.when(pl.program_id(0) == 0)
    def _():
        consts = constants(first_ref[...])
        second = second_ref[...].astype(F32)
        for part in range(8):
            weights_ref[part] = (consts[:, part : part + 1] * second).astype(BF16)

    left, right = thirds(coords_ref[...]), thirds(first_ref[...])
    pairs = ((0, 0), (0, 1), (1, 0), (0, 2), (2, 0), (1, 1))
    left = [left[i] for i, _ in pairs] + [jnp.zeros_like(left[0])] * 2
    right = [right[j] for _, j in pairs] + [jnp.zeros_like(right[0])] * 2
    values_ref[...] = dot(
        jnp.concatenate(left, axis=0).astype(BF16), jnp.concatenate(right, axis=0).astype(BF16), TN
    )

    def layer_one(rows, lanes):
        squash = jnp.tanh(values_ref[rows, lanes])
        _, one, two, three = slopes(squash)
        for group, part in enumerate((squash, one, two, three)):
            points_ref[group, rows, lanes] = part.astype(BF16)


    def layer_two(rows, lanes):
        z, zx, zy, lap, dif, mix, px, py = (wide_ref[part, rows, lanes] for part in range(8))
        squash = jnp.tanh(z)
        squash_ref[rows, lanes] = squash
        for part, value in enumerate((zx, zy, lap, dif, mix, px, py)):
            inner_ref[part, rows, lanes] = value.astype(BF16)
        _, one, two, three = slopes(squash)
        radius = zx * zx + zy * zy
        twice = lap + lap
        bend = three * radius
        along = zx * (twice + dif) + zy * mix
        across = zy * (twice - dif) + zx * mix
        combos = (
            one * zx,
            one * zy,
            one * lap - two * radius,
            one * px + two * along - bend * zx,
            one * py + two * across - bend * zy,
        )
        for k, combo in enumerate(combos):
            combos_ref[k, rows, lanes] = combo.astype(BF16)

    tile, width = values_ref.shape
    part_rows = tile // max(1, min(PARTS, tile // LANES))
    for start in range(0, tile, part_rows):
        rows = (start, start + part_rows)
        chunks(rows, width, layer_one)
        span = pl.ds(start, part_rows)
        for part, group in enumerate(GROUP):
            wide_ref[part, span] = dot(points_ref[group, span], weights_ref[part])
    for start in range(0, tile, part_rows):
        chunks((start, start + part_rows), width, layer_two)


def project_kernel(
    weight,
    scale,
    ones_ref,
    branch_second_ref,
    branch_third_ref,
    third_ref,
    combos_ref,
    forcing_ref,
    cots_ref,
    feats_ref,
    shares_ref,
    u_ref,
):
    @pl.when(pl.program_id(0) == 0)
    def _():
        u_ref[...] = jnp.zeros_like(u_ref)
        one = ones_ref[...].astype(F32).reshape(u_ref.shape).astype(BF16)
        two = jnp.tanh(dot(one, branch_second_ref[...])).astype(BF16)
        features = dot(two, branch_third_ref[...]).astype(BF16)
        feats_ref[...] = (dot(features, third_ref[...], NT) * scale).astype(BF16)

    feats = feats_ref[...]
    tile = forcing_ref.shape[1]
    for start in range(0, tile, min(CHUNK, tile)):
        span = pl.ds(start, min(CHUNK, tile))
        px, py, om, omx, omy = (dot(feats, combos_ref[k, span], NT) for k in range(5))
        residual = py * omx - px * omy + DRAG * om - forcing_ref[:, span].astype(F32)
        slope = residual * weight
        parts = (-slope * omy, slope * omx, DRAG * slope, slope * py, -slope * px)
        for k, part in enumerate(parts):
            cots_ref[k, :, span] = part.astype(BF16)
    total = u_ref[...]
    for k in range(5):
        total += dot(cots_ref[k], combos_ref[k])
    u_ref[...] = total

    @pl.when(pl.program_id(0) == pl.num_programs(0) - 1)
    def _():
        shares_ref[...] = u_ref[...].reshape(shares_ref.shape).astype(BF16)


def backward_kernel(
    squash_ref,
    points_ref,
    inner_ref,
    cots_ref,
    feats_ref,
    coords_ref,
    weights_ref,
    first_ref,
    second_ref,
    pieces_ref,
    back_ref,
    inner_back_ref,
    ones_ref,
    one_back_ref,
    grads_ref,
    value_ref,
):
    step = pl.program_id(0)
    last = pl.num_programs(0) - 1
    width = second_ref.shape[0]

    @pl.when(step == 0)
    def _():
        grads_ref[...] = jnp.zeros_like(grads_ref)
        value_ref[...] = jnp.zeros_like(value_ref)

    feats = feats_ref[...]

    def layer_two_back(rows, lanes):
        squash = squash_ref[rows, lanes]
        zx, zy, lap, dif, mix, px, py = (
            inner_ref[part, rows, lanes].astype(F32) for part in range(7)
        )
        gx, gy, gl, gp, gq = (back_ref[k, rows, lanes] for k in range(5))
        square, one, two, three = slopes(squash)
        four = two * (12.0 * square - 8.0)
        radius = zx * zx + zy * zy
        twice = lap + lap
        plus, minus = twice + dif, twice - dif
        along = zx * plus + zy * mix
        across = zy * minus + zx * mix
        pull = gp * zx + gq * zy
        one_bar = gx * zx + gy * zy + gl * lap + gp * px + gq * py
        two_bar = gp * along + gq * across - gl * radius
        three_bar = pull * radius
        along_bar, across_bar = two * gp, two * gq
        turn = -2.0 * (two * gl + three * pull)
        bend = three * radius
        xa, yc = zx * along_bar, zy * across_bar
        parts = (
            two * one_bar + three * two_bar - four * three_bar,
            one * gx - bend * gp + zx * turn + along_bar * plus + across_bar * mix,
            one * gy - bend * gq + zy * turn + across_bar * minus + along_bar * mix,
            one * gl + 2.0 * (xa + yc),
            xa - yc,
            zy * along_bar + zx * across_bar,
            one * gp,
            one * gq,
        )
        for part, value in enumerate(parts):
            inner_back_ref[part, rows, lanes] = value.astype(BF16)

    def layer_one_back(rows, lanes):
        squash, one, two, three = (points_ref[part, rows, lanes].astype(F32) for part in range(4))
        four = two * (4.0 - 12.0 * one)
        back = (
            one * ones_ref[0, rows, lanes]
            + two * ones_ref[1, rows, lanes]
            + three * ones_ref[2, rows, lanes]
            + four * ones_ref[3, rows, lanes]
        )
        one_back_ref[rows, lanes] = back.astype(BF16)

    tile = squash_ref.shape[0]
    part_rows = tile // max(1, min(PARTS, tile // LANES))
    spans = [(start, start + part_rows) for start in range(0, tile, part_rows)]
    for start, stop in spans:
        for k in range(5):
            back_ref[k, start:stop] = dot(cots_ref[k, :, start:stop], feats, TN)
    for start, stop in spans:
        chunks((start, stop), width, layer_two_back)
        for group in range(4):
            total = None
            for part in range(8):
                if GROUP[part] == group:
                    term = dot(inner_back_ref[part, start:stop], weights_ref[part], NT)
                    total = term if total is None else total + term
            ones_ref[group, start:stop] = total
    for part, group in enumerate(GROUP):
        grads_ref[part] += dot(points_ref[group], inner_back_ref[part], TN)
    for start, stop in spans:
        chunks((start, stop), width, layer_one_back)
    coords = jnp.concatenate(thirds(coords_ref[...]) + [jnp.zeros_like(coords_ref)] * 5, axis=0)
    value_ref[...] += dot(coords.astype(BF16), one_back_ref[...])

    @pl.when(step == last)
    def _():
        second = second_ref[...].astype(F32)
        consts = constants(first_ref[...])
        g = [grads_ref[part] for part in range(8)]
        column = lambda part: consts[:, part : part + 1]
        total = g[0]
        for part in range(1, 8):
            total += column(part) * g[part]
        both, less = g[3] + g[4], g[3] - g[4]
        by_a = g[1] + column(11) * both + column(13) * g[5] + column(14) * g[6] + column(15) * g[7]
        by_b = g[2] + column(19) * less + column(21) * g[5] + column(22) * g[6] + column(23) * g[7]
        first = [jnp.sum(second * by, axis=1, keepdims=True) for by in (by_a, by_b)]
        lane = lax.broadcasted_iota(jnp.int32, (width, LANES), 1)
        both = jnp.where(lane == 0, first[0], 0.0) + jnp.where(lane == 1, first[1], 0.0)
        first_grad = value_ref[0:2] + value_ref[2:4] + value_ref[4:6] + both.T[0:2]
        count, own, _ = pieces_ref.shape
        strips = width // LANES
        part = count // strips
        for strip in range(strips):
            block = total[:, strip * LANES : (strip + 1) * LANES]
            pieces_ref[strip * part : (strip + 1) * part, :, 0:LANES] = block.reshape(
                part, own, LANES
            )
        across = 2 * width // own
        rows = [
            first_grad[axis : axis + 1, lane : lane + across]
            for axis in range(2)
            for lane in range(0, width, across)
        ]
        told = jnp.concatenate(rows, axis=0)
        pieces_ref[:, :, LANES:] = jnp.broadcast_to(told[None], (count, *told.shape))


def branch_kernel(
    scale,
    fields,
    core_ref,
    from_ref,
    third_ref,
    branch_third_ref,
    branch_second_ref,
    *refs,
):
    first = len(refs) == 8
    sums = () if first else refs[:2]
    u_ref, features_ref, two_ref, feature_back_ref, one_ref, back_two_ref = refs[-8:-2]
    core = core_ref[0]
    width = third_ref.shape[0]
    half = u_ref.shape[0]
    across = 2 * width // from_ref.shape[1]
    here = width + LANES + across
    got = from_ref[...].astype(F32)
    total = jnp.sum(got[:, :, width : width + 2 * LANES], axis=0)
    got = got.reshape(half, -1)
    u = got[:, 0:width].astype(BF16)
    one = got[:, width + 2 * LANES :]
    columns = jnp.where(
        core == 0,
        got[:, here : here + fields],
        got[:, here + fields : here + 2 * fields],
    ).astype(BF16)
    u_ref[...] = u
    one_ref[...] = one.astype(BF16)
    wide = jnp.tanh(dot(one_ref[...], branch_second_ref[...]))
    two_ref[...] = wide.astype(BF16)
    features_ref[...] = dot(two_ref[...], branch_third_ref[...]).astype(BF16)
    feature_back = (dot(u, third_ref[...]) * scale).astype(BF16)
    feature_back_ref[...] = feature_back
    back_two = (dot(feature_back, branch_third_ref[...], NT) * (1.0 - wide * wide)).astype(BF16)
    back_two_ref[...] = back_two
    back_one = (dot(back_two, branch_second_ref[...], NT) * (1.0 - one * one)).astype(BF16)
    rows = dot(columns, back_one, TN)
    if first:
        refs[-2][...] = rows
        refs[-1][...] = total
        return
    rows_ref, first_ref = refs[-2:]
    rows, total = rows + sums[0][...], total + sums[1][...]
    parts = [rows[:, lane : lane + LANES] for lane in range(0, width, LANES)]
    rows_ref[...] = jnp.concatenate(parts + [total[:, 0:LANES]], axis=0).astype(BF16)
    deep = width // across
    for axis in range(2):
        for strip in range(deep):
            first_ref[axis : axis + 1, strip * across : (strip + 1) * across] = total[
                axis * deep + strip : axis * deep + strip + 1, LANES : LANES + across
            ]


def gradient_kernel(scale, *refs):
    mine, other, outs = refs[:6], refs[6:12], refs[12:]
    for out_ref, (left, right), by in zip(outs, ((0, 1), (2, 3), (4, 5)), (scale, None, None)):
        parts = [dot(half[left][...], half[right][...], TN) for half in (mine, other)]
        total = parts[0] + parts[1]
        out_ref[...] = total if by is None else total * by


def spread_rows(from_ref, grad_ref):
    got = from_ref[...].astype(F32)
    fields = grad_ref.shape[2]
    for lane in range(grad_ref.shape[3] // LANES):
        grad_ref[:, 0, :, lane * LANES : (lane + 1) * LANES] = got[
            :, lane * fields : (lane + 1) * fields
        ]
    return got


def mine_kernel(core_ref, mine_ref, grad_ref, second_ref):
    step = pl.program_id(0)
    tail = spread_rows(mine_ref, grad_ref)[:, -8:].reshape(-1, LANES)
    width = second_ref.shape[0]
    for now in range(width * width // tail.size):

        @pl.when(step == now)
        def _():
            strip, row = divmod(now * tail.shape[0], width)
            second_ref[row : row + tail.shape[0], strip * LANES : (strip + 1) * LANES] = tail


def other_kernel(core_ref, other_ref, kept_ref, grad_ref):
    spread_rows(other_ref, grad_ref)


def whole(*shape):
    return pl.BlockSpec(shape, lambda i: (0,) * len(shape))


def there(value):
    return pltpu.with_memory_space_constraint(value, pltpu.HBM)


SCALAR = pl.BlockSpec(memory_space=pltpu.SMEM)
LOCAL = pl.BlockSpec(memory_space=pltpu.VMEM)


def tiles(points):
    tile = min(TILE, points)
    deep = lambda n, width: pl.BlockSpec((n, tile, width), lambda i: (0, i, 0))
    return tile, deep


def first_call(sensors, first, count):
    own, depth = sensors.shape
    width = first.shape[1]
    part = depth // STEPS
    return pl.pallas_call(
        first_kernel,
        grid=(STEPS,),
        in_specs=[
            pl.BlockSpec((own, part), lambda i: (0, i)),
            pl.BlockSpec((part, width), lambda i: (i, 0)),
        ],
        out_specs=[whole(own, width), whole(count, own, width)],
        out_shape=[
            jax.ShapeDtypeStruct((own, width), BF16),
            jax.ShapeDtypeStruct((count, own, width), BF16),
        ],
        scratch_shapes=[pltpu.VMEM((own, width), F32)],
        compiler_params=PARAMS,
        name="branch_first",
    )(there(sensors), there(first))


def forward_call(coords, first, second):
    points, width = coords.shape[1], first.shape[1]
    tile, deep = tiles(points)
    flat = pl.BlockSpec((tile, width), lambda i: (i, 0))
    return pl.pallas_call(
        forward_kernel,
        grid=(points // tile,),
        in_specs=[
            pl.BlockSpec((2, tile), lambda i: (0, i)),
            whole(2, width),
            whole(width, width),
        ],
        out_specs=[deep(4, width), flat, deep(7, width), deep(5, width), whole(8, width, width)],
        out_shape=[
            pltpu.HBM((4, points, width), BF16),
            pltpu.HBM((points, width), F32),
            pltpu.HBM((7, points, width), BF16),
            pltpu.HBM((5, points, width), BF16),
            pltpu.HBM((8, width, width), BF16),
        ],
        scratch_shapes=[pltpu.VMEM((tile, width), F32), pltpu.VMEM((8, tile, width), F32)],
        compiler_params=PARAMS,
        name="trunk_forward",
    )(coords, first, second)


def project_call(ones, branch_second, branch_third, third, combos, forcing, weight, scale):
    funcs, points = forcing.shape
    width = third.shape[0]
    tile = min(PROJECT, points)
    return pl.pallas_call(
        functools.partial(project_kernel, weight, scale),
        grid=(points // tile,),
        in_specs=[
            whole(*ones.shape),
            whole(width, width),
            whole(width, width),
            whole(width, width),
            pl.BlockSpec((5, tile, width), lambda i: (0, i, 0)),
            pl.BlockSpec((funcs, tile), lambda i: (0, i)),
        ],
        out_specs=[
            pl.BlockSpec((5, funcs, tile), lambda i: (0, 0, i)),
            whole(funcs, width),
            whole(*ones.shape),
        ],
        out_shape=[
            pltpu.HBM((5, funcs, points), BF16),
            pltpu.HBM((funcs, width), BF16),
            jax.ShapeDtypeStruct(ones.shape, BF16),
        ],
        scratch_shapes=[pltpu.VMEM((funcs, width), F32)],
        compiler_params=PARAMS,
        name="project",
    )(ones, branch_second, branch_third, third, there(combos), there(forcing))


def backward_call(
    squash, points_all, inner, cots, feats, coords, weights, first, second, pieces
):
    points, width = squash.shape
    funcs = feats.shape[0]
    tile, deep = tiles(points)
    return pl.pallas_call(
        backward_kernel,
        grid=(points // tile,),
        in_specs=[
            pl.BlockSpec((tile, width), lambda i: (i, 0)),
            deep(4, width),
            deep(7, width),
            pl.BlockSpec((5, funcs, tile), lambda i: (0, 0, i)),
            whole(funcs, width),
            pl.BlockSpec((2, tile), lambda i: (0, i)),
            whole(8, width, width),
            whole(2, width),
            whole(width, width),
        ],
        out_specs=whole(*pieces),
        out_shape=jax.ShapeDtypeStruct(pieces, F32),
        scratch_shapes=[
            pltpu.VMEM((5, tile, width), F32),
            pltpu.VMEM((8, tile, width), BF16),
            pltpu.VMEM((4, tile, width), F32),
            pltpu.VMEM((tile, width), BF16),
            pltpu.VMEM((8, width, width), F32),
            pltpu.VMEM((16, width), F32),
        ],
        compiler_params=PARAMS,
        cost_estimate=pl.CostEstimate(
            flops=42 * points * width * width, bytes_accessed=48 * points * width, transcendentals=0
        ),
        name="trunk_backward",
    )(
        there(squash),
        there(points_all),
        there(inner),
        there(cots),
        there(feats),
        coords,
        there(weights),
        first,
        second,
    )


def branch_call(core, got, third, branch_third, branch_second, fields, scale, sums=()):
    count, own, width = got.shape[0] * got.shape[1], got.shape[1], third.shape[0]
    rows = fields * (width // LANES) + own
    last = [jax.ShapeDtypeStruct((fields, width), F32), jax.ShapeDtypeStruct((own, 2 * LANES), F32)]
    if sums:
        last = [jax.ShapeDtypeStruct((rows, LANES), BF16), jax.ShapeDtypeStruct((2, width), F32)]
    return pl.pallas_call(
        functools.partial(branch_kernel, scale, fields),
        in_specs=[SCALAR] + [LOCAL] * (4 + len(sums)),
        out_shape=[jax.ShapeDtypeStruct((count, width), BF16)] * 6 + last,
        compiler_params=SMALL,
        name="branch_other" if sums else "branch_mine",
    )(core, got, third, branch_third, branch_second, *sums)


def gradient_call(mine, other, scale):
    shape = (mine[0].shape[1], mine[1].shape[1])
    return pl.pallas_call(
        functools.partial(gradient_kernel, scale),
        in_specs=[LOCAL] * 12,
        out_shape=[jax.ShapeDtypeStruct(shape, F32)] * 3,
        compiler_params=SMALL,
        name="branch_gradients",
    )(*mine, *other)


def spread_specs(got, shape, side):
    steps = STEPS
    part = got.shape[0] // steps
    fields = shape[0] // (2 * got.shape[0])
    return (
        steps,
        pl.BlockSpec((part, *got.shape[1:]), lambda j, c: (j, 0, 0)),
        pl.BlockSpec((part, 1, fields, shape[1]), lambda j, c: (j, side(c[0]), 0, 0)),
        jax.ShapeDtypeStruct((got.shape[0], 2, fields, shape[1]), F32),
    )


def mine_call(core, mine, shape, width):
    steps, piece, place, out = spread_specs(mine, shape, lambda c: c)
    return pl.pallas_call(
        mine_kernel,
        grid_spec=pltpu.PrefetchScalarGridSpec(
            num_scalar_prefetch=1,
            grid=(steps,),
            in_specs=[piece],
            out_specs=[place, pl.BlockSpec((width, width), lambda j, c: (0, 0))],
        ),
        out_shape=[out, jax.ShapeDtypeStruct((width, width), F32)],
        compiler_params=PARAMS,
        name="spread_mine",
    )(core, mine)


def other_call(core, other, kept, shape):
    steps, piece, place, out = spread_specs(other, shape, lambda c: 1 - c)
    return pl.pallas_call(
        other_kernel,
        grid_spec=pltpu.PrefetchScalarGridSpec(
            num_scalar_prefetch=1,
            grid=(steps,),
            in_specs=[piece, pl.BlockSpec(memory_space=pl.ANY)],
            out_specs=place,
        ),
        out_shape=out,
        input_output_aliases={2: 0},
        compiler_params=PARAMS,
        name="spread_other",
    )(core, other, kept)


def swap(parts, axes):
    return lax.all_to_all(parts, axes, split_axis=0, concat_axis=0, tiled=True)


def across_chip(value):
    return lax.ppermute(value, "core", [(0, 1), (1, 0)])


def per_device(
    sensors,
    forcing,
    coords,
    branch_first,
    branch_second,
    branch_third,
    trunk_first,
    trunk_second,
    trunk_third,
):
    pairs, pts_size = lax.axis_size("pairs"), lax.axis_size("pts")
    func_size = 2 * pairs
    chips = pairs * pts_size
    core = lax.axis_index("core").reshape(1)
    funcs = forcing.shape[0]
    weight = 1.0 / math.sqrt(funcs * func_size * forcing.shape[1] * pts_size)
    width_out = trunk_third.shape[1]
    width = trunk_second.shape[0]
    scale = width_out ** (-0.5)
    own = sensors.shape[0]
    fields = sensors.shape[1] // chips

    own_one, told_one = first_call(sensors, branch_first, pts_size)
    ones = swap(told_one, "pts")
    blocks = sensors.reshape(own, chips, fields).transpose(1, 0, 2)
    points_all, squash, inner, combos, weights = forward_call(coords, trunk_first, trunk_second)
    cots, feats, shares = project_call(
        ones,
        branch_second,
        branch_third,
        trunk_third,
        combos,
        forcing,
        weight,
        scale,
    )
    u_own = swap(shares, "pts").astype(F32).sum(0).astype(BF16)
    second_pieces = backward_call(
        squash,
        points_all,
        inner,
        cots,
        feats,
        coords,
        weights,
        trunk_first,
        trunk_second,
        (chips, own, LANES + 2 * width // own),
    )
    told = lambda part: jnp.broadcast_to(part[None], (chips, *part.shape))
    pieces = jnp.concatenate(
        [
            told(u_own),
            second_pieces.astype(BF16),
            blocks,
            told(own_one),
        ],
        axis=2,
    )
    every = swap(pieces, ("pairs", "pts"))
    every_other = across_chip(every)
    branch = functools.partial(
        branch_call,
        core,
        third=trunk_third,
        branch_third=branch_third,
        branch_second=branch_second,
        fields=fields // 2,
        scale=scale,
    )
    *half_mine, rows, total = branch(got=every)
    *half_other, rows, grad_t1 = branch(got=every_other, sums=(rows, total))
    mine = swap(told(rows), ("pairs", "pts"))
    other = across_chip(mine)
    grad_t3, grad_b3, grad_b2 = gradient_call(half_mine, half_other, scale)
    kept, grad_t2 = mine_call(core, mine, branch_first.shape, width)
    grad_b1 = other_call(core, other, kept, branch_first.shape).reshape(branch_first.shape)
    return (grad_b1, grad_b2, grad_b3, grad_t1, grad_t2, grad_t3)


def solution(mesh):
    func_size, pts_size = mesh.devices.shape
    cores = jax.sharding.Mesh(mesh.devices.reshape(func_size // 2, 2, pts_size), AXES)
    return jax.shard_map(
        per_device,
        mesh=cores,
        in_specs=(
            P(AXES, None),
            P(("pairs", "core"), "pts"),
            P(None, "pts"),
            P(),
            P(),
            P(),
            P(),
            P(),
            P(),
        ),
        out_specs=(P(), P(), P(), P(), P(), P()),
        check_vma=False,
    )
```

```python
import functools
import math

import jax
import jax.numpy as jnp
from jax import lax
from jax.experimental import pallas as pl
from jax.experimental.pallas import tpu as pltpu
from jax.sharding import PartitionSpec as P

DRAG = 0.5
TILE = 512
PROJECT = 1024
ROWS = 16
PARTS = 2
CHUNK = 256
STEPS = 2
LANES = 128
F32 = jnp.float32
BF16 = jnp.bfloat16
AXES = ("pairs", "core", "pts")
GROUP = (0, 1, 1, 2, 2, 2, 3, 3)
NT = (((1,), (1,)), ((), ()))
TN = (((0,), (0,)), ((), ()))
PARAMS = pltpu.CompilerParams(
    dimension_semantics=("arbitrary",), vmem_limit_bytes=40 * 1024 * 1024
)
SMALL = pltpu.CompilerParams(vmem_limit_bytes=24 * 1024 * 1024)


def dot(left, right, dims=(((1,), (0,)), ((), ()))):
    return lax.dot_general(left, right, dims, preferred_element_type=F32)


def slopes(squash):
    square = squash * squash
    one = 1.0 - square
    two = -2.0 * (squash * one)
    three = one * (6.0 * square - 2.0)
    return square, one, two, three


def chunks(rows, width, body):
    for start in range(*rows, ROWS):
        body(pl.ds(start, ROWS), pl.ds(0, width))


def constants(first):
    a, b = first[0:1], first[1:2]
    one, zero = jnp.ones_like(a), jnp.zeros_like(a)
    square = a * a + b * b
    consts = [one, a, b, -square, b * b - a * a, -2.0 * a * b, -a * square, -b * square]
    by_a = [zero, one, zero, -2.0 * a, -2.0 * a, -2.0 * b, -(3.0 * a * a + b * b), -2.0 * a * b]
    by_b = [zero, zero, one, -2.0 * b, 2.0 * b, -2.0 * a, -2.0 * a * b, -(a * a + 3.0 * b * b)]
    return jnp.concatenate(consts + by_a + by_b, axis=0).T


def thirds(value):
    parts = []
    for _ in range(3):
        part = value.astype(BF16).astype(F32)
        parts.append(part)
        value = value - part
    return parts


def first_kernel(sensors_ref, first_ref, own_ref, told_ref, total_ref):
    step = pl.program_id(0)

    @pl.when(step == 0)
    def _():
        total_ref[...] = jnp.zeros_like(total_ref)

    total_ref[...] += dot(sensors_ref[...], first_ref[...])

    @pl.when(step == pl.num_programs(0) - 1)
    def _():
        one = jnp.tanh(total_ref[...])
        own_ref[...] = one.astype(BF16)
        told_ref[...] = jnp.broadcast_to(one[None], told_ref.shape).astype(BF16)


def forward_kernel(
    coords_ref,
    first_ref,
    second_ref,
    points_ref,
    squash_ref,
    inner_ref,
    combos_ref,
    weights_ref,
    values_ref,
    wide_ref,
):
    @pl.when(pl.program_id(0) == 0)
    def _():
        consts = constants(first_ref[...])
        second = second_ref[...].astype(F32)
        for part in range(8):
            weights_ref[part] = (consts[:, part : part + 1] * second).astype(BF16)

    left, right = thirds(coords_ref[...]), thirds(first_ref[...])
    pairs = ((0, 0), (0, 1), (1, 0), (0, 2), (2, 0), (1, 1))
    left = [left[i] for i, _ in pairs] + [jnp.zeros_like(left[0])] * 2
    right = [right[j] for _, j in pairs] + [jnp.zeros_like(right[0])] * 2
    values_ref[...] = dot(
        jnp.concatenate(left, axis=0).astype(BF16), jnp.concatenate(right, axis=0).astype(BF16), TN
    )

    def layer_one(rows, lanes):
        squash = jnp.tanh(values_ref[rows, lanes])
        _, one, two, three = slopes(squash)
        for group, part in enumerate((squash, one, two, three)):
            points_ref[group, rows, lanes] = part.astype(BF16)


    def layer_two(rows, lanes):
        z, zx, zy, lap, dif, mix, px, py = (wide_ref[part, rows, lanes] for part in range(8))
        squash = jnp.tanh(z)
        squash_ref[rows, lanes] = squash
        for part, value in enumerate((zx, zy, lap, dif, mix, px, py)):
            inner_ref[part, rows, lanes] = value.astype(BF16)
        _, one, two, three = slopes(squash)
        radius = zx * zx + zy * zy
        twice = lap + lap
        bend = three * radius
        along = zx * (twice + dif) + zy * mix
        across = zy * (twice - dif) + zx * mix
        combos = (
            one * zx,
            one * zy,
            one * lap - two * radius,
            one * px + two * along - bend * zx,
            one * py + two * across - bend * zy,
        )
        for k, combo in enumerate(combos):
            combos_ref[k, rows, lanes] = combo.astype(BF16)

    tile, width = values_ref.shape
    part_rows = tile // max(1, min(PARTS, tile // LANES))
    for start in range(0, tile, part_rows):
        rows = (start, start + part_rows)
        chunks(rows, width, layer_one)
        span = pl.ds(start, part_rows)
        for part, group in enumerate(GROUP):
            wide_ref[part, span] = dot(points_ref[group, span], weights_ref[part])
    for start in range(0, tile, part_rows):
        chunks((start, start + part_rows), width, layer_two)


def project_kernel(
    weight,
    scale,
    ones_ref,
    branch_second_ref,
    branch_third_ref,
    third_ref,
    combos_ref,
    forcing_ref,
    cots_ref,
    feats_ref,
    shares_ref,
    u_ref,
):
    @pl.when(pl.program_id(0) == 0)
    def _():
        u_ref[...] = jnp.zeros_like(u_ref)
        one = ones_ref[...].astype(F32).reshape(u_ref.shape).astype(BF16)
        two = jnp.tanh(dot(one, branch_second_ref[...])).astype(BF16)
        features = dot(two, branch_third_ref[...]).astype(BF16)
        feats_ref[...] = (dot(features, third_ref[...], NT) * scale).astype(BF16)

    feats = feats_ref[...]
    tile = forcing_ref.shape[1]
    for start in range(0, tile, min(CHUNK, tile)):
        span = pl.ds(start, min(CHUNK, tile))
        px, py, om, omx, omy = (dot(feats, combos_ref[k, span], NT) for k in range(5))
        residual = py * omx - px * omy + DRAG * om - forcing_ref[:, span].astype(F32)
        slope = residual * weight
        parts = (-slope * omy, slope * omx, DRAG * slope, slope * py, -slope * px)
        for k, part in enumerate(parts):
            cots_ref[k, :, span] = part.astype(BF16)
    total = u_ref[...]
    for k in range(5):
        total += dot(cots_ref[k], combos_ref[k])
    u_ref[...] = total

    @pl.when(pl.program_id(0) == pl.num_programs(0) - 1)
    def _():
        shares_ref[...] = u_ref[...].reshape(shares_ref.shape).astype(BF16)


def backward_kernel(
    squash_ref,
    points_ref,
    inner_ref,
    cots_ref,
    feats_ref,
    coords_ref,
    weights_ref,
    first_ref,
    second_ref,
    pieces_ref,
    back_ref,
    inner_back_ref,
    ones_ref,
    one_back_ref,
    grads_ref,
    value_ref,
):
    step = pl.program_id(0)
    last = pl.num_programs(0) - 1
    width = second_ref.shape[0]

    @pl.when(step == 0)
    def _():
        grads_ref[...] = jnp.zeros_like(grads_ref)
        value_ref[...] = jnp.zeros_like(value_ref)

    feats = feats_ref[...]

    def layer_two_back(rows, lanes):
        squash = squash_ref[rows, lanes]
        zx, zy, lap, dif, mix, px, py = (
            inner_ref[part, rows, lanes].astype(F32) for part in range(7)
        )
        gx, gy, gl, gp, gq = (back_ref[k, rows, lanes] for k in range(5))
        square, one, two, three = slopes(squash)
        four = two * (12.0 * square - 8.0)
        radius = zx * zx + zy * zy
        twice = lap + lap
        plus, minus = twice + dif, twice - dif
        along = zx * plus + zy * mix
        across = zy * minus + zx * mix
        pull = gp * zx + gq * zy
        one_bar = gx * zx + gy * zy + gl * lap + gp * px + gq * py
        two_bar = gp * along + gq * across - gl * radius
        three_bar = pull * radius
        along_bar, across_bar = two * gp, two * gq
        turn = -2.0 * (two * gl + three * pull)
        bend = three * radius
        xa, yc = zx * along_bar, zy * across_bar
        parts = (
            two * one_bar + three * two_bar - four * three_bar,
            one * gx - bend * gp + zx * turn + along_bar * plus + across_bar * mix,
            one * gy - bend * gq + zy * turn + across_bar * minus + along_bar * mix,
            one * gl + 2.0 * (xa + yc),
            xa - yc,
            zy * along_bar + zx * across_bar,
            one * gp,
            one * gq,
        )
        for part, value in enumerate(parts):
            inner_back_ref[part, rows, lanes] = value.astype(BF16)

    def layer_one_back(rows, lanes):
        squash, one, two, three = (points_ref[part, rows, lanes].astype(F32) for part in range(4))
        four = two * (4.0 - 12.0 * one)
        back = (
            one * ones_ref[0, rows, lanes]
            + two * ones_ref[1, rows, lanes]
            + three * ones_ref[2, rows, lanes]
            + four * ones_ref[3, rows, lanes]
        )
        one_back_ref[rows, lanes] = back.astype(BF16)

    tile = squash_ref.shape[0]
    part_rows = tile // max(1, min(PARTS, tile // LANES))
    spans = [(start, start + part_rows) for start in range(0, tile, part_rows)]
    for start, stop in spans:
        for k in range(5):
            back_ref[k, start:stop] = dot(cots_ref[k, :, start:stop], feats, TN)
    for start, stop in spans:
        chunks((start, stop), width, layer_two_back)
        for group in range(4):
            total = None
            for part in range(8):
                if GROUP[part] == group:
                    term = dot(inner_back_ref[part, start:stop], weights_ref[part], NT)
                    total = term if total is None else total + term
            ones_ref[group, start:stop] = total
    for part, group in enumerate(GROUP):
        grads_ref[part] += dot(points_ref[group], inner_back_ref[part], TN)
    for start, stop in spans:
        chunks((start, stop), width, layer_one_back)
    coords = jnp.concatenate(thirds(coords_ref[...]) + [jnp.zeros_like(coords_ref)] * 5, axis=0)
    value_ref[...] += dot(coords.astype(BF16), one_back_ref[...])

    @pl.when(step == last)
    def _():
        second = second_ref[...].astype(F32)
        consts = constants(first_ref[...])
        g = [grads_ref[part] for part in range(8)]
        column = lambda part: consts[:, part : part + 1]
        total = g[0]
        for part in range(1, 8):
            total += column(part) * g[part]
        both, less = g[3] + g[4], g[3] - g[4]
        by_a = g[1] + column(11) * both + column(13) * g[5] + column(14) * g[6] + column(15) * g[7]
        by_b = g[2] + column(19) * less + column(21) * g[5] + column(22) * g[6] + column(23) * g[7]
        first = [jnp.sum(second * by, axis=1, keepdims=True) for by in (by_a, by_b)]
        lane = lax.broadcasted_iota(jnp.int32, (width, LANES), 1)
        both = jnp.where(lane == 0, first[0], 0.0) + jnp.where(lane == 1, first[1], 0.0)
        first_grad = value_ref[0:2] + value_ref[2:4] + value_ref[4:6] + both.T[0:2]
        count, own, _ = pieces_ref.shape
        strips = width // LANES
        part = count // strips
        for strip in range(strips):
            block = total[:, strip * LANES : (strip + 1) * LANES]
            pieces_ref[strip * part : (strip + 1) * part, :, 0:LANES] = block.reshape(
                part, own, LANES
            )
        across = 2 * width // own
        rows = [
            first_grad[axis : axis + 1, lane : lane + across]
            for axis in range(2)
            for lane in range(0, width, across)
        ]
        told = jnp.concatenate(rows, axis=0)
        pieces_ref[:, :, LANES:] = jnp.broadcast_to(told[None], (count, *told.shape))


def branch_kernel(
    scale,
    fields,
    core_ref,
    from_ref,
    third_ref,
    branch_third_ref,
    branch_second_ref,
    *refs,
):
    first = len(refs) == 11
    sums = () if first else refs[:2]
    start = len(sums)
    u_ref, features_ref, two_ref, feature_back_ref, one_ref, back_two_ref = refs[start : start + 6]
    core = core_ref[0]
    width = third_ref.shape[0]
    half = u_ref.shape[0]
    across = 2 * width // from_ref.shape[1]
    here = width + LANES + across
    got = from_ref[...].astype(F32)
    total = jnp.sum(got[:, :, width : width + 2 * LANES], axis=0)
    got = got.reshape(half, -1)
    u = got[:, 0:width].astype(BF16)
    one = got[:, width + 2 * LANES :]
    columns = jnp.where(
        core == 0,
        got[:, here : here + fields],
        got[:, here + fields : here + 2 * fields],
    ).astype(BF16)
    u_ref[...] = u
    one_ref[...] = one.astype(BF16)
    wide = jnp.tanh(dot(one_ref[...], branch_second_ref[...]))
    two_ref[...] = wide.astype(BF16)
    features_ref[...] = dot(two_ref[...], branch_third_ref[...]).astype(BF16)
    feature_back = (dot(u, third_ref[...]) * scale).astype(BF16)
    feature_back_ref[...] = feature_back
    back_two = (dot(feature_back, branch_third_ref[...], NT) * (1.0 - wide * wide)).astype(BF16)
    back_two_ref[...] = back_two
    back_one = (dot(back_two, branch_second_ref[...], NT) * (1.0 - one * one)).astype(BF16)
    rows = dot(columns, back_one, TN)
    if first:
        refs[6][...] = rows
        refs[7][...] = total
        refs[8][...] = dot(u, features_ref[...], TN)
        refs[9][...] = dot(two_ref[...], feature_back, TN)
        refs[10][...] = dot(one_ref[...], back_two, TN)
        return
    rows_ref, first_ref = refs[-2:]
    rows, total = rows + sums[0][...], total + sums[1][...]
    parts = [rows[:, lane : lane + LANES] for lane in range(0, width, LANES)]
    rows_ref[...] = jnp.concatenate(parts + [total[:, 0:LANES]], axis=0).astype(BF16)
    deep = width // across
    for axis in range(2):
        for strip in range(deep):
            first_ref[axis : axis + 1, strip * across : (strip + 1) * across] = total[
                axis * deep + strip : axis * deep + strip + 1, LANES : LANES + across
            ]


def gradient_kernel(scale, *refs):
    mine, other, outs = refs[:3], refs[3:9], refs[9:]
    for k, by in enumerate((scale, None, None)):
        total = mine[k][...] + dot(other[2 * k][...], other[2 * k + 1][...], TN)
        outs[k][...] = total if by is None else total * by


def spread_rows(from_ref, grad_ref):
    got = from_ref[...].astype(F32)
    fields = grad_ref.shape[2]
    for lane in range(grad_ref.shape[3] // LANES):
        grad_ref[:, 0, :, lane * LANES : (lane + 1) * LANES] = got[
            :, lane * fields : (lane + 1) * fields
        ]
    return got


def mine_kernel(core_ref, mine_ref, grad_ref, second_ref):
    step = pl.program_id(0)
    tail = spread_rows(mine_ref, grad_ref)[:, -8:].reshape(-1, LANES)
    width = second_ref.shape[0]
    for now in range(width * width // tail.size):

        @pl.when(step == now)
        def _():
            strip, row = divmod(now * tail.shape[0], width)
            second_ref[row : row + tail.shape[0], strip * LANES : (strip + 1) * LANES] = tail


def other_kernel(core_ref, other_ref, kept_ref, grad_ref):
    spread_rows(other_ref, grad_ref)


def whole(*shape):
    return pl.BlockSpec(shape, lambda i: (0,) * len(shape))


def there(value):
    return pltpu.with_memory_space_constraint(value, pltpu.HBM)


SCALAR = pl.BlockSpec(memory_space=pltpu.SMEM)
LOCAL = pl.BlockSpec(memory_space=pltpu.VMEM)


def tiles(points):
    tile = min(TILE, points)
    deep = lambda n, width: pl.BlockSpec((n, tile, width), lambda i: (0, i, 0))
    return tile, deep


def first_call(sensors, first, count):
    own, depth = sensors.shape
    width = first.shape[1]
    part = depth // STEPS
    return pl.pallas_call(
        first_kernel,
        grid=(STEPS,),
        in_specs=[
            pl.BlockSpec((own, part), lambda i: (0, i)),
            pl.BlockSpec((part, width), lambda i: (i, 0)),
        ],
        out_specs=[whole(own, width), whole(count, own, width)],
        out_shape=[
            jax.ShapeDtypeStruct((own, width), BF16),
            jax.ShapeDtypeStruct((count, own, width), BF16),
        ],
        scratch_shapes=[pltpu.VMEM((own, width), F32)],
        compiler_params=PARAMS,
        name="branch_first",
    )(there(sensors), there(first))


def forward_call(coords, first, second):
    points, width = coords.shape[1], first.shape[1]
    tile, deep = tiles(points)
    flat = pl.BlockSpec((tile, width), lambda i: (i, 0))
    return pl.pallas_call(
        forward_kernel,
        grid=(points // tile,),
        in_specs=[
            pl.BlockSpec((2, tile), lambda i: (0, i)),
            whole(2, width),
            whole(width, width),
        ],
        out_specs=[deep(4, width), flat, deep(7, width), deep(5, width), whole(8, width, width)],
        out_shape=[
            pltpu.HBM((4, points, width), BF16),
            pltpu.HBM((points, width), F32),
            pltpu.HBM((7, points, width), BF16),
            pltpu.HBM((5, points, width), BF16),
            pltpu.HBM((8, width, width), BF16),
        ],
        scratch_shapes=[pltpu.VMEM((tile, width), F32), pltpu.VMEM((8, tile, width), F32)],
        compiler_params=PARAMS,
        name="trunk_forward",
    )(coords, first, second)


def project_call(ones, branch_second, branch_third, third, combos, forcing, weight, scale):
    funcs, points = forcing.shape
    width = third.shape[0]
    tile = min(PROJECT, points)
    return pl.pallas_call(
        functools.partial(project_kernel, weight, scale),
        grid=(points // tile,),
        in_specs=[
            whole(*ones.shape),
            whole(width, width),
            whole(width, width),
            whole(width, width),
            pl.BlockSpec((5, tile, width), lambda i: (0, i, 0)),
            pl.BlockSpec((funcs, tile), lambda i: (0, i)),
        ],
        out_specs=[
            pl.BlockSpec((5, funcs, tile), lambda i: (0, 0, i)),
            whole(funcs, width),
            whole(*ones.shape),
        ],
        out_shape=[
            pltpu.HBM((5, funcs, points), BF16),
            jax.ShapeDtypeStruct((funcs, width), BF16),
            jax.ShapeDtypeStruct(ones.shape, BF16),
        ],
        scratch_shapes=[pltpu.VMEM((funcs, width), F32)],
        compiler_params=PARAMS,
        name="project",
    )(ones, branch_second, branch_third, third, there(combos), there(forcing))


def backward_call(
    squash, points_all, inner, cots, feats, coords, weights, first, second, pieces
):
    points, width = squash.shape
    funcs = feats.shape[0]
    tile, deep = tiles(points)
    return pl.pallas_call(
        backward_kernel,
        grid=(points // tile,),
        in_specs=[
            pl.BlockSpec((tile, width), lambda i: (i, 0)),
            deep(4, width),
            deep(7, width),
            pl.BlockSpec((5, funcs, tile), lambda i: (0, 0, i)),
            whole(funcs, width),
            pl.BlockSpec((2, tile), lambda i: (0, i)),
            whole(8, width, width),
            whole(2, width),
            whole(width, width),
        ],
        out_specs=whole(*pieces),
        out_shape=jax.ShapeDtypeStruct(pieces, F32),
        scratch_shapes=[
            pltpu.VMEM((5, tile, width), F32),
            pltpu.VMEM((8, tile, width), BF16),
            pltpu.VMEM((4, tile, width), F32),
            pltpu.VMEM((tile, width), BF16),
            pltpu.VMEM((8, width, width), F32),
            pltpu.VMEM((16, width), F32),
        ],
        compiler_params=PARAMS,
        cost_estimate=pl.CostEstimate(
            flops=42 * points * width * width, bytes_accessed=48 * points * width, transcendentals=0
        ),
        name="trunk_backward",
    )(
        there(squash),
        there(points_all),
        there(inner),
        there(cots),
        feats,
        coords,
        weights,
        first,
        second,
    )


def branch_call(core, got, third, branch_third, branch_second, fields, scale, sums=()):
    count, own, width = got.shape[0] * got.shape[1], got.shape[1], third.shape[0]
    rows = fields * (width // LANES) + own
    last = [jax.ShapeDtypeStruct((fields, width), F32), jax.ShapeDtypeStruct((own, 2 * LANES), F32)]
    last += [jax.ShapeDtypeStruct((width, width), F32)] * 3
    if sums:
        last = [jax.ShapeDtypeStruct((rows, LANES), BF16), jax.ShapeDtypeStruct((2, width), F32)]
    return pl.pallas_call(
        functools.partial(branch_kernel, scale, fields),
        in_specs=[SCALAR] + [LOCAL] * (4 + len(sums)),
        out_shape=[jax.ShapeDtypeStruct((count, width), BF16)] * 6 + last,
        compiler_params=SMALL,
        name="branch_other" if sums else "branch_mine",
    )(core, got, third, branch_third, branch_second, *sums)


def gradient_call(mine, other, scale):
    shape = mine[0].shape
    return pl.pallas_call(
        functools.partial(gradient_kernel, scale),
        in_specs=[LOCAL] * 9,
        out_shape=[jax.ShapeDtypeStruct(shape, F32)] * 3,
        compiler_params=SMALL,
        name="branch_gradients",
    )(*mine, *other)


def spread_specs(got, shape, side):
    steps = STEPS
    part = got.shape[0] // steps
    fields = shape[0] // (2 * got.shape[0])
    return (
        steps,
        pl.BlockSpec((part, *got.shape[1:]), lambda j, c: (j, 0, 0)),
        pl.BlockSpec((part, 1, fields, shape[1]), lambda j, c: (j, side(c[0]), 0, 0)),
        jax.ShapeDtypeStruct((got.shape[0], 2, fields, shape[1]), F32),
    )


def mine_call(core, mine, shape, width):
    steps, piece, place, out = spread_specs(mine, shape, lambda c: c)
    return pl.pallas_call(
        mine_kernel,
        grid_spec=pltpu.PrefetchScalarGridSpec(
            num_scalar_prefetch=1,
            grid=(steps,),
            in_specs=[piece],
            out_specs=[place, pl.BlockSpec((width, width), lambda j, c: (0, 0))],
        ),
        out_shape=[out, jax.ShapeDtypeStruct((width, width), F32)],
        compiler_params=PARAMS,
        name="spread_mine",
    )(core, mine)


def other_call(core, other, kept, shape):
    steps, piece, place, out = spread_specs(other, shape, lambda c: 1 - c)
    return pl.pallas_call(
        other_kernel,
        grid_spec=pltpu.PrefetchScalarGridSpec(
            num_scalar_prefetch=1,
            grid=(steps,),
            in_specs=[piece, pl.BlockSpec(memory_space=pl.ANY)],
            out_specs=place,
        ),
        out_shape=out,
        input_output_aliases={2: 0},
        compiler_params=PARAMS,
        name="spread_other",
    )(core, other, kept)


def swap(parts, axes):
    return lax.all_to_all(parts, axes, split_axis=0, concat_axis=0, tiled=True)


def across_chip(value):
    return lax.ppermute(value, "core", [(0, 1), (1, 0)])


def per_device(
    sensors,
    forcing,
    coords,
    branch_first,
    branch_second,
    branch_third,
    trunk_first,
    trunk_second,
    trunk_third,
):
    pairs, pts_size = lax.axis_size("pairs"), lax.axis_size("pts")
    func_size = 2 * pairs
    chips = pairs * pts_size
    core = lax.axis_index("core").reshape(1)
    funcs = forcing.shape[0]
    weight = 1.0 / math.sqrt(funcs * func_size * forcing.shape[1] * pts_size)
    width_out = trunk_third.shape[1]
    width = trunk_second.shape[0]
    scale = width_out ** (-0.5)
    own = sensors.shape[0]
    fields = sensors.shape[1] // chips

    own_one, told_one = first_call(sensors, branch_first, pts_size)
    ones = swap(told_one, "pts")
    blocks = sensors.reshape(own, chips, fields).transpose(1, 0, 2)
    points_all, squash, inner, combos, weights = forward_call(coords, trunk_first, trunk_second)
    cots, feats, shares = project_call(
        ones,
        branch_second,
        branch_third,
        trunk_third,
        combos,
        forcing,
        weight,
        scale,
    )
    u_own = swap(shares, "pts").astype(F32).sum(0).astype(BF16)
    second_pieces = backward_call(
        squash,
        points_all,
        inner,
        cots,
        feats,
        coords,
        weights,
        trunk_first,
        trunk_second,
        (chips, own, LANES + 2 * width // own),
    )
    told = lambda part: jnp.broadcast_to(part[None], (chips, *part.shape))
    pieces = jnp.concatenate(
        [
            told(u_own),
            second_pieces.astype(BF16),
            blocks,
            told(own_one),
        ],
        axis=2,
    )
    every = swap(pieces, ("pairs", "pts"))
    every_other = across_chip(every)
    branch = functools.partial(
        branch_call,
        core,
        third=trunk_third,
        branch_third=branch_third,
        branch_second=branch_second,
        fields=fields // 2,
        scale=scale,
    )
    *_, rows, total, sum_t3, sum_b3, sum_b2 = branch(got=every)
    *half_other, rows, grad_t1 = branch(got=every_other, sums=(rows, total))
    mine = swap(told(rows), ("pairs", "pts"))
    other = across_chip(mine)
    grad_t3, grad_b3, grad_b2 = gradient_call(
        (sum_t3, sum_b3, sum_b2), half_other, scale
    )
    kept, grad_t2 = mine_call(core, mine, branch_first.shape, width)
    grad_b1 = other_call(core, other, kept, branch_first.shape).reshape(branch_first.shape)
    return (grad_b1, grad_b2, grad_b3, grad_t1, grad_t2, grad_t3)


def solution(mesh):
    func_size, pts_size = mesh.devices.shape
    cores = jax.sharding.Mesh(mesh.devices.reshape(func_size // 2, 2, pts_size), AXES)
    return jax.shard_map(
        per_device,
        mesh=cores,
        in_specs=(
            P(AXES, None),
            P(("pairs", "core"), "pts"),
            P(None, "pts"),
            P(),
            P(),
            P(),
            P(),
            P(),
            P(),
        ),
        out_specs=(P(), P(), P(), P(), P(), P()),
        check_vma=False,
    )
```

```python
import functools
import math

import jax
import jax.numpy as jnp
from jax import lax
from jax.experimental import pallas as pl
from jax.experimental.pallas import tpu as pltpu
from jax.sharding import PartitionSpec as P

DRAG = 0.5
TILE = 512
PROJECT = 1024
ROWS = 32
PARTS = 1
CHUNK = 512
STEPS = 2
LANES = 128
F32 = jnp.float32
BF16 = jnp.bfloat16
AXES = ("pairs", "core", "pts")
GROUP = (0, 1, 1, 2, 2, 2, 3, 3)
NT = (((1,), (1,)), ((), ()))
TN = (((0,), (0,)), ((), ()))
PARAMS = pltpu.CompilerParams(
    dimension_semantics=("arbitrary",), vmem_limit_bytes=40 * 1024 * 1024
)
SMALL = pltpu.CompilerParams(vmem_limit_bytes=24 * 1024 * 1024)


def dot(left, right, dims=(((1,), (0,)), ((), ()))):
    return lax.dot_general(left, right, dims, preferred_element_type=F32)


def slopes(squash):
    square = squash * squash
    one = 1.0 - square
    two = -2.0 * (squash * one)
    three = one * (6.0 * square - 2.0)
    return square, one, two, three


def chunks(rows, width, body):
    for start in range(*rows, ROWS):
        body(pl.ds(start, ROWS), pl.ds(0, width))


def constants(first):
    a, b = first[0:1], first[1:2]
    one, zero = jnp.ones_like(a), jnp.zeros_like(a)
    square = a * a + b * b
    consts = [one, a, b, -square, b * b - a * a, -2.0 * a * b, -a * square, -b * square]
    by_a = [zero, one, zero, -2.0 * a, -2.0 * a, -2.0 * b, -(3.0 * a * a + b * b), -2.0 * a * b]
    by_b = [zero, zero, one, -2.0 * b, 2.0 * b, -2.0 * a, -2.0 * a * b, -(a * a + 3.0 * b * b)]
    return jnp.concatenate(consts + by_a + by_b, axis=0).T


def thirds(value):
    parts = []
    for _ in range(3):
        part = value.astype(BF16).astype(F32)
        parts.append(part)
        value = value - part
    return parts


def first_kernel(sensors_ref, first_ref, own_ref, told_ref, total_ref):
    step = pl.program_id(0)

    @pl.when(step == 0)
    def _():
        total_ref[...] = jnp.zeros_like(total_ref)

    total_ref[...] += dot(sensors_ref[...], first_ref[...])

    @pl.when(step == pl.num_programs(0) - 1)
    def _():
        one = jnp.tanh(total_ref[...])
        own_ref[...] = one.astype(BF16)
        told_ref[...] = jnp.broadcast_to(one[None], told_ref.shape).astype(BF16)


def forward_kernel(
    coords_ref,
    first_ref,
    second_ref,
    points_ref,
    squash_ref,
    inner_ref,
    combos_ref,
    weights_ref,
    values_ref,
    wide_ref,
):
    @pl.when(pl.program_id(0) == 0)
    def _():
        consts = constants(first_ref[...])
        second = second_ref[...].astype(F32)
        for part in range(8):
            weights_ref[part] = (consts[:, part : part + 1] * second).astype(BF16)

    left, right = thirds(coords_ref[...]), thirds(first_ref[...])
    pairs = ((0, 0), (0, 1), (1, 0), (0, 2), (2, 0), (1, 1))
    left = [left[i] for i, _ in pairs] + [jnp.zeros_like(left[0])] * 2
    right = [right[j] for _, j in pairs] + [jnp.zeros_like(right[0])] * 2
    values_ref[...] = dot(
        jnp.concatenate(left, axis=0).astype(BF16), jnp.concatenate(right, axis=0).astype(BF16), TN
    )

    def layer_one(rows, lanes):
        squash = jnp.tanh(values_ref[rows, lanes])
        _, one, two, three = slopes(squash)
        for group, part in enumerate((squash, one, two, three)):
            points_ref[group, rows, lanes] = part.astype(BF16)


    def layer_two(rows, lanes):
        z, zx, zy, lap, dif, mix, px, py = (wide_ref[part, rows, lanes] for part in range(8))
        squash = jnp.tanh(z)
        squash_ref[rows, lanes] = squash
        for part, value in enumerate((zx, zy, lap, dif, mix, px, py)):
            inner_ref[part, rows, lanes] = value.astype(BF16)
        _, one, two, three = slopes(squash)
        radius = zx * zx + zy * zy
        twice = lap + lap
        bend = three * radius
        along = zx * (twice + dif) + zy * mix
        across = zy * (twice - dif) + zx * mix
        combos = (
            one * zx,
            one * zy,
            one * lap - two * radius,
            one * px + two * along - bend * zx,
            one * py + two * across - bend * zy,
        )
        for k, combo in enumerate(combos):
            combos_ref[k, rows, lanes] = combo.astype(BF16)

    tile, width = values_ref.shape
    part_rows = tile // max(1, min(PARTS, tile // LANES))
    for start in range(0, tile, part_rows):
        rows = (start, start + part_rows)
        chunks(rows, width, layer_one)
        span = pl.ds(start, part_rows)
        for part, group in enumerate(GROUP):
            wide_ref[part, span] = dot(points_ref[group, span], weights_ref[part])
    for start in range(0, tile, part_rows):
        chunks((start, start + part_rows), width, layer_two)


def project_kernel(
    weight,
    scale,
    ones_ref,
    branch_second_ref,
    branch_third_ref,
    third_ref,
    combos_ref,
    forcing_ref,
    cots_ref,
    feats_ref,
    shares_ref,
    u_ref,
):
    @pl.when(pl.program_id(0) == 0)
    def _():
        u_ref[...] = jnp.zeros_like(u_ref)
        one = ones_ref[...].astype(F32).reshape(u_ref.shape).astype(BF16)
        two = jnp.tanh(dot(one, branch_second_ref[...])).astype(BF16)
        features = dot(two, branch_third_ref[...]).astype(BF16)
        feats_ref[...] = (dot(features, third_ref[...], NT) * scale).astype(BF16)

    feats = feats_ref[...]
    tile = forcing_ref.shape[1]
    for start in range(0, tile, min(CHUNK, tile)):
        span = pl.ds(start, min(CHUNK, tile))
        px, py, om, omx, omy = (dot(feats, combos_ref[k, span], NT) for k in range(5))
        residual = py * omx - px * omy + DRAG * om - forcing_ref[:, span].astype(F32)
        slope = residual * weight
        parts = (-slope * omy, slope * omx, DRAG * slope, slope * py, -slope * px)
        for k, part in enumerate(parts):
            cots_ref[k, :, span] = part.astype(BF16)
    total = u_ref[...]
    for k in range(5):
        total += dot(cots_ref[k], combos_ref[k])
    u_ref[...] = total

    @pl.when(pl.program_id(0) == pl.num_programs(0) - 1)
    def _():
        shares_ref[...] = u_ref[...].reshape(shares_ref.shape).astype(BF16)


def backward_kernel(
    squash_ref,
    points_ref,
    inner_ref,
    cots_ref,
    feats_ref,
    coords_ref,
    weights_ref,
    first_ref,
    second_ref,
    pieces_ref,
    back_ref,
    inner_back_ref,
    ones_ref,
    one_back_ref,
    grads_ref,
    value_ref,
):
    step = pl.program_id(0)
    last = pl.num_programs(0) - 1
    width = second_ref.shape[0]

    @pl.when(step == 0)
    def _():
        grads_ref[...] = jnp.zeros_like(grads_ref)
        value_ref[...] = jnp.zeros_like(value_ref)

    feats = feats_ref[...]

    def layer_two_back(rows, lanes):
        squash = squash_ref[rows, lanes]
        zx, zy, lap, dif, mix, px, py = (
            inner_ref[part, rows, lanes].astype(F32) for part in range(7)
        )
        gx, gy, gl, gp, gq = (back_ref[k, rows, lanes] for k in range(5))
        square, one, two, three = slopes(squash)
        four = two * (12.0 * square - 8.0)
        radius = zx * zx + zy * zy
        twice = lap + lap
        plus, minus = twice + dif, twice - dif
        along = zx * plus + zy * mix
        across = zy * minus + zx * mix
        pull = gp * zx + gq * zy
        one_bar = gx * zx + gy * zy + gl * lap + gp * px + gq * py
        two_bar = gp * along + gq * across - gl * radius
        three_bar = pull * radius
        along_bar, across_bar = two * gp, two * gq
        turn = -2.0 * (two * gl + three * pull)
        bend = three * radius
        xa, yc = zx * along_bar, zy * across_bar
        parts = (
            two * one_bar + three * two_bar - four * three_bar,
            one * gx - bend * gp + zx * turn + along_bar * plus + across_bar * mix,
            one * gy - bend * gq + zy * turn + across_bar * minus + along_bar * mix,
            one * gl + 2.0 * (xa + yc),
            xa - yc,
            zy * along_bar + zx * across_bar,
            one * gp,
            one * gq,
        )
        for part, value in enumerate(parts):
            inner_back_ref[part, rows, lanes] = value.astype(BF16)

    def layer_one_back(rows, lanes):
        squash, one, two, three = (points_ref[part, rows, lanes].astype(F32) for part in range(4))
        four = two * (4.0 - 12.0 * one)
        back = (
            one * ones_ref[0, rows, lanes]
            + two * ones_ref[1, rows, lanes]
            + three * ones_ref[2, rows, lanes]
            + four * ones_ref[3, rows, lanes]
        )
        one_back_ref[rows, lanes] = back.astype(BF16)

    tile = squash_ref.shape[0]
    part_rows = tile // max(1, min(PARTS, tile // LANES))
    spans = [(start, start + part_rows) for start in range(0, tile, part_rows)]
    for start, stop in spans:
        for k in range(5):
            back_ref[k, start:stop] = dot(cots_ref[k, :, start:stop], feats, TN)
    for start, stop in spans:
        chunks((start, stop), width, layer_two_back)
        for group in range(4):
            total = None
            for part in range(8):
                if GROUP[part] == group:
                    term = dot(inner_back_ref[part, start:stop], weights_ref[part], NT)
                    total = term if total is None else total + term
            ones_ref[group, start:stop] = total
    for part, group in enumerate(GROUP):
        grads_ref[part] += dot(points_ref[group], inner_back_ref[part], TN)
    for start, stop in spans:
        chunks((start, stop), width, layer_one_back)
    coords = jnp.concatenate(thirds(coords_ref[...]) + [jnp.zeros_like(coords_ref)] * 5, axis=0)
    value_ref[...] += dot(coords.astype(BF16), one_back_ref[...])

    @pl.when(step == last)
    def _():
        second = second_ref[...].astype(F32)
        consts = constants(first_ref[...])
        g = [grads_ref[part] for part in range(8)]
        column = lambda part: consts[:, part : part + 1]
        total = g[0]
        for part in range(1, 8):
            total += column(part) * g[part]
        both, less = g[3] + g[4], g[3] - g[4]
        by_a = g[1] + column(11) * both + column(13) * g[5] + column(14) * g[6] + column(15) * g[7]
        by_b = g[2] + column(19) * less + column(21) * g[5] + column(22) * g[6] + column(23) * g[7]
        first = [jnp.sum(second * by, axis=1, keepdims=True) for by in (by_a, by_b)]
        lane = lax.broadcasted_iota(jnp.int32, (width, LANES), 1)
        both = jnp.where(lane == 0, first[0], 0.0) + jnp.where(lane == 1, first[1], 0.0)
        first_grad = value_ref[0:2] + value_ref[2:4] + value_ref[4:6] + both.T[0:2]
        count, own, _ = pieces_ref.shape
        strips = width // LANES
        part = count // strips
        for strip in range(strips):
            block = total[:, strip * LANES : (strip + 1) * LANES]
            pieces_ref[strip * part : (strip + 1) * part, :, 0:LANES] = block.reshape(
                part, own, LANES
            )
        across = 2 * width // own
        rows = [
            first_grad[axis : axis + 1, lane : lane + across]
            for axis in range(2)
            for lane in range(0, width, across)
        ]
        told = jnp.concatenate(rows, axis=0)
        pieces_ref[:, :, LANES:] = jnp.broadcast_to(told[None], (count, *told.shape))


def branch_kernel(
    scale,
    fields,
    core_ref,
    from_ref,
    third_ref,
    branch_third_ref,
    branch_second_ref,
    *refs,
):
    first = len(refs) == 11
    sums = () if first else refs[:2]
    start = len(sums)
    u_ref, features_ref, two_ref, feature_back_ref, one_ref, back_two_ref = refs[start : start + 6]
    core = core_ref[0]
    width = third_ref.shape[0]
    half = u_ref.shape[0]
    across = 2 * width // from_ref.shape[1]
    here = width + LANES + across
    got = from_ref[...].astype(F32)
    total = jnp.sum(got[:, :, width : width + 2 * LANES], axis=0)
    got = got.reshape(half, -1)
    u = got[:, 0:width].astype(BF16)
    one = got[:, width + 2 * LANES :]
    columns = jnp.where(
        core == 0,
        got[:, here : here + fields],
        got[:, here + fields : here + 2 * fields],
    ).astype(BF16)
    u_ref[...] = u
    one_ref[...] = one.astype(BF16)
    wide = jnp.tanh(dot(one_ref[...], branch_second_ref[...]))
    two_ref[...] = wide.astype(BF16)
    features_ref[...] = dot(two_ref[...], branch_third_ref[...]).astype(BF16)
    feature_back = (dot(u, third_ref[...]) * scale).astype(BF16)
    feature_back_ref[...] = feature_back
    back_two = (dot(feature_back, branch_third_ref[...], NT) * (1.0 - wide * wide)).astype(BF16)
    back_two_ref[...] = back_two
    back_one = (dot(back_two, branch_second_ref[...], NT) * (1.0 - one * one)).astype(BF16)
    rows = dot(columns, back_one, TN)
    if first:
        refs[6][...] = rows
        refs[7][...] = total
        refs[8][...] = dot(u, features_ref[...], TN)
        refs[9][...] = dot(two_ref[...], feature_back, TN)
        refs[10][...] = dot(one_ref[...], back_two, TN)
        return
    rows_ref, first_ref = refs[-2:]
    rows, total = rows + sums[0][...], total + sums[1][...]
    parts = [rows[:, lane : lane + LANES] for lane in range(0, width, LANES)]
    rows_ref[...] = jnp.concatenate(parts + [total[:, 0:LANES]], axis=0).astype(BF16)
    deep = width // across
    for axis in range(2):
        for strip in range(deep):
            first_ref[axis : axis + 1, strip * across : (strip + 1) * across] = total[
                axis * deep + strip : axis * deep + strip + 1, LANES : LANES + across
            ]


def gradient_kernel(scale, *refs):
    mine, other, outs = refs[:3], refs[3:9], refs[9:]
    for k, by in enumerate((scale, None, None)):
        total = mine[k][...] + dot(other[2 * k][...], other[2 * k + 1][...], TN)
        outs[k][...] = total if by is None else total * by


def spread_rows(from_ref, grad_ref):
    got = from_ref[...].astype(F32)
    fields = grad_ref.shape[2]
    for lane in range(grad_ref.shape[3] // LANES):
        grad_ref[:, 0, :, lane * LANES : (lane + 1) * LANES] = got[
            :, lane * fields : (lane + 1) * fields
        ]
    return got


def mine_kernel(core_ref, mine_ref, grad_ref, second_ref):
    step = pl.program_id(0)
    tail = spread_rows(mine_ref, grad_ref)[:, -8:].reshape(-1, LANES)
    width = second_ref.shape[0]
    for now in range(width * width // tail.size):

        @pl.when(step == now)
        def _():
            strip, row = divmod(now * tail.shape[0], width)
            second_ref[row : row + tail.shape[0], strip * LANES : (strip + 1) * LANES] = tail


def other_kernel(core_ref, other_ref, kept_ref, grad_ref):
    spread_rows(other_ref, grad_ref)


def whole(*shape):
    return pl.BlockSpec(shape, lambda i: (0,) * len(shape))


def there(value):
    return pltpu.with_memory_space_constraint(value, pltpu.HBM)


SCALAR = pl.BlockSpec(memory_space=pltpu.SMEM)
LOCAL = pl.BlockSpec(memory_space=pltpu.VMEM)


def tiles(points):
    tile = min(TILE, points)
    deep = lambda n, width: pl.BlockSpec((n, tile, width), lambda i: (0, i, 0))
    return tile, deep


def first_call(sensors, first, count):
    own, depth = sensors.shape
    width = first.shape[1]
    part = depth // STEPS
    return pl.pallas_call(
        first_kernel,
        grid=(STEPS,),
        in_specs=[
            pl.BlockSpec((own, part), lambda i: (0, i)),
            pl.BlockSpec((part, width), lambda i: (i, 0)),
        ],
        out_specs=[whole(own, width), whole(count, own, width)],
        out_shape=[
            jax.ShapeDtypeStruct((own, width), BF16),
            jax.ShapeDtypeStruct((count, own, width), BF16),
        ],
        scratch_shapes=[pltpu.VMEM((own, width), F32)],
        compiler_params=PARAMS,
        name="branch_first",
    )(there(sensors), there(first))


def forward_call(coords, first, second):
    points, width = coords.shape[1], first.shape[1]
    tile, deep = tiles(points)
    flat = pl.BlockSpec((tile, width), lambda i: (i, 0))
    return pl.pallas_call(
        forward_kernel,
        grid=(points // tile,),
        in_specs=[
            pl.BlockSpec((2, tile), lambda i: (0, i)),
            whole(2, width),
            whole(width, width),
        ],
        out_specs=[deep(4, width), flat, deep(7, width), deep(5, width), whole(8, width, width)],
        out_shape=[
            pltpu.HBM((4, points, width), BF16),
            pltpu.HBM((points, width), F32),
            pltpu.HBM((7, points, width), BF16),
            pltpu.HBM((5, points, width), BF16),
            pltpu.HBM((8, width, width), BF16),
        ],
        scratch_shapes=[pltpu.VMEM((tile, width), F32), pltpu.VMEM((8, tile, width), F32)],
        compiler_params=PARAMS,
        name="trunk_forward",
    )(coords, first, second)


def project_call(ones, branch_second, branch_third, third, combos, forcing, weight, scale):
    funcs, points = forcing.shape
    width = third.shape[0]
    tile = min(PROJECT, points)
    return pl.pallas_call(
        functools.partial(project_kernel, weight, scale),
        grid=(points // tile,),
        in_specs=[
            whole(*ones.shape),
            whole(width, width),
            whole(width, width),
            whole(width, width),
            pl.BlockSpec((5, tile, width), lambda i: (0, i, 0)),
            pl.BlockSpec((funcs, tile), lambda i: (0, i)),
        ],
        out_specs=[
            pl.BlockSpec((5, funcs, tile), lambda i: (0, 0, i)),
            whole(funcs, width),
            whole(*ones.shape),
        ],
        out_shape=[
            pltpu.HBM((5, funcs, points), BF16),
            jax.ShapeDtypeStruct((funcs, width), BF16),
            jax.ShapeDtypeStruct(ones.shape, BF16),
        ],
        scratch_shapes=[pltpu.VMEM((funcs, width), F32)],
        compiler_params=PARAMS,
        name="project",
    )(ones, branch_second, branch_third, third, there(combos), there(forcing))


def backward_call(
    squash, points_all, inner, cots, feats, coords, weights, first, second, pieces
):
    points, width = squash.shape
    funcs = feats.shape[0]
    tile, deep = tiles(points)
    return pl.pallas_call(
        backward_kernel,
        grid=(points // tile,),
        in_specs=[
            pl.BlockSpec((tile, width), lambda i: (i, 0)),
            deep(4, width),
            deep(7, width),
            pl.BlockSpec((5, funcs, tile), lambda i: (0, 0, i)),
            whole(funcs, width),
            pl.BlockSpec((2, tile), lambda i: (0, i)),
            whole(8, width, width),
            whole(2, width),
            whole(width, width),
        ],
        out_specs=whole(*pieces),
        out_shape=jax.ShapeDtypeStruct(pieces, F32),
        scratch_shapes=[
            pltpu.VMEM((5, tile, width), F32),
            pltpu.VMEM((8, tile, width), BF16),
            pltpu.VMEM((4, tile, width), F32),
            pltpu.VMEM((tile, width), BF16),
            pltpu.VMEM((8, width, width), F32),
            pltpu.VMEM((16, width), F32),
        ],
        compiler_params=PARAMS,
        cost_estimate=pl.CostEstimate(
            flops=42 * points * width * width, bytes_accessed=48 * points * width, transcendentals=0
        ),
        name="trunk_backward",
    )(
        there(squash),
        there(points_all),
        there(inner),
        there(cots),
        feats,
        coords,
        weights,
        first,
        second,
    )


def branch_call(core, got, third, branch_third, branch_second, fields, scale, sums=()):
    count, own, width = got.shape[0] * got.shape[1], got.shape[1], third.shape[0]
    rows = fields * (width // LANES) + own
    last = [jax.ShapeDtypeStruct((fields, width), F32), jax.ShapeDtypeStruct((own, 2 * LANES), F32)]
    last += [jax.ShapeDtypeStruct((width, width), F32)] * 3
    if sums:
        last = [jax.ShapeDtypeStruct((rows, LANES), BF16), jax.ShapeDtypeStruct((2, width), F32)]
    return pl.pallas_call(
        functools.partial(branch_kernel, scale, fields),
        in_specs=[SCALAR] + [LOCAL] * (4 + len(sums)),
        out_shape=[jax.ShapeDtypeStruct((count, width), BF16)] * 6 + last,
        compiler_params=SMALL,
        name="branch_other" if sums else "branch_mine",
    )(core, got, third, branch_third, branch_second, *sums)


def gradient_call(mine, other, scale):
    shape = mine[0].shape
    return pl.pallas_call(
        functools.partial(gradient_kernel, scale),
        in_specs=[LOCAL] * 9,
        out_shape=[jax.ShapeDtypeStruct(shape, F32)] * 3,
        compiler_params=SMALL,
        name="branch_gradients",
    )(*mine, *other)


def spread_specs(got, shape, side):
    steps = STEPS
    part = got.shape[0] // steps
    fields = shape[0] // (2 * got.shape[0])
    return (
        steps,
        pl.BlockSpec((part, *got.shape[1:]), lambda j, c: (j, 0, 0)),
        pl.BlockSpec((part, 1, fields, shape[1]), lambda j, c: (j, side(c[0]), 0, 0)),
        jax.ShapeDtypeStruct((got.shape[0], 2, fields, shape[1]), F32),
    )


def mine_call(core, mine, shape, width):
    steps, piece, place, out = spread_specs(mine, shape, lambda c: c)
    return pl.pallas_call(
        mine_kernel,
        grid_spec=pltpu.PrefetchScalarGridSpec(
            num_scalar_prefetch=1,
            grid=(steps,),
            in_specs=[piece],
            out_specs=[place, pl.BlockSpec((width, width), lambda j, c: (0, 0))],
        ),
        out_shape=[out, jax.ShapeDtypeStruct((width, width), F32)],
        compiler_params=PARAMS,
        name="spread_mine",
    )(core, mine)


def other_call(core, other, kept, shape):
    steps, piece, place, out = spread_specs(other, shape, lambda c: 1 - c)
    return pl.pallas_call(
        other_kernel,
        grid_spec=pltpu.PrefetchScalarGridSpec(
            num_scalar_prefetch=1,
            grid=(steps,),
            in_specs=[piece, pl.BlockSpec(memory_space=pl.ANY)],
            out_specs=place,
        ),
        out_shape=out,
        input_output_aliases={2: 0},
        compiler_params=PARAMS,
        name="spread_other",
    )(core, other, kept)


def swap(parts, axes):
    return lax.all_to_all(parts, axes, split_axis=0, concat_axis=0, tiled=True)


def across_chip(value):
    return lax.ppermute(value, "core", [(0, 1), (1, 0)])


def per_device(
    sensors,
    forcing,
    coords,
    branch_first,
    branch_second,
    branch_third,
    trunk_first,
    trunk_second,
    trunk_third,
):
    pairs, pts_size = lax.axis_size("pairs"), lax.axis_size("pts")
    func_size = 2 * pairs
    chips = pairs * pts_size
    core = lax.axis_index("core").reshape(1)
    funcs = forcing.shape[0]
    weight = 1.0 / math.sqrt(funcs * func_size * forcing.shape[1] * pts_size)
    width_out = trunk_third.shape[1]
    width = trunk_second.shape[0]
    scale = width_out ** (-0.5)
    own = sensors.shape[0]
    fields = sensors.shape[1] // chips

    own_one, told_one = first_call(sensors, branch_first, pts_size)
    ones = swap(told_one, "pts")
    blocks = sensors.reshape(own, chips, fields).transpose(1, 0, 2)
    points_all, squash, inner, combos, weights = forward_call(coords, trunk_first, trunk_second)
    cots, feats, shares = project_call(
        ones,
        branch_second,
        branch_third,
        trunk_third,
        combos,
        forcing,
        weight,
        scale,
    )
    u_own = swap(shares, "pts").astype(F32).sum(0).astype(BF16)
    second_pieces = backward_call(
        squash,
        points_all,
        inner,
        cots,
        feats,
        coords,
        weights,
        trunk_first,
        trunk_second,
        (chips, own, LANES + 2 * width // own),
    )
    told = lambda part: jnp.broadcast_to(part[None], (chips, *part.shape))
    pieces = jnp.concatenate(
        [
            told(u_own),
            second_pieces.astype(BF16),
            blocks,
            told(own_one),
        ],
        axis=2,
    )
    every = swap(pieces, ("pairs", "pts"))
    every_other = across_chip(every)
    branch = functools.partial(
        branch_call,
        core,
        third=trunk_third,
        branch_third=branch_third,
        branch_second=branch_second,
        fields=fields // 2,
        scale=scale,
    )
    *_, rows, total, sum_t3, sum_b3, sum_b2 = branch(got=every)
    *half_other, rows, grad_t1 = branch(got=every_other, sums=(rows, total))
    mine = swap(told(rows), ("pairs", "pts"))
    other = across_chip(mine)
    grad_t3, grad_b3, grad_b2 = gradient_call(
        (sum_t3, sum_b3, sum_b2), half_other, scale
    )
    kept, grad_t2 = mine_call(core, mine, branch_first.shape, width)
    grad_b1 = other_call(core, other, kept, branch_first.shape).reshape(branch_first.shape)
    return (grad_b1, grad_b2, grad_b3, grad_t1, grad_t2, grad_t3)


def solution(mesh):
    func_size, pts_size = mesh.devices.shape
    cores = jax.sharding.Mesh(mesh.devices.reshape(func_size // 2, 2, pts_size), AXES)
    return jax.shard_map(
        per_device,
        mesh=cores,
        in_specs=(
            P(AXES, None),
            P(("pairs", "core"), "pts"),
            P(None, "pts"),
            P(),
            P(),
            P(),
            P(),
            P(),
            P(),
        ),
        out_specs=(P(), P(), P(), P(), P(), P()),
        check_vma=False,
    )
```
